256 devices in a mesh: lon: 32 (over y_lo, z, core), lat: 8 (over x, y_hi).
Axes of the slice: x: 4, y: 4 (y_hi: 2, y_lo: 2; y = y_hi * 2 + y_lo), z: 8, core: 2. Of those that a mesh axis runs over, the one named last changes fastest.
Arguments:
- tokens: bfloat16 [2, 192, 73728], P(None, 'lat', 'lon'), may hold values from -8 to 8
- fine_attend: bfloat16 [192, 576], replicated, may hold values from -0.4375 to 0.4375
- fine_project: bfloat16 [192, 192], replicated, may hold values from -0.4375 to 0.4375
- fine_gain_one: float32 [192], replicated, may hold values from 0.25 to 1.75
- fine_expand: bfloat16 [192, 768], replicated, may hold values from -0.4375 to 0.4375
- fine_reduce: bfloat16 [768, 192], replicated, may hold values from -0.21875 to 0.21875
- fine_gain_two: float32 [192], replicated, may hold values from 0.25 to 1.75
- fine_bias: float32 [32, 6, 23, 144], P('lat'), may hold values from -4 to 260
- merge_gain: float32 [768], replicated, may hold values from 0.25 to 1.75
- merge_weight: bfloat16 [768, 384], replicated, may hold values from -0.21875 to 0.21875
- coarse_attend: bfloat16 [384, 1152], replicated, may hold values from -0.3125 to 0.3125
- coarse_project: bfloat16 [384, 384], replicated, may hold values from -0.3125 to 0.3125
- coarse_gain_one: float32 [384], replicated, may hold values from 0.25 to 1.75
- coarse_expand: bfloat16 [384, 1536], replicated, may hold values from -0.3125 to 0.3125
- coarse_reduce: bfloat16 [1536, 384], replicated, may hold values from -0.15625 to 0.15625
- coarse_gain_two: float32 [384], replicated, may hold values from 0.25 to 1.75
- coarse_bias: float32 [16, 12, 23, 144], P('lat'), may hold values from -4 to 260
- cotangent: bfloat16 [2, 96, 73728], P(None, 'lat', 'lon'), may hold values from -6 to 6
Outputs:
- coarse_out: bfloat16 [2, 96, 73728], P(None, 'lat', 'lon')
- grad_tokens: bfloat16 [2, 192, 73728], P(None, 'lat', 'lon')
- grad_fine_bias: float32 [32, 6, 23, 144], P('lat')
- grad_coarse_bias: float32 [16, 12, 23, 144], P('lat')
The draws below stay inside these ranges and needn't reach their ends.
All inputs are finite; a program needn't handle non-finite values.
Results may differ from the reference program's by a relative error of at most 0.034.
Values may be sent and summed in bfloat16 or wider, within the bound.
No kernel may reach another device: no remote copies, remote signals or barrier semaphores. Data moves between devices by JAX's collectives and lax.ppermute only.
A program may use at most 256 MiB of HBM per device.

```python
import math
import jax
import jax.numpy as jnp
from jax import lax

C1 = 192
C2 = 384
HD = 32
H1 = 6
H2 = 12
NZ = 2
WZ = 2
WLAT = 6
WLON = 12
NLAT = 192
NLON = 384
OFFS = 23
PAIRS = 144
TYPES1 = 32
TYPES2 = 16


def draw_tokens(key, part):
    key = jax.random.fold_in(key, 11)
    key_one, key_two = jax.random.split(key, 2)
    column_scale = jnp.exp(jax.random.uniform(key_one, (C1,), jnp.float32, math.log(0.3), math.log(3.0)))
    values = jax.random.normal(key_two, (NZ, NLAT, NLON, C1), jnp.float32) * column_scale
    return jnp.clip(values, -8.0, 8.0).reshape(NZ, NLAT, NLON * C1).astype(jnp.bfloat16)


def draw_fine_bias(key, part):
    key = jax.random.fold_in(key, 21)
    array_shape = (TYPES1, H1, OFFS, PAIRS)
    return jnp.clip(jax.random.normal(key, array_shape, jnp.float32), -4.0, 4.0)


def draw_coarse_bias(key, part):
    key = jax.random.fold_in(key, 31)
    array_shape = (TYPES2, H2, OFFS, PAIRS)
    return jnp.clip(jax.random.normal(key, array_shape, jnp.float32), -4.0, 4.0)


def block_scale(own_key, shape, shards, low, largest):
    level = 1.0
    for dim, parts in shards:
        draws = jax.random.uniform(jax.random.fold_in(jax.random.fold_in(own_key, 6), dim), (parts,), jnp.float32, low / len(shards), largest / len(shards))
        level = level * jnp.repeat(jnp.exp(draws), shape[dim] // parts).reshape((-1,) + (1,) * (len(shape) - 1 - dim))
    return level


def gaussian(rng, shape, deviation, bound, shards=(), held_as=jnp.bfloat16):
    values = deviation * jax.random.normal(rng, shape, jnp.float32)
    if shards:
        values = values * block_scale(rng, shape, shards, -0.22, 0.18)
    return jnp.clip(values, -bound, bound).astype(held_as)


def setup_inputs(seed: int = 0) -> dict:
    arg_keys = jax.random.split(jax.random.key(seed), 19)
    return {
        "tokens": draw_tokens(jax.random.fold_in(arg_keys[18], 71), 0),
        "fine_attend": gaussian(arg_keys[1], (C1, 3 * C1), C1 ** -0.5, 0.4375),
        "fine_project": gaussian(arg_keys[2], (C1, C1), C1 ** -0.5, 0.4375),
        "fine_gain_one": jnp.clip(1.0 + 0.15 * jax.random.normal(arg_keys[3], (C1,), jnp.float32), 0.25, 1.75),
        "fine_expand": gaussian(arg_keys[4], (C1, 4 * C1), C1 ** -0.5, 0.4375),
        "fine_reduce": gaussian(arg_keys[5], (4 * C1, C1), (4 * C1) ** -0.5, 0.21875),
        "fine_gain_two": jnp.clip(1.0 + 0.15 * jax.random.normal(arg_keys[6], (C1,), jnp.float32), 0.25, 1.75),
        "fine_bias": draw_fine_bias(jax.random.fold_in(arg_keys[18], 71), 0),
        "merge_gain": jnp.clip(1.0 + 0.15 * jax.random.normal(arg_keys[8], (4 * C1,), jnp.float32), 0.25, 1.75),
        "merge_weight": gaussian(arg_keys[9], (4 * C1, C2), (4 * C1) ** -0.5, 0.21875),
        "coarse_attend": gaussian(arg_keys[10], (C2, 3 * C2), C2 ** -0.5, 0.3125),
        "coarse_project": gaussian(arg_keys[11], (C2, C2), C2 ** -0.5, 0.3125),
        "coarse_gain_one": jnp.clip(1.0 + 0.15 * jax.random.normal(arg_keys[12], (C2,), jnp.float32), 0.25, 1.75),
        "coarse_expand": gaussian(arg_keys[13], (C2, 4 * C2), C2 ** -0.5, 0.3125),
        "coarse_reduce": gaussian(arg_keys[14], (4 * C2, C2), (4 * C2) ** -0.5, 0.15625),
        "coarse_gain_two": jnp.clip(1.0 + 0.15 * jax.random.normal(arg_keys[15], (C2,), jnp.float32), 0.25, 1.75),
        "coarse_bias": draw_coarse_bias(jax.random.fold_in(arg_keys[18], 71), 0),
        "cotangent": gaussian(arg_keys[17], (NZ, NLAT // 2, (NLON // 2) * C2), 1.0, 6.0, ((1, 8), (2, 32))),
    }


EPSILON = 1e-05
MASKED = -1000000000.0

def layer_norm(values):
    average = lax.optimization_barrier(jnp.mean(values, axis=-1, keepdims=True))
    centred = values - average
    variance = lax.optimization_barrier(jnp.mean(centred * centred, axis=-1, keepdims=True))
    return centred * lax.rsqrt(variance + EPSILON)

def offset_onehot():
    position = jnp.arange(WLON, dtype=jnp.int32)
    offset_index = position[:, None] - position[None, :] + (WLON - 1)
    offsets = jnp.arange(2 * WLON - 1, dtype=jnp.int32)
    return (offset_index[None, :, :] == offsets[:, None, None]).astype(jnp.float32)

def build_bias(bias_table):
    groups, head_count = (bias_table.shape[0], bias_table.shape[1])
    plane_cells = WZ * WLAT
    shaped = bias_table.reshape(groups, head_count, 2 * WLON - 1, plane_cells, plane_cells)
    spread = jnp.einsum('ghdab,dpq->ghapbq', shaped, offset_onehot(), precision=lax.Precision.HIGHEST)
    return spread.reshape(groups, head_count, plane_cells * WLON, plane_cells * WLON)

def region(position, extent, window):
    return (position >= extent - window).astype(jnp.int32) + (position >= extent - window // 2).astype(jnp.int32)

def pair_allowed(lat_windows, level_windows, row_start, lat_total):
    token_index = jnp.arange(WZ * WLAT * WLON, dtype=jnp.int32)
    level_in = token_index // (WLAT * WLON)
    row_in = token_index // WLON % WLAT
    level_pos = jnp.arange(level_windows, dtype=jnp.int32)[:, None] * WZ + level_in[None, :]
    row_pos = row_start + jnp.arange(lat_windows, dtype=jnp.int32)[:, None] * WLAT + row_in[None, :]
    region_code = region(level_pos, NZ, WZ)[None, :, :] * 3 + region(row_pos, lat_total, WLAT)[:, None, :]
    return region_code[..., :, None] == region_code[..., None, :]

def project(tokens_in, weight):
    return jnp.dot(tokens_in, weight, preferred_element_type=jnp.float32).astype(jnp.bfloat16)

def to_heads(block_data, head_count):
    shaped = lax.optimization_barrier(block_data).astype(jnp.float32)
    shaped = shaped.reshape(block_data.shape[:-1] + (head_count, HD))
    return jnp.swapaxes(shaped, -2, -3)

def split_qkv(packed, head_count):
    block_width = packed.shape[-1] // 3
    return (to_heads(packed[..., :block_width], head_count), to_heads(packed[..., block_width:2 * block_width], head_count), to_heads(packed[..., 2 * block_width:], head_count))

def attend(query_heads, key_heads, value_heads, bias_full, allowed):
    scores = jnp.einsum('gwhqd,gwhkd->gwhqk', query_heads, key_heads, precision=lax.Precision.HIGHEST)
    scores = scores / math.sqrt(HD) + bias_full[:, None]
    scores = jnp.where(allowed[:, None, None], scores, MASKED)
    softmaxed = jax.nn.softmax(scores, axis=-1).astype(jnp.bfloat16)
    mixture = jnp.einsum('gwhqk,gwhkd->gwqhd', lax.optimization_barrier(softmaxed).astype(jnp.float32), value_heads, precision=lax.Precision.HIGHEST)
    return mixture.reshape(mixture.shape[:3] + (-1,)).astype(jnp.bfloat16)

def block_tail(tokens_in, head_out, level_weights):
    w_project, gain_attend, w_expand, w_reduce, gain_mixer = level_weights[1:]
    attention = jnp.dot(head_out, w_project, preferred_element_type=jnp.float32)
    middle = (tokens_in.astype(jnp.float32) + gain_attend * layer_norm(attention)).astype(jnp.bfloat16)
    expanded = jnp.dot(middle, w_expand, preferred_element_type=jnp.float32)
    activated = jax.nn.gelu(expanded, approximate=False).astype(jnp.bfloat16)
    reduced = jnp.dot(activated, w_reduce, preferred_element_type=jnp.float32)
    middle_wide = lax.optimization_barrier(middle).astype(jnp.float32)
    return (middle_wide + gain_mixer * layer_norm(reduced)).astype(jnp.bfloat16)

def window_block(tokens_in, bias_table, allowed, level_weights):
    head_count = bias_table.shape[1]
    query_heads, key_heads, value_heads = split_qkv(project(tokens_in, level_weights[0]), head_count)
    head_out = attend(query_heads, key_heads, value_heads, build_bias(bias_table), allowed)
    return block_tail(tokens_in, head_out, level_weights)

def windows_of(cell_grid):
    levels, row_count, col_count, channels = cell_grid.shape
    shaped = cell_grid.reshape(levels // WZ, WZ, row_count // WLAT, WLAT, col_count // WLON, WLON, channels)
    shaped = shaped.transpose(2, 0, 4, 1, 3, 5, 6)
    return shaped.reshape(row_count // WLAT, levels // WZ, col_count // WLON, WZ * WLAT * WLON, channels)

def grid_of(windows, levels, row_count, col_count):
    channels = windows.shape[-1]
    shaped = windows.reshape(row_count // WLAT, levels // WZ, col_count // WLON, WZ, WLAT, WLON, channels)
    return shaped.transpose(1, 3, 0, 4, 2, 5, 6).reshape(levels, row_count, col_count, channels)

def run_level(cell_grid, bias_table, allowed, level_weights):
    levels, row_count, col_count, channels = cell_grid.shape
    windows = windows_of(cell_grid)
    tables = bias_table.reshape((row_count // WLAT, levels // WZ) + bias_table.shape[1:])
    group_step = jax.checkpoint(lambda inputs: window_block(inputs[0], inputs[1], inputs[2], level_weights))
    mixture = lax.map(group_step, (windows, tables, allowed))
    return grid_of(mixture, levels, row_count, col_count)

def merge_level(fine_grid, norm_gain, weight):
    levels, row_count, col_count, channels = fine_grid.shape
    quadrants = fine_grid.reshape(levels, row_count // 2, 2, col_count // 2, 2, channels)
    quadrants = quadrants.transpose(0, 1, 3, 2, 4, 5).reshape(levels, row_count // 2, col_count // 2, 4 * channels)
    normed = (norm_gain * layer_norm(quadrants.astype(jnp.float32))).astype(jnp.bfloat16)
    return jnp.dot(normed, weight, preferred_element_type=jnp.float32).astype(jnp.bfloat16)

def forward(tokens, fine_bias, coarse_bias, fine_weights, merge_gain, merge_weight, coarse_weights):
    cell_grid = tokens.reshape(NZ, NLAT, NLON, C1)
    rolled = jnp.roll(cell_grid, (-1, -(WLAT // 2), -(WLON // 2)), axis=(0, 1, 2))
    fine_allowed = pair_allowed(NLAT // WLAT, NZ // WZ, 0, NLAT)
    mixture = run_level(rolled, fine_bias, fine_allowed, fine_weights)
    fine_grid = jnp.roll(mixture, (1, WLAT // 2, WLON // 2), axis=(0, 1, 2))
    coarse_grid = merge_level(fine_grid, merge_gain, merge_weight)
    window_cells = WZ * WLAT * WLON
    coarse_allowed = jnp.ones((NLAT // (2 * WLAT), NZ // WZ, window_cells, window_cells), jnp.bool_)
    result = run_level(coarse_grid, coarse_bias, coarse_allowed, coarse_weights)
    return result.reshape(NZ, NLAT // 2, NLON // 2 * C2)

def reference(tokens, fine_attend, fine_project, fine_gain_one, fine_expand, fine_reduce, fine_gain_two, fine_bias, merge_gain, merge_weight, coarse_attend, coarse_project, coarse_gain_one, coarse_expand, coarse_reduce, coarse_gain_two, coarse_bias, cotangent):
    fine_weights = (fine_attend, fine_project, fine_gain_one, fine_expand, fine_reduce, fine_gain_two)
    coarse_weights = (coarse_attend, coarse_project, coarse_gain_one, coarse_expand, coarse_reduce, coarse_gain_two)

    def whole(tokens_in, bias_one, bias_two):
        return forward(tokens_in, bias_one, bias_two, fine_weights, merge_gain, merge_weight, coarse_weights)
    result, pullback = jax.vjp(whole, tokens, fine_bias, coarse_bias)
    grad_tokens, grad_fine_bias, grad_coarse_bias = pullback(cotangent)
    return (result, grad_tokens, grad_fine_bias, grad_coarse_bias)
```

```python
import functools
import math

import jax
import jax.numpy as jnp
import numpy as np
from jax import lax
from jax.experimental import pallas as pl
from jax.experimental.pallas import tpu as pltpu
from jax.sharding import PartitionSpec as P

C1 = 192
C2 = 384
HD = 32
H1 = 6
H2 = 12
WLON = 12
HALF = 72
EPSILON = 1e-05
MASKED = -1000000000.0
SCALE = 1.0 / math.sqrt(HD)
F32 = jnp.float32
BF16 = jnp.bfloat16


def pair_lane(pair):
    return pair // 5 * 128 + pair % 5 * 24


def spread_onehot(pairs, lanes):
    onehot = np.zeros((WLON, (pairs + 4) // 5 * 128, lanes), np.float32)
    for p in range(WLON):
        for b in range(pairs):
            for q in range(WLON):
                onehot[p, pair_lane(b) + p - q + WLON - 1, b * WLON + q] = 1.0
    return onehot.astype(jnp.bfloat16)


def merge_onehot():
    onehot = np.zeros((4, 2, 2, 48, 648), np.float32)
    for rr in range(2):
        for cc in range(2):
            for bh in range(2):
                for lam in range(2):
                    for z in range(2):
                        for a in range(6):
                            for b in range(3):
                                row = 2 * (lam * 6 + a) + rr
                                col = 2 * (bh * 3 + b) + cc
                                if row < 3:
                                    cell = 576 + z * 36 + row * 12 + col
                                else:
                                    cell = z * 288 + (row - 3) * 12 + col
                                onehot[rr * 2 + cc, bh, lam, z * 18 + a * 3 + b, cell] = 1.0
    return onehot.reshape(768, 648).astype(jnp.bfloat16)


def strip_onehot():
    onehot = np.zeros((576, 72), np.float32)
    for z in range(2):
        for k in range(36):
            onehot[z * 288 + 252 + k, z * 36 + k] = 1.0
    return onehot.astype(jnp.bfloat16)


def window_onehot():
    onehot = np.zeros((2, 144, 192), np.float32)
    for parity in range(2):
        for z in range(2):
            for a in range(6):
                for c in range(12):
                    kept = (c < 6) == (parity == 0)
                    local = c % 6
                    place = (0 if kept else 96) + local // 3 * 48 + z * 18 + a * 3 + local % 3
                    onehot[parity, z * 72 + a * 12 + c, place] = 1.0
    return onehot.astype(jnp.bfloat16)


def halves_onehot():
    onehot = np.zeros((2, 144, 144), np.float32)
    for parity in range(2):
        for z in range(2):
            for a in range(6):
                for c in range(12):
                    kept = (c < 6) == (parity == 0)
                    place = (0 if kept else 72) + z * 36 + a * 6 + c % 6
                    onehot[parity, z * 72 + a * 12 + c, place] = 1.0
    return onehot.astype(jnp.bfloat16)


def nn(left, right):
    return lax.dot_general(left, right, (((1,), (0,)), ((), ())), preferred_element_type=F32)


def nt(left, right):
    return lax.dot_general(left, right, (((1,), (1,)), ((), ())), preferred_element_type=F32)


def tn(left, right):
    return lax.dot_general(left, right, (((0,), (0,)), ((), ())), preferred_element_type=F32)


def norm_parts(values):
    average = jnp.mean(values, axis=-1, keepdims=True)
    centred = values - average
    scale = lax.rsqrt(jnp.mean(centred * centred, axis=-1, keepdims=True) + EPSILON)
    return centred * scale, scale


def norm_back(grad, normed, scale):
    first = jnp.mean(grad, axis=-1, keepdims=True)
    second = jnp.mean(grad * normed, axis=-1, keepdims=True)
    return scale * (grad - first - normed * second)


def split3(values):
    high = values.astype(BF16)
    rest = values - high.astype(F32)
    mid = rest.astype(BF16)
    low = (rest - mid.astype(F32)).astype(BF16)
    return high, mid, low


def head_mask(rows, heads, width):
    row = lax.broadcasted_iota(jnp.int32, (heads * rows, width), 0) // rows
    lane = lax.broadcasted_iota(jnp.int32, (heads * rows, width), 1) // HD
    return (row == lane).astype(F32)


def heads_stack(values, heads, mask):
    return (jnp.concatenate([values] * heads, axis=0) * mask).astype(BF16)


def heads_fold(stacked, heads, mask):
    rows = stacked.shape[0] // heads
    kept = stacked * mask
    total = kept[:rows]
    for h in range(1, heads):
        total = total + kept[h * rows : (h + 1) * rows]
    return total


def gelu_parts(values):
    phi = 0.5 * (1.0 + lax.erf(values * (1.0 / math.sqrt(2.0))))
    density = jnp.exp(-0.5 * values * values) * (1.0 / math.sqrt(2.0 * math.pi))
    return values * phi, phi + values * density


def softmax(scores):
    top = jnp.max(scores, axis=-1, keepdims=True)
    powers = jnp.exp(scores - top)
    return powers / jnp.sum(powers, axis=-1, keepdims=True)


def bias_kernel(par_ref, fine_ref, coarse_ref, ef_ref, ec_ref, bf_ref, bc_ref, cols_f, cols_c):
    cols_f[...] = jnp.zeros_like(cols_f)
    cols_c[...] = jnp.zeros_like(cols_c)
    for th in range(24):
        cols_f[th * 144 : (th + 1) * 144, 0:23] = jnp.swapaxes(fine_ref[th], 0, 1)
    par = par_ref[0]
    for h in range(12):
        cols_c[h * 144 : (h + 1) * 144, 0:23] = jnp.swapaxes(coarse_ref[par, h], 0, 1)
    low_level = lax.broadcasted_iota(jnp.int32, (288, 128), 0) % 12 < 6
    tiles = []
    for t in range(2):
        tile = None
        for jm in range(t * 5, min(t * 5 + 5, 6)):
            piece = jnp.where(
                low_level,
                cols_f[pl.ds(jm, 288, stride=12), :],
                cols_f[pl.ds(6 + jm, 288, stride=12), :],
            )
            if jm % 5:
                piece = pltpu.roll(piece, jm % 5 * 24, 1)
            tile = piece if tile is None else tile + piece
        tiles.append(tile)
    table = jnp.concatenate(tiles, axis=1)
    parts = jnp.concatenate(split3(table), axis=0)
    for p in range(WLON):
        spread = nn(parts, ef_ref[p])
        bf_ref[pl.ds(p, 288, stride=12), :] = spread[:288] + spread[288:576] + spread[576:]
    tiles = []
    for t in range(3):
        tile = None
        for b in range(t * 5, min(t * 5 + 5, 12)):
            piece = cols_c[pl.ds(b, 144, stride=12), :]
            if b % 5:
                piece = pltpu.roll(piece, b % 5 * 24, 1)
            tile = piece if tile is None else tile + piece
        tiles.append(tile)
    table = jnp.concatenate(tiles, axis=1)
    parts = jnp.concatenate(split3(table), axis=0)
    for p in range(WLON):
        spread = nn(parts, ec_ref[p])
        total = spread[:144] + spread[144:288] + spread[288:]
        bc_ref[0, pl.ds(p, 144, stride=12), :] = total[:, :128]
        bc_ref[1, pl.ds(p, 144, stride=12), :] = total[:, 128:]


def bias_call(par, fine_table, coarse_tables):
    return pl.pallas_call(
        bias_kernel,
        out_shape=(
            jax.ShapeDtypeStruct((3456, 128), F32),
            jax.ShapeDtypeStruct((2, 1728, 128), F32),
        ),
        in_specs=[pl.BlockSpec(memory_space=pltpu.SMEM)]
        + [pl.BlockSpec(memory_space=pltpu.VMEM)] * 4,
        scratch_shapes=[pltpu.VMEM((3456, 128), F32), pltpu.VMEM((1728, 128), F32)],
        compiler_params=pltpu.CompilerParams(vmem_limit_bytes=24 << 20),
        name="bias_spread",
    )(par, fine_table, coarse_tables, spread_onehot(6, 128), spread_onehot(12, 256))


def fine_kernel(
    last_ref, x_ref, wa_ref, wp_ref, g1_ref, we_ref, wr_ref, g2_ref, bias_ref,
    y_ref, q_ref, k_ref, v_ref, a_ref, att_ref, slope_ref, red_ref, o_ref,
):
    x = x_ref[...]
    q_ref[...] = nn(x, wa_ref[:, :C1]).astype(BF16).astype(F32)
    k_ref[...] = nn(x, wa_ref[:, C1 : 2 * C1]).astype(BF16).astype(F32)
    v_ref[...] = nn(x, wa_ref[:, 2 * C1 :]).astype(BF16).astype(F32)
    mask = head_mask(HALF, H1, C1)
    last = last_ref[0]
    for z in range(2):
        for w in range(4):
            rows = slice(z * 288 + w * 72, z * 288 + w * 72 + 72)
            qs = heads_stack(q_ref[rows, :], H1, mask)
            places = [((w * 6 + h) * 2 + 1 - z) * 72 for h in range(H1)]
            bias = jnp.concatenate([bias_ref[s : s + 72, :] for s in places], axis=0)[:, :72]
            scores = nt(qs, k_ref[rows, :].astype(BF16)) * SCALE + bias
            if w == 3:
                row = lax.broadcasted_iota(jnp.int32, scores.shape, 0) % 72 < 36
                col = lax.broadcasted_iota(jnp.int32, scores.shape, 1) < 36
                scores = jnp.where(jnp.logical_and(row != col, last == 1), MASKED, scores)
            weights = softmax(scores).astype(BF16)
            block = z * 4 + w
            a_ref[block * 432 : (block + 1) * 432, :] = weights
            o_ref[rows, :] = heads_fold(nn(weights, v_ref[rows, :].astype(BF16)), H1, mask)
    for c in range(4):
        rows = slice(c * 144, (c + 1) * 144)
        att = nn(o_ref[rows, :].astype(BF16), wp_ref[...])
        att_ref[rows, :] = att
        normed, _ = norm_parts(att)
        middle = (x_ref[rows, :].astype(F32) + g1_ref[...] * normed).astype(BF16)
        act, slope = gelu_parts(nn(middle, we_ref[...]))
        slope_ref[rows, :] = slope.astype(BF16)
        red = nn(act.astype(BF16), wr_ref[...])
        red_ref[rows, :] = red
        normed, _ = norm_parts(red)
        y_ref[rows, :] = (middle.astype(F32) + g2_ref[...] * normed).astype(BF16)


def fine_call(last, x, weights, bias):
    wa, wp, g1, we, wr, g2 = weights
    shape = jax.ShapeDtypeStruct
    return pl.pallas_call(
        fine_kernel,
        out_shape=(
            shape((576, C1), BF16),
            shape((576, C1), F32),
            shape((576, C1), F32),
            shape((576, C1), F32),
            shape((3456, 72), BF16),
            shape((576, C1), F32),
            shape((576, 4 * C1), BF16),
            shape((576, C1), F32),
        ),
        in_specs=[pl.BlockSpec(memory_space=pltpu.SMEM)]
        + [pl.BlockSpec(memory_space=pltpu.VMEM)] * 8,
        scratch_shapes=[pltpu.VMEM((576, C1), F32)],
        compiler_params=pltpu.CompilerParams(vmem_limit_bytes=32 << 20),
        name="fine_forward",
    )(last, x, wa, wp, g1.reshape(1, C1), we, wr, g2.reshape(1, C1), bias)


def merge_kernel(y_ref, strip_ref, pick_ref, gain_ref, w_ref, out_ref, f_ref):
    cells = jnp.concatenate([y_ref[...], strip_ref[...]], axis=0)
    f = nn(pick_ref[...], cells)
    f_ref[...] = f.astype(BF16)
    total = sum(jnp.sum(f[k * 192 : (k + 1) * 192], axis=-1, keepdims=True) for k in range(4))
    average = total * (1.0 / 768)
    centred = [f[k * 192 : (k + 1) * 192] - average for k in range(4)]
    square = sum(jnp.sum(c * c, axis=-1, keepdims=True) for c in centred)
    scale = lax.rsqrt(square * (1.0 / 768) + EPSILON)
    result = None
    for k in range(4):
        normed = (gain_ref[k : k + 1, :] * (centred[k] * scale)).astype(BF16)
        part = nn(normed, w_ref[k * 192 : (k + 1) * 192, :])
        result = part if result is None else result + part
    out_ref[...] = result.astype(BF16)


def merge_call(y, strip, pick, gain, weight):
    shape = jax.ShapeDtypeStruct
    return pl.pallas_call(
        merge_kernel,
        out_shape=(shape((192, C2), BF16), shape((768, C1), BF16)),
        in_specs=[pl.BlockSpec(memory_space=pltpu.VMEM)] * 5,
        compiler_params=pltpu.CompilerParams(vmem_limit_bytes=24 << 20),
        name="merge_forward",
    )(y, strip, pick, gain.reshape(4, C1), weight)


def coarse_kernel(
    par_ref, keep_ref, got_ref, ckeep_ref, cgot_ref, pick_ref, half_ref,
    wa_ref, wp_ref, g1_ref, we_ref, wr_ref, g2_ref, bias_ref, ec_ref,
    okeep_ref, osend_ref, gkeep_ref, gsend_ref, dt_ref,
    a_ref, qs_ref, o_ref, ds_ref, slope_ref,
):
    par = par_ref[0]
    pick = pick_ref[par]
    half = half_ref[par]
    x = nn(pick, jnp.concatenate([keep_ref[...], got_ref[...]], axis=0)).astype(BF16)
    seed = nn(half, jnp.concatenate([ckeep_ref[...], cgot_ref[...]], axis=0))
    packed = nn(x, wa_ref[...]).astype(BF16)
    mask = head_mask(144, 4, 128)
    for g in range(3):
        lanes = slice(g * 128, (g + 1) * 128)
        rows = slice(g * 576, (g + 1) * 576)
        qs = heads_stack(packed[:, lanes].astype(F32), 4, mask)
        qs_ref[rows, :] = qs
        key = packed[:, C2 + g * 128 : C2 + (g + 1) * 128]
        value = packed[:, 2 * C2 + g * 128 : 2 * C2 + (g + 1) * 128]
        bias = jnp.concatenate([bias_ref[0, rows, :], bias_ref[1, rows, :]], axis=1)[:, :144]
        weights = softmax(nt(qs, key) * SCALE + bias).astype(BF16)
        a_ref[rows, :] = weights
        o_ref[:, lanes] = heads_fold(nn(weights, value), 4, mask)
    att = nn(o_ref[...].astype(BF16), wp_ref[...])
    normed1, scale1 = norm_parts(att)
    middle = (x.astype(F32) + g1_ref[...] * normed1).astype(BF16)
    act, slope = gelu_parts(nn(middle, we_ref[...]))
    slope_ref[...] = slope
    red = nn(act.astype(BF16), wr_ref[...])
    normed2, scale2 = norm_parts(red)
    out = (middle.astype(F32) + g2_ref[...] * normed2).astype(BF16)
    parted = tn(half, out)
    okeep_ref[...] = parted[:72].astype(BF16)
    osend_ref[...] = parted[72:].astype(BF16)
    grad_red = norm_back(seed * g2_ref[...], normed2, scale2).astype(BF16)
    grad_act = nt(grad_red, wr_ref[...]).astype(BF16).astype(F32)
    grad_exp = (grad_act * slope_ref[...]).astype(BF16)
    grad_middle = (seed + nt(grad_exp, we_ref[...]).astype(BF16).astype(F32)).astype(BF16)
    grad_middle = grad_middle.astype(F32)
    grad_att = norm_back(grad_middle * g1_ref[...], normed1, scale1).astype(BF16)
    grad_o = nt(grad_att, wp_ref[...]).astype(BF16)
    grad_x = grad_middle
    for g in range(3):
        lanes = slice(g * 128, (g + 1) * 128)
        rows = slice(g * 576, (g + 1) * 576)
        os = heads_stack(grad_o[:, lanes].astype(F32), 4, mask)
        key = packed[:, C2 + g * 128 : C2 + (g + 1) * 128]
        value = packed[:, 2 * C2 + g * 128 : 2 * C2 + (g + 1) * 128]
        weights = a_ref[rows, :]
        grad_a = nt(os, value)
        wide = weights.astype(F32)
        grad_s = wide * (grad_a - jnp.sum(wide * grad_a, axis=-1, keepdims=True))
        ds_ref[0, rows, :] = grad_s[:, :128]
        ds_ref[1, rows, 0:16] = grad_s[:, 128:]
        short = grad_s.astype(BF16)
        grad_v = tn(weights, os).astype(BF16)
        grad_q = (heads_fold(nn(short, key), 4, mask) * SCALE).astype(BF16)
        grad_k = (tn(short, qs_ref[rows, :]) * SCALE).astype(BF16)
        grad_x = grad_x + nt(grad_q, wa_ref[:, g * 128 : (g + 1) * 128])
        grad_x = grad_x + nt(grad_k, wa_ref[:, C2 + g * 128 : C2 + (g + 1) * 128])
        grad_x = grad_x + nt(grad_v, wa_ref[:, 2 * C2 + g * 128 : 2 * C2 + (g + 1) * 128])
    parted = tn(pick, grad_x.astype(BF16))
    gkeep_ref[...] = parted[:96].astype(BF16)
    gsend_ref[...] = parted[96:].astype(BF16)
    table = None
    for p in range(WLON):
        piece = jnp.concatenate(
            [
                ds_ref[0, pl.ds(p, 144, stride=12), :],
                ds_ref[1, pl.ds(p, 144, stride=12), :][:, :16],
            ],
            axis=1,
        ).astype(BF16)
        part = nt(piece, ec_ref[p])
        table = part if table is None else table + part
    dt_ref[...] = table.astype(BF16)


def coarse_call(par, keep, got, ckeep, cgot, weights, bias):
    wa, wp, g1, we, wr, g2 = weights
    shape = jax.ShapeDtypeStruct
    return pl.pallas_call(
        coarse_kernel,
        out_shape=(
            shape((72, C2), BF16),
            shape((72, C2), BF16),
            shape((96, C2), BF16),
            shape((96, C2), BF16),
            shape((144, 384), BF16),
        ),
        in_specs=[pl.BlockSpec(memory_space=pltpu.SMEM)]
        + [pl.BlockSpec(memory_space=pltpu.VMEM)] * 14,
        scratch_shapes=[
            pltpu.VMEM((1728, 144), BF16),
            pltpu.VMEM((1728, 128), BF16),
            pltpu.VMEM((144, C2), F32),
            pltpu.VMEM((2, 1728, 128), F32),
            pltpu.VMEM((144, 4 * C2), F32),
        ],
        compiler_params=pltpu.CompilerParams(vmem_limit_bytes=36 << 20),
        name="coarse_both",
    )(
        par, keep, got, ckeep, cgot, window_onehot(), halves_onehot(),
        wa, wp, g1.reshape(1, C2), we, wr, g2.reshape(1, C2), bias,
        spread_onehot(12, 144),
    )


def merge_back_kernel(g_ref, f_ref, place_ref, gain_ref, w_ref, gy_ref, gstrip_ref):
    f = f_ref[...].astype(F32)
    total = sum(jnp.sum(f[k * 192 : (k + 1) * 192], axis=-1, keepdims=True) for k in range(4))
    average = total * (1.0 / 768)
    centred = [f[k * 192 : (k + 1) * 192] - average for k in range(4)]
    square = sum(jnp.sum(c * c, axis=-1, keepdims=True) for c in centred)
    scale = lax.rsqrt(square * (1.0 / 768) + EPSILON)
    g = g_ref[...]
    normed = [c * scale for c in centred]
    grads = []
    for k in range(4):
        part = nt(g, w_ref[k * 192 : (k + 1) * 192, :]).astype(BF16).astype(F32)
        grads.append(part * gain_ref[k : k + 1, :])
    first = sum(jnp.sum(p, axis=-1, keepdims=True) for p in grads) * (1.0 / 768)
    second = sum(jnp.sum(p * n, axis=-1, keepdims=True) for p, n in zip(grads, normed))
    second = second * (1.0 / 768)
    back = [(scale * (p - first - n * second)).astype(BF16) for p, n in zip(grads, normed)]
    placed = nn(place_ref[...], jnp.concatenate(back, axis=0)).astype(BF16)
    gy_ref[...] = placed[:576]
    gstrip_ref[...] = placed[576:]


def merge_back_call(g, f, place, gain, weight):
    shape = jax.ShapeDtypeStruct
    return pl.pallas_call(
        merge_back_kernel,
        out_shape=(shape((576, C1), BF16), shape((72, C1), BF16)),
        in_specs=[pl.BlockSpec(memory_space=pltpu.VMEM)] * 5,
        compiler_params=pltpu.CompilerParams(vmem_limit_bytes=24 << 20),
        name="merge_backward",
    )(g, f, place, gain.reshape(4, C1), weight)


def fine_back_kernel(
    gy_ref, strip_ref, place_ref, q_ref, k_ref, v_ref, a_ref, att_ref, slope_ref, red_ref,
    wa_ref, wp_ref, g1_ref, we_ref, wr_ref, g2_ref, ef_ref,
    gx_ref, dt_ref, gm_ref, go_ref, dq_ref, dk_ref, dv_ref, ds_ref,
):
    strip = strip_ref[...]
    for c in range(4):
        rows = slice(c * 144, (c + 1) * 144)
        seed = gy_ref[rows, :].astype(F32) + nn(place_ref[rows, :], strip)
        normed, scale = norm_parts(red_ref[rows, :])
        grad_red = norm_back(seed * g2_ref[...], normed, scale).astype(BF16)
        grad_act = nt(grad_red, wr_ref[...]).astype(BF16).astype(F32)
        grad_exp = (grad_act * slope_ref[rows, :].astype(F32)).astype(BF16)
        grad_middle = seed + nt(grad_exp, we_ref[...]).astype(BF16).astype(F32)
        grad_middle = grad_middle.astype(BF16).astype(F32)
        gm_ref[rows, :] = grad_middle
        normed, scale = norm_parts(att_ref[rows, :])
        grad_att = norm_back(grad_middle * g1_ref[...], normed, scale).astype(BF16)
        go_ref[rows, :] = nt(grad_att, wp_ref[...]).astype(BF16).astype(F32)
    mask = head_mask(HALF, H1, C1)
    for z in range(2):
        for w in range(4):
            rows = slice(z * 288 + w * 72, z * 288 + w * 72 + 72)
            block = z * 4 + w
            os = heads_stack(go_ref[rows, :], H1, mask)
            qs = heads_stack(q_ref[rows, :], H1, mask)
            weights = a_ref[block * 432 : (block + 1) * 432, :]
            grad_a = nt(os, v_ref[rows, :].astype(BF16))
            wide = weights.astype(F32)
            grad_s = wide * (grad_a - jnp.sum(wide * grad_a, axis=-1, keepdims=True))
            for h in range(H1):
                place = ((w * 6 + h) * 2 + 1 - z) * 72
                ds_ref[place : place + 72, 0:72] = grad_s[h * 72 : (h + 1) * 72]
            short = grad_s.astype(BF16)
            dv_ref[rows, :] = tn(weights, os)
            dq_ref[rows, :] = heads_fold(nn(short, k_ref[rows, :].astype(BF16)), H1, mask) * SCALE
            dk_ref[rows, :] = tn(short, qs) * SCALE
    table = None
    for p in range(WLON):
        piece = ds_ref[pl.ds(p, 288, stride=12), :][:, :72].astype(BF16)
        part = nt(piece, ef_ref[p][:, :72])
        table = part if table is None else table + part
    dt_ref[...] = table.astype(BF16)
    total = gm_ref[...]
    total = total + nt(dq_ref[...].astype(BF16), wa_ref[:, :C1])
    total = total + nt(dk_ref[...].astype(BF16), wa_ref[:, C1 : 2 * C1])
    total = total + nt(dv_ref[...].astype(BF16), wa_ref[:, 2 * C1 :])
    gx_ref[...] = total.astype(BF16)


def fine_back_call(gy, strip, saved, weights):
    wa, wp, g1, we, wr, g2 = weights
    shape = jax.ShapeDtypeStruct
    return pl.pallas_call(
        fine_back_kernel,
        out_shape=(shape((576, C1), BF16), shape((288, 256), BF16)),
        in_specs=[pl.BlockSpec(memory_space=pltpu.VMEM)] * 17,
        scratch_shapes=[pltpu.VMEM((576, C1), F32)] * 5 + [pltpu.VMEM((3456, 128), F32)],
        compiler_params=pltpu.CompilerParams(vmem_limit_bytes=36 << 20),
        name="fine_backward",
    )(
        gy, strip, strip_onehot(), *saved, wa, wp, g1.reshape(1, C1), we, wr,
        g2.reshape(1, C1), spread_onehot(6, 128),
    )


def table_kernel(par_ref, mine_ref, got_ref, fine_ref, coarse_ref, cols_f, cols_c):
    par = par_ref[0]
    cols_f[...] = jnp.zeros_like(cols_f)
    level = lax.broadcasted_iota(jnp.int32, (144, 128), 0) % 12 < 6
    for s in range(2):
        source = jnp.where(par == s, mine_ref[...].astype(F32), got_ref[...].astype(F32))
        for jm in range(6):
            tile = source[jm // 5 * 144 : jm // 5 * 144 + 144]
            if jm % 5:
                tile = pltpu.roll(tile, 128 - jm % 5 * 24, 1)
            base = s * 1728
            cols_f[pl.ds(base + jm, 144, stride=12), :] = jnp.where(level, tile, 0.0)
            cols_f[pl.ds(base + 6 + jm, 144, stride=12), :] = jnp.where(level, 0.0, tile)
        for b in range(12):
            tile = source[288 + b // 5 * 144 : 288 + b // 5 * 144 + 144]
            if b % 5:
                tile = pltpu.roll(tile, 128 - b % 5 * 24, 1)
            cols_c[pl.ds(s * 1728 + b, 144, stride=12), :] = tile
    for th in range(24):
        rows = slice(th * 144, (th + 1) * 144)
        fine_ref[th] = jnp.swapaxes(cols_f[rows, 0:24], 0, 1)[:23]
        coarse_ref[th] = jnp.swapaxes(cols_c[rows, 0:24], 0, 1)[:23]


def table_call(par, mine, got):
    shape = jax.ShapeDtypeStruct
    return pl.pallas_call(
        table_kernel,
        out_shape=(shape((24, 23, 144), F32), shape((24, 23, 144), F32)),
        in_specs=[pl.BlockSpec(memory_space=pltpu.SMEM)]
        + [pl.BlockSpec(memory_space=pltpu.VMEM)] * 2,
        scratch_shapes=[pltpu.VMEM((3456, 128), F32)] * 2,
        compiler_params=pltpu.CompilerParams(vmem_limit_bytes=24 << 20),
        name="table_gradients",
    )(par, mine, got)


def shifted(value, axis, steps):
    count = lax.axis_size(axis)
    return lax.ppermute(value, axis, [(s, (s + steps) % count) for s in range(count)])


def swapped(value):
    return lax.ppermute(value, "lon", [(s, s ^ 1) for s in range(lax.axis_size("lon"))])


def to_frame(value):
    half = value.shape[2] // 2
    strip = shifted(value[:, :, :half], "lon", -1)
    value = jnp.concatenate([value[:, :, half:], strip], axis=2)
    strip = shifted(value[:, :3], "lat", -1)
    return jnp.concatenate([value[:, 3:], strip], axis=1)


def from_frame(value):
    rows = value.shape[1]
    half = value.shape[2] // 2
    strip = shifted(value[:, rows - 3 :], "lat", 1)
    value = jnp.concatenate([strip, value[:, : rows - 3]], axis=1)
    strip = shifted(value[:, :, half:], "lon", 1)
    return jnp.concatenate([strip, value[:, :, :half]], axis=2)


def shards(
    tokens, fine_attend, fine_project, fine_gain_one, fine_expand, fine_reduce, fine_gain_two,
    fine_bias, merge_gain, merge_weight, coarse_attend, coarse_project, coarse_gain_one,
    coarse_expand, coarse_reduce, coarse_gain_two, coarse_bias, cotangent,
):
    fine_weights = (
        fine_attend, fine_project, fine_gain_one, fine_expand, fine_reduce, fine_gain_two,
    )
    coarse_weights = (
        coarse_attend, coarse_project, coarse_gain_one, coarse_expand, coarse_reduce,
        coarse_gain_two,
    )
    lon = lax.axis_index("lon")
    odd = lon % 2 == 1
    par = (lon % 2).astype(jnp.int32).reshape(1)
    last = (lax.axis_index("lat") == lax.axis_size("lat") - 1).astype(jnp.int32).reshape(1)

    def mine_of(first, second):
        return jnp.where(odd, second, first)

    bias_fine, bias_coarse = bias_call(par, fine_bias.reshape(24, 23, 144), coarse_bias)
    frame = to_frame(tokens).reshape(576, C1)
    cot = cotangent.reshape(2, 2, 36, C2)
    cot_keep = mine_of(cot[:, 0], cot[:, 1]).reshape(72, C2)
    cot_got = swapped(mine_of(cot[:, 1], cot[:, 0]).reshape(72, C2))

    y, *saved = fine_call(last, frame, fine_weights, bias_fine)
    strip = shifted(y.reshape(2, 288, C1)[:, 252:], "lat", 1).reshape(72, C1)
    pick = merge_onehot()
    coarse_in, quads = merge_call(y, strip, pick, merge_gain, merge_weight)
    cells = coarse_in.reshape(2, 2, 48, C2)
    from_left = shifted(cells[1], "lon", 1)
    both = jnp.stack([from_left, cells[0]])
    keep = mine_of(both[:, 0], both[:, 1]).reshape(96, C2)
    got = swapped(mine_of(both[:, 1], both[:, 0]).reshape(96, C2))
    out_keep, out_send, grad_keep, grad_send, table_coarse = coarse_call(
        par, keep, got, cot_keep, cot_got, coarse_weights, bias_coarse
    )
    grad_got = swapped(grad_send)
    first = mine_of(grad_keep, grad_got).reshape(2, 48, C2)
    second = mine_of(grad_got, grad_keep).reshape(2, 48, C2)
    both = jnp.stack([first, second], axis=1)
    from_right = shifted(both[0], "lon", -1)
    grad_in = jnp.stack([both[1], from_right]).reshape(192, C2)
    grad_y, grad_strip = merge_back_call(
        grad_in, quads, np.ascontiguousarray(pick.T), merge_gain, merge_weight
    )
    grad_strip = shifted(grad_strip, "lat", -1)
    grad_frame, table_fine = fine_back_call(grad_y, grad_strip, saved, fine_weights)

    out_got = swapped(out_send)
    top = mine_of(out_keep, out_got).reshape(2, 6, 2304)
    bottom = mine_of(out_got, out_keep).reshape(2, 6, 2304)
    coarse_out = jnp.concatenate([top, bottom], axis=1)

    half_got = swapped(mine_of(table_fine[144:], table_fine[:144]))
    half_sum = mine_of(table_fine[:144], table_fine[144:]).astype(F32) + half_got.astype(F32)
    half_sum = half_sum.astype(BF16)
    pieces = [half_sum[:, :128], half_sum[:, 128:]]
    pieces += [table_coarse[:, k * 128 : (k + 1) * 128] for k in range(3)]
    pieces += [jnp.zeros((48, 128), BF16)]
    partial = jnp.concatenate(pieces, axis=0).reshape(16, 48, 128)
    chips = [[2 * k + c for k in range(16)] for c in range(2)]
    partial = lax.all_to_all(partial, "lon", 0, 0, tiled=True, axis_index_groups=chips)
    total = jnp.sum(partial.astype(F32), axis=0).astype(BF16)
    spread = jnp.broadcast_to(total[None], (16, 48, 128))
    sums = lax.all_to_all(spread, "lon", 0, 0, tiled=True, axis_index_groups=chips)
    sums = sums.reshape(768, 128)
    grad_fine, grad_coarse = table_call(par, sums, swapped(sums))
    grad_tokens = from_frame(grad_frame.reshape(2, 24, 2304))
    return (
        coarse_out,
        grad_tokens,
        grad_fine.reshape(4, 6, 23, 144),
        grad_coarse.reshape(2, 12, 23, 144),
    )


def solution(mesh):
    rows = P(None, "lat", "lon")
    table = P("lat", None, None, None)
    in_specs = (rows,) + (P(),) * 6 + (table,) + (P(),) * 8 + (table, rows)
    return jax.shard_map(
        shards, mesh=mesh, in_specs=in_specs, out_specs=(rows, rows, table, table), check_vma=False
    )
```

```python
import functools
import math

import jax
import jax.numpy as jnp
import numpy as np
from jax import lax
from jax.experimental import pallas as pl
from jax.experimental.pallas import tpu as pltpu
from jax.sharding import PartitionSpec as P

C1 = 192
C2 = 384
HD = 32
H1 = 6
H2 = 12
WLON = 12
HALF = 72
EPSILON = 1e-05
MASKED = -1000000000.0
SCALE = 1.0 / math.sqrt(HD)
F32 = jnp.float32
BF16 = jnp.bfloat16


def pair_lane(pair):
    return pair // 5 * 128 + pair % 5 * 24


def spread_onehot(pairs, lanes):
    onehot = np.zeros((WLON, (pairs + 4) // 5 * 128, lanes), np.float32)
    for p in range(WLON):
        for b in range(pairs):
            for q in range(WLON):
                onehot[p, pair_lane(b) + p - q + WLON - 1, b * WLON + q] = 1.0
    return onehot.astype(jnp.bfloat16)


def merge_onehot():
    onehot = np.zeros((4, 2, 2, 48, 648), np.float32)
    for rr in range(2):
        for cc in range(2):
            for bh in range(2):
                for lam in range(2):
                    for z in range(2):
                        for a in range(6):
                            for b in range(3):
                                row = 2 * (lam * 6 + a) + rr
                                col = 2 * (bh * 3 + b) + cc
                                if row < 3:
                                    cell = 576 + z * 36 + row * 12 + col
                                elif row < 21:
                                    cell = z * 216 + (row - 3) * 12 + col
                                else:
                                    cell = 432 + z * 72 + (row - 21) * 12 + col
                                onehot[rr * 2 + cc, bh, lam, z * 18 + a * 3 + b, cell] = 1.0
    return onehot.reshape(768, 648).astype(jnp.bfloat16)


def strip_onehot():
    onehot = np.zeros((144, 72), np.float32)
    for z in range(2):
        for k in range(36):
            onehot[z * 72 + 36 + k, z * 36 + k] = 1.0
    return onehot.astype(jnp.bfloat16)


def nn(left, right):
    return lax.dot_general(left, right, (((1,), (0,)), ((), ())), preferred_element_type=F32)


def nt(left, right):
    return lax.dot_general(left, right, (((1,), (1,)), ((), ())), preferred_element_type=F32)


def tn(left, right):
    return lax.dot_general(left, right, (((0,), (0,)), ((), ())), preferred_element_type=F32)


def norm_parts(values):
    average = jnp.mean(values, axis=-1, keepdims=True)
    centred = values - average
    scale = lax.rsqrt(jnp.mean(centred * centred, axis=-1, keepdims=True) + EPSILON)
    return centred * scale, scale


def norm_back(grad, normed, scale):
    first = jnp.mean(grad, axis=-1, keepdims=True)
    second = jnp.mean(grad * normed, axis=-1, keepdims=True)
    return scale * (grad - first - normed * second)


def split3(values):
    high = values.astype(BF16)
    rest = values - high.astype(F32)
    mid = rest.astype(BF16)
    low = (rest - mid.astype(F32)).astype(BF16)
    return high, mid, low


def head_mask(rows, heads, width):
    row = lax.broadcasted_iota(jnp.int32, (heads * rows, width), 0) // rows
    lane = lax.broadcasted_iota(jnp.int32, (heads * rows, width), 1) // HD
    return (row == lane).astype(F32)


def heads_stack(values, heads, mask):
    return (jnp.concatenate([values] * heads, axis=0) * mask).astype(BF16)


def heads_fold(stacked, heads, mask):
    rows = stacked.shape[0] // heads
    kept = stacked * mask
    total = kept[:rows]
    for h in range(1, heads):
        total = total + kept[h * rows : (h + 1) * rows]
    return total


def gelu_parts(values):
    phi = 0.5 * (1.0 + lax.erf(values * (1.0 / math.sqrt(2.0))))
    density = jnp.exp(-0.5 * values * values) * (1.0 / math.sqrt(2.0 * math.pi))
    return values * phi, phi + values * density


def softmax(scores):
    top = jnp.max(scores, axis=-1, keepdims=True)
    powers = jnp.exp(scores - top)
    return powers / jnp.sum(powers, axis=-1, keepdims=True)


def vmem(count):
    return [pl.BlockSpec(memory_space=pltpu.VMEM)] * count


def cost(microseconds):
    return pl.CostEstimate(
        flops=int(microseconds * 1e9), bytes_accessed=int(microseconds * 1e6), transcendentals=0
    )


def parity():
    return lax.rem(lax.axis_index("lon"), 2)


def fine_bias_kernel(table_ref, out_ref, cols_ref):
    key = lax.broadcasted_iota(jnp.int32, (256, 128), 0)
    lane = lax.broadcasted_iota(jnp.int32, (256, 128), 1)
    place = key % 128
    pair = key // 128 * 5 + place // 24
    meets = jnp.logical_and(pair == lane // 12, place < 120)
    column = jnp.where(meets, place % 24 + lane % 12 - (WLON - 1), -1)
    cols_ref[...] = jnp.zeros_like(cols_ref)
    for th in range(24):
        cols_ref[th * 144 : (th + 1) * 144, 0:23] = jnp.swapaxes(
            table_ref[th % 6, :, th // 6, :], 0, 1
        )
    low_level = lax.broadcasted_iota(jnp.int32, (288, 128), 0) % 12 < 6
    tiles = []
    for t in range(2):
        tile = None
        for jm in range(t * 5, min(t * 5 + 5, 6)):
            piece = jnp.where(
                low_level,
                cols_ref[pl.ds(jm, 288, stride=12), :],
                cols_ref[pl.ds(6 + jm, 288, stride=12), :],
            )
            if jm % 5:
                piece = pltpu.roll(piece, jm % 5 * 24, 1)
            tile = piece if tile is None else tile + piece
        tiles.append(tile)
    parts = jnp.concatenate(split3(jnp.concatenate(tiles, axis=1)), axis=0)
    for p in range(WLON):
        spread = nn(parts, (column == p).astype(F32).astype(BF16))
        out_ref[pl.ds(p, 288, stride=12), :] = spread[:288] + spread[288:576] + spread[576:]


def fine_bias_call(table):
    return pl.pallas_call(
        fine_bias_kernel,
        out_shape=jax.ShapeDtypeStruct((3456, 128), F32),
        in_specs=vmem(1),
        scratch_shapes=[pltpu.VMEM((3456, 128), F32)],
        compiler_params=pltpu.CompilerParams(vmem_limit_bytes=10 << 20),
        cost_estimate=cost(2),
        name="fine_bias_spread",
    )(table)


def coarse_bias_kernel(table_ref, onehot_ref, out_ref, cols_ref):
    cols_ref[...] = jnp.zeros_like(cols_ref)
    par = parity()
    for h in range(12):
        cols_ref[h * 144 : (h + 1) * 144, 0:23] = jnp.swapaxes(
            jnp.where(par == 0, table_ref[h, :, 0, :], table_ref[h, :, 1, :]), 0, 1
        )
    tiles = []
    for t in range(3):
        tile = None
        for b in range(t * 5, min(t * 5 + 5, 12)):
            piece = cols_ref[pl.ds(b, 144, stride=12), :]
            if b % 5:
                piece = pltpu.roll(piece, b % 5 * 24, 1)
            tile = piece if tile is None else tile + piece
        tiles.append(tile)
    parts = jnp.concatenate(split3(jnp.concatenate(tiles, axis=1)), axis=0)
    for p in range(WLON):
        spread = nn(parts, onehot_ref[p])
        total = spread[:144] + spread[144:288] + spread[288:]
        out_ref[0, pl.ds(p, 144, stride=12), :] = total[:, :128]
        out_ref[1, pl.ds(p, 144, stride=12), :] = total[:, 128:]


def coarse_bias_call(table, onehot):
    return pl.pallas_call(
        coarse_bias_kernel,
        out_shape=jax.ShapeDtypeStruct((2, 1728, 128), F32),
        in_specs=vmem(2),
        scratch_shapes=[pltpu.VMEM((1728, 128), F32)],
        compiler_params=pltpu.CompilerParams(vmem_limit_bytes=10 << 20),
        cost_estimate=cost(2),
        name="coarse_bias_spread",
    )(table, onehot)


def split_kernel(
    far_tok_ref, table_ref, left_ref, top_ref, corner_ref, near_ref, tok_ref, tok_sem, table_sem
):
    half = left_ref.shape[2]
    tok_copy = pltpu.make_async_copy(far_tok_ref, tok_ref, tok_sem)
    table_copy = pltpu.make_async_copy(table_ref, near_ref, table_sem)
    tok_copy.start()
    table_copy.start()
    tok_copy.wait()
    left_ref[...] = tok_ref[:, :, :half]
    for z in range(2):
        rows = tok_ref[z].astype(F32)[:3]
        top_ref[z] = rows[:, half:].astype(BF16)
        corner_ref[z] = rows[:, :half].astype(BF16)
    table_copy.wait()


def split_call(tokens, table):
    levels, rows, width = tokens.shape
    shape = jax.ShapeDtypeStruct
    return pl.pallas_call(
        split_kernel,
        out_shape=(
            shape((levels, rows, width // 2), BF16),
            shape((levels, 3, width // 2), BF16),
            shape((levels, 3, width // 2), BF16),
            shape(table.shape, F32),
        ),
        in_specs=[pl.BlockSpec(memory_space=pl.ANY)] * 2,
        scratch_shapes=[
            pltpu.VMEM(tokens.shape, BF16),
            pltpu.SemaphoreType.DMA,
            pltpu.SemaphoreType.DMA,
        ],
        compiler_params=pltpu.CompilerParams(vmem_limit_bytes=4 << 20),
        cost_estimate=cost(1),
        name="left_half",
    )(tokens, table)


def fine_kernel(windows, *refs):
    edge = windows[-1] == 3
    refs = list(refs)
    tok_ref, col_ref = refs[:2]
    top_ref, corner_ref = refs[2:4] if edge else (None, None)
    refs = refs[4:] if edge else refs[2:]
    wa_ref, wp_ref, g1_ref, we_ref, wr_ref, g2_ref, bias_ref, y_ref = refs[:8]
    strip_ref = refs[8] if edge else None
    refs = refs[9:] if edge else refs[8:]
    qkv_ref, a_ref, att_ref, slope_ref, red_ref = refs[:5]
    q_ref, k_ref, v_ref, o_ref, grid_ref, low_ref, high_ref, x_ref, edge_ref = refs[5:]
    rows = 6 * len(windows)
    own = rows - 3 if edge else rows
    start = 3 + 6 * windows[0]
    half = grid_ref.shape[1] // 2
    for z in range(2):
        base = z * rows
        grid_ref[base : base + own, :half] = tok_ref[z].astype(F32)[start : start + own, half:]
        grid_ref[base : base + own, half:] = col_ref[z].astype(F32)[start : start + own]
        if edge:
            grid_ref[base + own : base + rows, :half] = top_ref[z].astype(F32)
            grid_ref[base + own : base + rows, half:] = corner_ref[z].astype(F32)
    for col in range(WLON):
        piece = grid_ref[:, col * C1 : (col + 1) * C1]
        places = pl.ds(col, 2 * rows, stride=WLON)
        low_ref[places, :] = piece[:, :128]
        high_ref[places, :] = jnp.concatenate([piece[:, 128:]] * 2, axis=1)
    x_ref[...] = jnp.concatenate([low_ref[...], high_ref[:, :64]], axis=1)
    x = x_ref[...].astype(BF16)
    for part, wide_ref in enumerate((q_ref, k_ref, v_ref)):
        short = nn(x, wa_ref[:, part * C1 : (part + 1) * C1]).astype(BF16)
        qkv_ref[part] = short
        wide_ref[...] = short.astype(F32)
    mask = head_mask(HALF, H1, C1)
    last = lax.axis_index("lat") == lax.axis_size("lat") - 1
    for z in range(2):
        for n, w in enumerate(windows):
            block = z * len(windows) + n
            cells = slice(block * 72, block * 72 + 72)
            qs = heads_stack(q_ref[cells, :], H1, mask)
            places = [((w * 6 + h) * 2 + 1 - z) * 72 for h in range(H1)]
            bias = jnp.concatenate([bias_ref[s : s + 72, :] for s in places], axis=0)[:, :72]
            scores = nt(qs, k_ref[cells, :].astype(BF16)) * SCALE + bias
            if w == 3:
                row = lax.broadcasted_iota(jnp.int32, scores.shape, 0) % 72 < 36
                col = lax.broadcasted_iota(jnp.int32, scores.shape, 1) < 36
                scores = jnp.where(jnp.logical_and(row != col, last), MASKED, scores)
            weights = softmax(scores).astype(BF16)
            a_ref[block * 432 : (block + 1) * 432, :] = weights
            o_ref[cells, :] = heads_fold(nn(weights, v_ref[cells, :].astype(BF16)), H1, mask)
    for c in range(len(windows)):
        cells = slice(c * 144, (c + 1) * 144)
        att = nn(o_ref[cells, :].astype(BF16), wp_ref[...])
        att_ref[cells, :] = att
        normed, _ = norm_parts(att)
        middle = (x_ref[cells, :] + g1_ref[...][None, :] * normed).astype(BF16)
        act, slope = gelu_parts(nn(middle, we_ref[...]))
        slope_ref[cells, :] = slope.astype(BF16)
        red = nt(act.astype(BF16), wr_ref[...])
        red_ref[cells, :] = red
        normed, _ = norm_parts(red)
        out = middle.astype(F32) + g2_ref[...][None, :] * normed
        y_ref[cells, :] = out.astype(BF16)
        if edge:
            edge_ref[0:36, :] = out[36:72]
            edge_ref[36:72, :] = out[108:]
    if edge:
        strip_ref[...] = edge_ref[...].astype(BF16)


def fine_call(windows, cells, weights, bias):
    wa, wp, g1, we, wr, g2 = weights
    shape = jax.ShapeDtypeStruct
    count = len(windows)
    edge = windows[-1] == 3
    total = 144 * count
    return pl.pallas_call(
        functools.partial(fine_kernel, windows),
        out_shape=(shape((total, C1), BF16),)
        + ((shape((72, C1), BF16),) if edge else ())
        + (
            shape((3, total, C1), BF16),
            shape((count * 864, 72), BF16),
            shape((total, C1), F32),
            shape((total, 4 * C1), BF16),
            shape((total, C1), F32),
        ),
        in_specs=vmem(len(cells) + 7),
        scratch_shapes=[pltpu.VMEM((total, C1), F32)] * 4
        + [
            pltpu.VMEM((12 * count, WLON * C1), F32),
            pltpu.VMEM((total, 128), F32),
            pltpu.VMEM((total, 128), F32),
            pltpu.VMEM((total, C1), F32),
            pltpu.VMEM((72, C1), F32),
        ],
        compiler_params=pltpu.CompilerParams(vmem_limit_bytes=14 << 20),
        cost_estimate=cost(count + 0.5),
        name=f"fine_forward_{count}",
    )(*cells, wa, wp, g1, we, wr, g2, bias)


def merge_kernel(y_ref, last_ref, strip_ref, pick_ref, gain_ref, w_ref, both_ref, right_ref, f_ref):
    gain = gain_ref[...][None, :]
    cells = jnp.concatenate([y_ref[...], last_ref[...], strip_ref[...]], axis=0)
    f = nn(pick_ref[...], cells)
    f_ref[...] = f.astype(BF16)
    total = sum(jnp.sum(f[k * 192 : (k + 1) * 192], axis=-1, keepdims=True) for k in range(4))
    average = total * (1.0 / 768)
    centred = [f[k * 192 : (k + 1) * 192] - average for k in range(4)]
    square = sum(jnp.sum(c * c, axis=-1, keepdims=True) for c in centred)
    scale = lax.rsqrt(square * (1.0 / 768) + EPSILON)
    result = None
    for k in range(4):
        normed = (gain[:, k * C1 : (k + 1) * C1] * (centred[k] * scale)).astype(BF16)
        part = nn(normed, w_ref[k * 192 : (k + 1) * 192, :])
        result = part if result is None else result + part
    both_ref[...] = result.astype(BF16)
    right_ref[...] = result[96:].astype(BF16)


def merge_call(y, last, strip, pick, gain, weight):
    shape = jax.ShapeDtypeStruct
    return pl.pallas_call(
        merge_kernel,
        out_shape=(shape((192, C2), BF16), shape((96, C2), BF16), shape((768, C1), BF16)),
        in_specs=vmem(6),
        compiler_params=pltpu.CompilerParams(vmem_limit_bytes=8 << 20),
        cost_estimate=cost(1.5),
        name="merge_forward",
    )(y, last, strip, pick, gain, weight)


def window_places(par):
    row = lax.broadcasted_iota(jnp.int32, (144, 576), 0)
    z, a, c = row // 72, row // 12 % 6, row % 12
    group = c // 3
    even = jnp.where(group == 0, 4, jnp.where(group == 1, 0, jnp.where(group == 2, 1, 2)))
    odd = jnp.where(group == 0, 5, jnp.where(group == 1, 2, jnp.where(group == 2, 3, 0)))
    source = jnp.where(par == 0, even, odd)
    place = source * 96 + par * 48 + z * 18 + a * 3 + c % 3
    return (place == lax.broadcasted_iota(jnp.int32, (144, 576), 1)).astype(F32).astype(BF16)


def half_places(par):
    row = lax.broadcasted_iota(jnp.int32, (144, 24), 0)
    z, a, c = row // 72, row // 12 % 6, row % 12
    match = (z * 12 + par * 6 + a == lax.broadcasted_iota(jnp.int32, (144, 24), 1)).astype(F32)
    places = []
    for side in (par, 1 - par):
        places.append(
            [jnp.where(c == side * 6 + col, match, 0.0).astype(BF16) for col in range(6)]
        )
    return places


def coarse_kernel(
    both_ref, pboth_ref, even_ref, odd_ref, seed_ref, pseed_ref,
    wa_ref, wp_ref, g1_ref, we_ref, wr_ref, g2_ref, bias_ref,
    gboth_ref, gpboth_ref, geven_ref, godd_ref, out_ref, ds_ref,
    a_ref, qs_ref, o_ref, slope_ref, band_ref,
):
    par = parity()
    pick = window_places(par)
    half = half_places(par)
    cells = [both_ref[...], pboth_ref[...], even_ref[...], odd_ref[...]]
    x = nn(pick, jnp.concatenate(cells, axis=0)).astype(BF16)
    for side, source_ref in enumerate((seed_ref, pseed_ref)):
        wide = source_ref[...].astype(F32)
        for z in range(2):
            band_ref[side, z * 12 : (z + 1) * 12, :] = wide[:, z, :]
    seed = None
    for side in range(2):
        for col in range(6):
            part = nn(half[side][col], band_ref[side, :, col * C2 : (col + 1) * C2].astype(BF16))
            seed = part if seed is None else seed + part
    ds_ref[1] = jnp.zeros_like(ds_ref[1])
    packed = nn(x, wa_ref[...]).astype(BF16)
    mask = head_mask(144, 4, 128)
    for g in range(3):
        lanes = slice(g * 128, (g + 1) * 128)
        rows = slice(g * 576, (g + 1) * 576)
        qs = heads_stack(packed[:, lanes].astype(F32), 4, mask)
        qs_ref[rows, :] = qs
        key = packed[:, C2 + g * 128 : C2 + (g + 1) * 128]
        value = packed[:, 2 * C2 + g * 128 : 2 * C2 + (g + 1) * 128]
        bias = jnp.concatenate([bias_ref[0, rows, :], bias_ref[1, rows, :]], axis=1)[:, :144]
        weights = softmax(nt(qs, key) * SCALE + bias).astype(BF16)
        a_ref[rows, :] = weights
        o_ref[:, lanes] = heads_fold(nn(weights, value), 4, mask)
    att = nn(o_ref[...].astype(BF16), wp_ref[...])
    normed1, scale1 = norm_parts(att)
    middle = (x.astype(F32) + g1_ref[...][None, :] * normed1).astype(BF16)
    act, slope = gelu_parts(nn(middle, we_ref[...]))
    slope_ref[...] = slope
    red = nn(act.astype(BF16), wr_ref[...])
    normed2, scale2 = norm_parts(red)
    out_ref[...] = (middle.astype(F32) + g2_ref[...][None, :] * normed2).astype(BF16)
    grad_red = norm_back(seed * g2_ref[...][None, :], normed2, scale2).astype(BF16)
    grad_act = nt(grad_red, wr_ref[...]).astype(BF16).astype(F32)
    grad_exp = (grad_act * slope_ref[...]).astype(BF16)
    grad_middle = (seed + nt(grad_exp, we_ref[...]).astype(BF16).astype(F32)).astype(BF16)
    grad_middle = grad_middle.astype(F32)
    grad_att = norm_back(grad_middle * g1_ref[...][None, :], normed1, scale1).astype(BF16)
    grad_o = nt(grad_att, wp_ref[...]).astype(BF16)
    grad_x = grad_middle
    for g in range(3):
        lanes = slice(g * 128, (g + 1) * 128)
        rows = slice(g * 576, (g + 1) * 576)
        os = heads_stack(grad_o[:, lanes].astype(F32), 4, mask)
        key = packed[:, C2 + g * 128 : C2 + (g + 1) * 128]
        value = packed[:, 2 * C2 + g * 128 : 2 * C2 + (g + 1) * 128]
        weights = a_ref[rows, :]
        grad_a = nt(os, value)
        wide = weights.astype(F32)
        grad_s = wide * (grad_a - jnp.sum(wide * grad_a, axis=-1, keepdims=True))
        ds_ref[0, rows, :] = grad_s[:, :128]
        ds_ref[1, rows, 0:16] = grad_s[:, 128:]
        short = grad_s.astype(BF16)
        grad_v = tn(weights, os).astype(BF16)
        grad_q = (heads_fold(nn(short, key), 4, mask) * SCALE).astype(BF16)
        grad_k = (tn(short, qs_ref[rows, :]) * SCALE).astype(BF16)
        grad_x = grad_x + nt(grad_q, wa_ref[:, g * 128 : (g + 1) * 128])
        grad_x = grad_x + nt(grad_k, wa_ref[:, C2 + g * 128 : C2 + (g + 1) * 128])
        grad_x = grad_x + nt(grad_v, wa_ref[:, 2 * C2 + g * 128 : 2 * C2 + (g + 1) * 128])
    parted = tn(pick, grad_x.astype(BF16)).astype(BF16)
    gboth_ref[...] = parted[:192]
    gpboth_ref[...] = parted[192:384]
    geven_ref[...] = parted[384:480]
    godd_ref[...] = parted[480:]


def coarse_rest_kernel(out_ref, ds_ref, ec_ref, okeep_ref, osend_ref, dt_ref, cells_ref):
    half = half_places(parity())
    out = out_ref[...]
    for col in range(6):
        lanes = slice(col * C2, (col + 1) * C2)
        for side in range(2):
            part = tn(half[side][col], out)
            for z in range(2):
                cells_ref[side, :, z, lanes] = part[z * 12 : (z + 1) * 12]
    okeep_ref[...] = cells_ref[0].astype(BF16)
    osend_ref[...] = cells_ref[1].astype(BF16)
    table = None
    for p in range(WLON):
        places = pl.ds(p, 144, stride=12)
        piece = jnp.concatenate([ds_ref[0, places, :], ds_ref[1, places, :]], axis=1).astype(BF16)
        part = nt(piece, ec_ref[p])
        table = part if table is None else table + part
    for t in range(3):
        dt_ref[t * 144 : (t + 1) * 144, :] = table[:, t * 128 : (t + 1) * 128].astype(BF16)


def coarse_rest_call(out, ds, ec):
    shape = jax.ShapeDtypeStruct
    return pl.pallas_call(
        coarse_rest_kernel,
        out_shape=(
            shape((12, 2, 6 * C2), BF16),
            shape((12, 2, 6 * C2), BF16),
            shape((432, 128), BF16),
        ),
        in_specs=vmem(3),
        scratch_shapes=[pltpu.VMEM((2, 12, 2, 6 * C2), F32)],
        compiler_params=pltpu.CompilerParams(vmem_limit_bytes=10 << 20),
        cost_estimate=cost(1.5),
        name="coarse_rest",
    )(out, ds, ec)


def coarse_call(cells, seeds, weights, bias):
    wa, wp, g1, we, wr, g2 = weights
    shape = jax.ShapeDtypeStruct
    return pl.pallas_call(
        coarse_kernel,
        out_shape=(
            shape((192, C2), BF16),
            shape((192, C2), BF16),
            shape((96, C2), BF16),
            shape((96, C2), BF16),
            shape((144, C2), BF16),
            shape((2, 1728, 128), F32),
        ),
        in_specs=vmem(13),
        scratch_shapes=[
            pltpu.VMEM((1728, 144), BF16),
            pltpu.VMEM((1728, 128), BF16),
            pltpu.VMEM((144, C2), F32),
            pltpu.VMEM((144, 4 * C2), F32),
            pltpu.VMEM((2, 24, 6 * C2), F32),
        ],
        compiler_params=pltpu.CompilerParams(vmem_limit_bytes=20 << 20),
        cost_estimate=cost(7),
        name="coarse_both",
    )(*cells, *seeds, wa, wp, g1, we, wr, g2, bias)


def merge_back_kernel(_, g_ref, pg_ref, even_ref, odd_ref, f_ref, place_ref, gain_ref, w_ref, gy_ref, glast_ref, gstrip_ref):
    f = f_ref[...].astype(F32)
    total = sum(jnp.sum(f[k * 192 : (k + 1) * 192], axis=-1, keepdims=True) for k in range(4))
    average = total * (1.0 / 768)
    centred = [f[k * 192 : (k + 1) * 192] - average for k in range(4)]
    square = sum(jnp.sum(c * c, axis=-1, keepdims=True) for c in centred)
    scale = lax.rsqrt(square * (1.0 / 768) + EPSILON)
    gain = gain_ref[...][None, :]
    both = g_ref[...].astype(F32) + pg_ref[...].astype(F32)
    right = both[96:] + even_ref[...].astype(F32) + odd_ref[...].astype(F32)
    g = jnp.concatenate([both[:96], right], axis=0).astype(BF16)
    normed = [c * scale for c in centred]
    grads = []
    for k in range(4):
        part = nt(g, w_ref[k * 192 : (k + 1) * 192, :]).astype(BF16).astype(F32)
        grads.append(part * gain[:, k * C1 : (k + 1) * C1])
    first = sum(jnp.sum(p, axis=-1, keepdims=True) for p in grads) * (1.0 / 768)
    second = sum(jnp.sum(p * n, axis=-1, keepdims=True) for p, n in zip(grads, normed))
    second = second * (1.0 / 768)
    back = [(scale * (p - first - n * second)).astype(BF16) for p, n in zip(grads, normed)]
    placed = nn(place_ref[...], jnp.concatenate(back, axis=0)).astype(BF16)
    gy_ref[...] = placed[:432]
    glast_ref[...] = placed[432:576]
    gstrip_ref[...] = placed[576:]


def merge_back_call(after, grads, f, place, gain, weight):
    shape = jax.ShapeDtypeStruct
    return pl.pallas_call(
        merge_back_kernel,
        out_shape=(shape((432, C1), BF16), shape((144, C1), BF16), shape((72, C1), BF16)),
        in_specs=[pl.BlockSpec(memory_space=pl.ANY)] + vmem(8),
        compiler_params=pltpu.CompilerParams(vmem_limit_bytes=8 << 20),
        cost_estimate=cost(1),
        name="merge_backward",
    )(after, *grads, f, place, gain, weight)


def fine_back_kernel(windows, *refs):
    edge = windows[-1] == 3
    count = len(windows)
    refs = list(refs)
    gy_ref = refs.pop(0)
    if edge:
        strip_ref, place_ref, table_ref, body_ref = refs[:4]
        refs = refs[4:]
    qkv_ref, a_ref, att_ref, slope_ref, red_ref = refs[:5]
    wa_ref, wp_ref, g1_ref, we_ref, wr_ref, g2_ref, ef_ref = refs[5:12]
    refs = refs[12:]
    if edge:
        own_ref, last_ref, keep_ref, send_ref = refs[:4]
        refs = refs[4:]
    else:
        gx_ref, dt_ref = refs[:2]
        refs = refs[2:]
    low_ref, high_ref, grid_ref, q_ref, k_ref, v_ref = refs[:6]
    gm_ref, go_ref, dq_ref, dk_ref, dv_ref, ds_ref = refs[6:12]
    for part, wide_ref in enumerate((q_ref, k_ref, v_ref)):
        wide_ref[...] = qkv_ref[part].astype(F32)
    ds_ref[...] = jnp.zeros_like(ds_ref)
    for c in range(count):
        cells = slice(c * 144, (c + 1) * 144)
        seed = gy_ref[cells, :].astype(F32)
        if edge:
            seed = seed + nn(place_ref[...], strip_ref[...])
        normed, scale = norm_parts(red_ref[cells, :])
        grad_red = norm_back(seed * g2_ref[...][None, :], normed, scale).astype(BF16)
        grad_act = nn(grad_red, wr_ref[...]).astype(BF16).astype(F32)
        grad_exp = (grad_act * slope_ref[cells, :].astype(F32)).astype(BF16)
        grad_middle = seed + nt(grad_exp, we_ref[...]).astype(BF16).astype(F32)
        grad_middle = grad_middle.astype(BF16).astype(F32)
        gm_ref[cells, :] = grad_middle
        normed, scale = norm_parts(att_ref[cells, :])
        grad_att = norm_back(grad_middle * g1_ref[...][None, :], normed, scale).astype(BF16)
        go_ref[cells, :] = nt(grad_att, wp_ref[...]).astype(BF16).astype(F32)
    mask = head_mask(HALF, H1, C1)
    for z in range(2):
        for n in range(count):
            block = z * count + n
            cells = slice(block * 72, block * 72 + 72)
            os = heads_stack(go_ref[cells, :], H1, mask)
            qs = heads_stack(q_ref[cells, :], H1, mask)
            weights = a_ref[block * 432 : (block + 1) * 432, :]
            grad_a = nt(os, v_ref[cells, :].astype(BF16))
            wide = weights.astype(F32)
            grad_s = wide * (grad_a - jnp.sum(wide * grad_a, axis=-1, keepdims=True))
            for h in range(H1):
                place = ((n * 6 + h) * 2 + 1 - z) * 72
                ds_ref[place : place + 72, 0:72] = grad_s[h * 72 : (h + 1) * 72]
            short = grad_s.astype(BF16)
            dv_ref[cells, :] = tn(weights, os)
            dq_ref[cells, :] = heads_fold(nn(short, k_ref[cells, :].astype(BF16)), H1, mask) * SCALE
            dk_ref[cells, :] = tn(short, qs) * SCALE
    table = None
    for p in range(WLON):
        piece = ds_ref[pl.ds(p, 72 * count, stride=12), :].astype(BF16)
        part = nt(piece, ef_ref[p])
        table = part if table is None else table + part
    if edge:
        first = parity() == 0
        whole = jnp.concatenate([table_ref[...], table], axis=0)
        for half_ref, taken in ((keep_ref, first), (send_ref, jnp.logical_not(first))):
            half = jnp.where(taken, whole[:144], whole[144:]).astype(BF16)
            half_ref[:144, :] = half[:, :128]
            half_ref[144:, :] = half[:, 128:]
    else:
        dt_ref[...] = table
    total = gm_ref[...]
    total = total + nt(dq_ref[...].astype(BF16), wa_ref[:, :C1])
    total = total + nt(dk_ref[...].astype(BF16), wa_ref[:, C1 : 2 * C1])
    total = total + nt(dv_ref[...].astype(BF16), wa_ref[:, 2 * C1 :])
    low_ref[...] = total[:, :128]
    high_ref[:, 0:64] = total[:, 128:]
    rows = 6 * count
    for col in range(WLON):
        lanes = slice(col * C1, (col + 1) * C1)
        low = low_ref[pl.ds(col, 2 * rows, stride=WLON), :]
        high = high_ref[pl.ds(col, 2 * rows, stride=WLON), :]
        grid_ref[:, lanes] = jnp.concatenate([low, high[:, :64]], axis=1)
    for z in range(2):
        band = grid_ref[z * rows : (z + 1) * rows, :]
        if edge:
            own_ref[z] = jnp.concatenate([body_ref[z].astype(F32), band[:3]], axis=0).astype(BF16)
            last_ref[z] = band[3:].astype(BF16)
        else:
            gx_ref[z] = band.astype(BF16)


def fine_back_call(windows, grads, saved, weights, ef):
    wa, wp, g1, we, wr, g2 = weights
    shape = jax.ShapeDtypeStruct
    count = len(windows)
    total = 144 * count
    width = WLON * C1
    if windows[-1] == 3:
        outs = (shape((2, 21, width), BF16), shape((2, 3, width), BF16))
        outs = outs + (shape((288, 128), BF16),) * 2
    else:
        outs = (shape((2, 6 * count, width), BF16), shape((72 * count, 256), F32))
    return pl.pallas_call(
        functools.partial(fine_back_kernel, windows),
        out_shape=outs,
        in_specs=vmem(len(grads) + 12),
        scratch_shapes=[pltpu.VMEM((total, 128), F32)] * 2
        + [pltpu.VMEM((12 * count, width), F32)]
        + [pltpu.VMEM((total, C1), F32)] * 8
        + [pltpu.VMEM((864 * count, 128), F32)],
        compiler_params=pltpu.CompilerParams(vmem_limit_bytes=16 << 20),
        cost_estimate=cost(2 * count),
        name=f"fine_backward_{count}",
    )(*grads, *saved, wa, wp, g1, we, wr, g2, ef)


def partial_kernel(keep_ref, got_ref, coarse_ref, out_ref):
    out_ref[:288, :] = (keep_ref[...].astype(F32) + got_ref[...].astype(F32)).astype(BF16)
    out_ref[288:720, :] = coarse_ref[...]
    out_ref[720:, :] = jnp.zeros((48, 128), BF16)


def partial_call(keep, got, coarse):
    return pl.pallas_call(
        partial_kernel,
        out_shape=jax.ShapeDtypeStruct((768, 128), BF16),
        in_specs=vmem(3),
        compiler_params=pltpu.CompilerParams(vmem_limit_bytes=4 << 20),
        cost_estimate=cost(0.5),
        name="partial_sums",
    )(keep, got, coarse)


def sum_kernel(parts_ref, out_ref):
    total = jnp.sum(parts_ref[...].astype(F32), axis=0, keepdims=True).astype(BF16)
    out_ref[...] = jnp.broadcast_to(total, out_ref.shape)


def sum_call(parts):
    return pl.pallas_call(
        sum_kernel,
        out_shape=jax.ShapeDtypeStruct(parts.shape, BF16),
        in_specs=vmem(1),
        compiler_params=pltpu.CompilerParams(vmem_limit_bytes=4 << 20),
        cost_estimate=cost(0.7),
        name="chip_sums",
    )(parts)


def table_kernel(
    mine_ref, got_ref, okeep_ref, ogot_ref, out_ref, fine_ref, coarse_ref, cols_f, cols_c
):
    par = parity()
    out_ref[...] = (okeep_ref[...].astype(F32) + ogot_ref[...].astype(F32)).astype(BF16)
    level = lax.broadcasted_iota(jnp.int32, (144, 128), 0) % 12 < 6
    for s in range(2):
        source = jnp.where(par == s, mine_ref[...].astype(F32), got_ref[...].astype(F32))
        for jm in range(6):
            tile = source[jm // 5 * 144 : jm // 5 * 144 + 144]
            if jm % 5:
                tile = pltpu.roll(tile, 128 - jm % 5 * 24, 1)
            base = s * 1728
            cols_f[pl.ds(base + jm, 144, stride=12), :] = jnp.where(level, tile, 0.0)
            cols_f[pl.ds(base + 6 + jm, 144, stride=12), :] = jnp.where(level, 0.0, tile)
        for b in range(12):
            tile = source[288 + b // 5 * 144 : 288 + b // 5 * 144 + 144]
            if b % 5:
                tile = pltpu.roll(tile, 128 - b % 5 * 24, 1)
            cols_c[pl.ds(s * 1728 + b, 144, stride=12), :] = tile
    for th in range(24):
        rows = slice(th * 144, (th + 1) * 144)
        fine_ref[th % 6, :, th // 6, :] = jnp.swapaxes(cols_f[rows, 0:24], 0, 1)[:23]
        coarse_ref[th % 12, :, th // 12, :] = jnp.swapaxes(cols_c[rows, 0:24], 0, 1)[:23]


def table_call(mine, got, okeep, ogot):
    shape = jax.ShapeDtypeStruct
    return pl.pallas_call(
        table_kernel,
        out_shape=(
            shape((12, 2, 6 * C2), BF16),
            shape((6, 23, 4, 144), F32),
            shape((12, 23, 2, 144), F32),
        ),
        in_specs=vmem(4),
        scratch_shapes=[pltpu.VMEM((3456, 128), F32)] * 2,
        compiler_params=pltpu.CompilerParams(vmem_limit_bytes=10 << 20),
        cost_estimate=cost(2),
        name="results",
    )(mine, got, okeep, ogot)


def shifted(value, axis, steps):
    count = lax.axis_size(axis)
    return lax.ppermute(value, axis, [(s, (s + steps) % count) for s in range(count)])


def diagonal(value, steps):
    lon, lat = lax.axis_size("lon"), lax.axis_size("lat")
    pairs = [
        (a * lat + b, (a + steps) % lon * lat + (b + steps) % lat)
        for a in range(lon)
        for b in range(lat)
    ]
    return lax.ppermute(value, ("lon", "lat"), pairs)


def swapped(value):
    return lax.ppermute(value, "lon", [(s, s ^ 1) for s in range(lax.axis_size("lon"))])


def shards(
    tokens, fine_attend, fine_project, fine_gain_one, fine_expand, fine_reduce, fine_gain_two,
    fine_bias, merge_gain, merge_weight, coarse_attend, coarse_project, coarse_gain_one,
    coarse_expand, coarse_reduce, coarse_gain_two, coarse_bias, cotangent,
):
    fine_weights = (
        fine_attend, fine_project, fine_gain_one, fine_expand, fine_reduce.T, fine_gain_two,
    )
    coarse_weights = (
        coarse_attend, coarse_project, coarse_gain_one, coarse_expand, coarse_reduce,
        coarse_gain_two,
    )
    ef = spread_onehot(6, 128)
    ec = spread_onehot(12, 256)
    pick = merge_onehot()
    seed = jnp.transpose(cotangent, (1, 0, 2))
    seeds = (seed, swapped(seed))
    cols, top, corner, table = split_call(tokens, jnp.transpose(fine_bias, (1, 2, 0, 3)))
    cols = shifted(cols, "lon", -1)
    top = shifted(top, "lat", -1)
    corner = diagonal(corner, -1)
    bias_fine = fine_bias_call(table)
    bias_coarse = coarse_bias_call(jnp.transpose(coarse_bias, (1, 2, 0, 3)), ec)

    most, final = (0, 1, 2), (3,)
    y_last, strip, *saved_last = fine_call(
        final, (tokens, cols, top, corner), fine_weights, bias_fine
    )
    strip = shifted(strip, "lat", 1)
    y_most, *saved_most = fine_call(most, (tokens, cols), fine_weights, bias_fine)
    both, right, quads = merge_call(y_most, y_last, strip, pick, merge_gain, merge_weight)
    cells = (both, swapped(both), shifted(right, "lon", 1), shifted(right, "lon", 2))
    grad_both, grad_pboth, grad_even, grad_odd, out, grad_scores = coarse_call(
        cells, seeds, coarse_weights, bias_coarse
    )
    grads = (
        grad_both,
        swapped(grad_pboth),
        shifted(grad_even, "lon", -1),
        shifted(grad_odd, "lon", -2),
    )
    out_keep, out_send, table_coarse = coarse_rest_call(out, grad_scores, ec)
    grad_most, grad_last, grad_strip = merge_back_call(
        table_coarse, grads, quads, np.ascontiguousarray(pick.T), merge_gain, merge_weight
    )
    grad_strip = shifted(grad_strip, "lat", -1)
    body, table_most = fine_back_call(most, (grad_most,), saved_most, fine_weights, ef)
    grads = (grad_last, grad_strip, strip_onehot(), table_most, body)
    own, edge, table_keep, table_send = fine_back_call(
        final, grads, saved_last, fine_weights, ef
    )
    partial = partial_call(table_keep, swapped(table_send), table_coarse).reshape(16, 48, 128)
    chips = [[2 * k + c for k in range(16)] for c in range(2)]
    partial = lax.all_to_all(partial, "lon", 0, 0, tiled=True, axis_index_groups=chips)
    sums = lax.all_to_all(sum_call(partial), "lon", 0, 0, tiled=True, axis_index_groups=chips)
    sums = sums.reshape(768, 128)
    coarse_out, grad_fine, grad_coarse = table_call(
        sums, swapped(sums), out_keep, swapped(out_send)
    )
    band = jnp.concatenate([shifted(edge, "lat", 1), own], axis=1)
    half = band.shape[2] // 2
    grad_tokens = jnp.concatenate(
        [shifted(band[:, :, half:], "lon", 1), band[:, :, :half]], axis=2
    )
    return (
        jnp.transpose(coarse_out, (1, 0, 2)),
        grad_tokens,
        jnp.transpose(grad_fine, (2, 0, 1, 3)),
        jnp.transpose(grad_coarse, (2, 0, 1, 3)),
    )


def solution(mesh):
    rows = P(None, "lat", "lon")
    table = P("lat", None, None, None)
    in_specs = (rows,) + (P(),) * 6 + (table,) + (P(),) * 8 + (table, rows)
    return jax.shard_map(
        shards, mesh=mesh, in_specs=in_specs, out_specs=(rows, rows, table, table), check_vma=False
    )
```

```python
import functools
import math

import jax
import jax.numpy as jnp
import numpy as np
from jax import lax
from jax.experimental import pallas as pl
from jax.experimental.pallas import tpu as pltpu
from jax.sharding import PartitionSpec as P

C1 = 192
C2 = 384
HD = 32
H1 = 6
H2 = 12
WLON = 12
HALF = 72
EPSILON = 1e-05
MASKED = -1000000000.0
SCALE = 1.0 / math.sqrt(HD)
F32 = jnp.float32
BF16 = jnp.bfloat16


def pair_lane(pair):
    return pair // 5 * 128 + pair % 5 * 24


def spread_onehot(pairs, lanes):
    onehot = np.zeros((WLON, (pairs + 4) // 5 * 128, lanes), np.float32)
    for p in range(WLON):
        for b in range(pairs):
            for q in range(WLON):
                onehot[p, pair_lane(b) + p - q + WLON - 1, b * WLON + q] = 1.0
    return onehot.astype(jnp.bfloat16)


def merge_onehot():
    onehot = np.zeros((4, 2, 2, 48, 648), np.float32)
    for rr in range(2):
        for cc in range(2):
            for bh in range(2):
                for lam in range(2):
                    for z in range(2):
                        for a in range(6):
                            for b in range(3):
                                row = 2 * (lam * 6 + a) + rr
                                col = 2 * (bh * 3 + b) + cc
                                if row < 3:
                                    cell = 576 + z * 36 + row * 12 + col
                                elif row < 21:
                                    cell = z * 216 + (row - 3) * 12 + col
                                else:
                                    cell = 432 + z * 72 + (row - 21) * 12 + col
                                onehot[rr * 2 + cc, bh, lam, z * 18 + a * 3 + b, cell] = 1.0
    return onehot.reshape(768, 648).astype(jnp.bfloat16)


def strip_onehot():
    onehot = np.zeros((144, 72), np.float32)
    for z in range(2):
        for k in range(36):
            onehot[z * 72 + 36 + k, z * 36 + k] = 1.0
    return onehot.astype(jnp.bfloat16)


def nn(left, right):
    return lax.dot_general(left, right, (((1,), (0,)), ((), ())), preferred_element_type=F32)


def nt(left, right):
    return lax.dot_general(left, right, (((1,), (1,)), ((), ())), preferred_element_type=F32)


def tn(left, right):
    return lax.dot_general(left, right, (((0,), (0,)), ((), ())), preferred_element_type=F32)


def norm_parts(values):
    average = jnp.mean(values, axis=-1, keepdims=True)
    centred = values - average
    scale = lax.rsqrt(jnp.mean(centred * centred, axis=-1, keepdims=True) + EPSILON)
    return centred * scale, scale


def norm_back(grad, normed, scale):
    first = jnp.mean(grad, axis=-1, keepdims=True)
    second = jnp.mean(grad * normed, axis=-1, keepdims=True)
    return scale * (grad - first - normed * second)


def split3(values):
    high = values.astype(BF16)
    rest = values - high.astype(F32)
    mid = rest.astype(BF16)
    low = (rest - mid.astype(F32)).astype(BF16)
    return high, mid, low


def head_mask(rows, heads, width):
    row = lax.broadcasted_iota(jnp.int32, (heads * rows, width), 0) // rows
    lane = lax.broadcasted_iota(jnp.int32, (heads * rows, width), 1) // HD
    return (row == lane).astype(F32)


def heads_stack(values, heads, mask):
    return (jnp.concatenate([values] * heads, axis=0) * mask).astype(BF16)


def heads_fold(stacked, heads, mask):
    rows = stacked.shape[0] // heads
    kept = stacked * mask
    total = kept[:rows]
    for h in range(1, heads):
        total = total + kept[h * rows : (h + 1) * rows]
    return total


def gelu_parts(values):
    phi = 0.5 * (1.0 + lax.erf(values * (1.0 / math.sqrt(2.0))))
    density = jnp.exp(-0.5 * values * values) * (1.0 / math.sqrt(2.0 * math.pi))
    return values * phi, phi + values * density


def softmax(scores):
    top = jnp.max(scores, axis=-1, keepdims=True)
    powers = jnp.exp(scores - top)
    return powers / jnp.sum(powers, axis=-1, keepdims=True)


def vmem(count):
    return [pl.BlockSpec(memory_space=pltpu.VMEM)] * count


def cost(microseconds):
    return pl.CostEstimate(
        flops=int(microseconds * 1e9), bytes_accessed=int(microseconds * 1e6), transcendentals=0
    )


def parity():
    return lax.rem(lax.axis_index("lon"), 2)


def fine_bias_kernel(table_ref, out_ref, cols_ref):
    key = lax.broadcasted_iota(jnp.int32, (256, 256), 0)
    lane = lax.broadcasted_iota(jnp.int32, (256, 256), 1) % 128
    second = lax.broadcasted_iota(jnp.int32, (256, 256), 1) // 128
    place = key % 128
    pair = key // 128 * 5 + place // 24
    meets = jnp.logical_and(pair == lane // 12, place < 120)
    column = jnp.where(meets, place % 24 + lane % 12 - (WLON - 1) - second, -2)
    cols_ref[...] = jnp.zeros_like(cols_ref)
    for th in range(24):
        cols_ref[th * 144 : (th + 1) * 144, 0:23] = jnp.swapaxes(
            table_ref[th % 6, :, th // 6, :], 0, 1
        )
    low_level = lax.broadcasted_iota(jnp.int32, (288, 128), 0) % 12 < 6
    tiles = []
    for t in range(2):
        tile = None
        for jm in range(t * 5, min(t * 5 + 5, 6)):
            piece = jnp.where(
                low_level,
                cols_ref[pl.ds(jm, 288, stride=12), :],
                cols_ref[pl.ds(6 + jm, 288, stride=12), :],
            )
            if jm % 5:
                piece = pltpu.roll(piece, jm % 5 * 24, 1)
            tile = piece if tile is None else tile + piece
        tiles.append(tile)
    parts = jnp.concatenate(split3(jnp.concatenate(tiles, axis=1)), axis=0)
    for p in range(0, WLON, 2):
        spread = nn(parts, (column == p).astype(F32).astype(BF16))
        total = spread[:288] + spread[288:576] + spread[576:]
        out_ref[pl.ds(p, 288, stride=12), :] = total[:, :128]
        out_ref[pl.ds(p + 1, 288, stride=12), :] = total[:, 128:]


def fine_bias_call(table):
    return pl.pallas_call(
        fine_bias_kernel,
        out_shape=jax.ShapeDtypeStruct((3456, 128), F32),
        in_specs=vmem(1),
        scratch_shapes=[pltpu.VMEM((3456, 128), F32)],
        compiler_params=pltpu.CompilerParams(vmem_limit_bytes=10 << 20),
        cost_estimate=cost(2),
        name="fine_bias_spread",
    )(table)


def coarse_bias_kernel(table_ref, onehot_ref, tail_ref, out_ref, cols_ref):
    cols_ref[...] = jnp.zeros_like(cols_ref)
    par = parity()
    for h in range(12):
        cols_ref[h * 144 : (h + 1) * 144, 0:23] = jnp.swapaxes(
            jnp.where(par == 0, table_ref[h, :, 0, :], table_ref[h, :, 1, :]), 0, 1
        )
    tiles = []
    for t in range(3):
        tile = None
        for b in range(t * 5, min(t * 5 + 5, 12)):
            piece = cols_ref[pl.ds(b, 144, stride=12), :]
            if b % 5:
                piece = pltpu.roll(piece, b % 5 * 24, 1)
            tile = piece if tile is None else tile + piece
        tiles.append(tile)
    parts = jnp.concatenate(split3(jnp.concatenate(tiles, axis=1)), axis=0)
    for p in range(0, WLON, 2):
        pair = jnp.concatenate([onehot_ref[p, :, :128], onehot_ref[p + 1, :, :128]], axis=1)
        spread = nn(parts, pair)
        total = spread[:144] + spread[144:288] + spread[288:]
        out_ref[0, pl.ds(p, 144, stride=12), :] = total[:, :128]
        out_ref[0, pl.ds(p + 1, 144, stride=12), :] = total[:, 128:]
    spread = nn(parts, tail_ref[...])
    total = spread[:144] + spread[144:288] + spread[288:]
    for p in range(WLON):
        tile = total[:, p // 8 * 128 : p // 8 * 128 + 128]
        if p % 8:
            tile = pltpu.roll(tile, 128 - p % 8 * 16, 1)
        out_ref[1, pl.ds(p, 144, stride=12), :] = tile


def coarse_bias_call(table, onehot):
    tail = np.zeros((onehot.shape[1], 256), onehot.dtype)
    for p in range(WLON):
        tail[:, p * 16 : p * 16 + 16] = onehot[p, :, 128:144]
    return pl.pallas_call(
        coarse_bias_kernel,
        out_shape=jax.ShapeDtypeStruct((2, 1728, 128), F32),
        in_specs=vmem(3),
        scratch_shapes=[pltpu.VMEM((1728, 128), F32)],
        compiler_params=pltpu.CompilerParams(vmem_limit_bytes=10 << 20),
        cost_estimate=cost(2),
        name="coarse_bias_spread",
    )(table, onehot, tail)


def split_kernel(tok_ref, left_ref, top_ref, corner_ref):
    half = left_ref.shape[2]
    left_ref[...] = tok_ref[:, :, :half]
    for z in range(2):
        rows = tok_ref[z].astype(F32)[:3]
        top_ref[z] = rows[:, half:].astype(BF16)
        corner_ref[z] = rows[:, :half].astype(BF16)


def split_call(tokens):
    levels, rows, width = tokens.shape
    shape = jax.ShapeDtypeStruct
    return pl.pallas_call(
        split_kernel,
        out_shape=(
            shape((levels, rows, width // 2), BF16),
            shape((levels, 3, width // 2), BF16),
            shape((levels, 3, width // 2), BF16),
        ),
        in_specs=vmem(1),
        compiler_params=pltpu.CompilerParams(vmem_limit_bytes=4 << 20),
        cost_estimate=cost(8),
        name="left_half",
    )(tokens)


def fine_kernel(windows, *refs):
    edge = windows[-1] == 3
    refs = list(refs)
    tok_ref, col_ref = refs[:2]
    top_ref, corner_ref = refs[2:4] if edge else (None, None)
    refs = refs[4:] if edge else refs[2:]
    wa_ref, wp_ref, g1_ref, we_ref, wr_ref, g2_ref, bias_ref, y_ref = refs[:8]
    strip_ref = refs[8] if edge else None
    refs = refs[9:] if edge else refs[8:]
    qkv_ref, a_ref, att_ref, slope_ref, red_ref = refs[:5]
    q_ref, k_ref, v_ref, o_ref, grid_ref, low_ref, high_ref, x_ref, edge_ref = refs[5:]
    rows = 6 * len(windows)
    own = rows - 3 if edge else rows
    start = 3 + 6 * windows[0]
    half = grid_ref.shape[1] // 2
    for z in range(2):
        base = z * rows
        grid_ref[base : base + own, :half] = tok_ref[z].astype(F32)[start : start + own, half:]
        grid_ref[base : base + own, half:] = col_ref[z].astype(F32)[start : start + own]
        if edge:
            grid_ref[base + own : base + rows, :half] = top_ref[z].astype(F32)
            grid_ref[base + own : base + rows, half:] = corner_ref[z].astype(F32)
    for col in range(WLON):
        piece = grid_ref[:, col * C1 : (col + 1) * C1]
        places = pl.ds(col, 2 * rows, stride=WLON)
        low_ref[places, :] = piece[:, :128]
        high_ref[places, :] = jnp.concatenate([piece[:, 128:]] * 2, axis=1)
    x_ref[...] = jnp.concatenate([low_ref[...], high_ref[:, :64]], axis=1)
    x = x_ref[...].astype(BF16)
    for part, wide_ref in enumerate((q_ref, k_ref, v_ref)):
        short = nn(x, wa_ref[:, part * C1 : (part + 1) * C1]).astype(BF16)
        qkv_ref[part] = short
        wide_ref[...] = short.astype(F32)
    mask = head_mask(HALF, H1, C1)
    last = lax.axis_index("lat") == lax.axis_size("lat") - 1
    for z in range(2):
        for n, w in enumerate(windows):
            block = z * len(windows) + n
            cells = slice(block * 72, block * 72 + 72)
            qs = heads_stack(q_ref[cells, :], H1, mask)
            places = [((w * 6 + h) * 2 + 1 - z) * 72 for h in range(H1)]
            bias = jnp.concatenate([bias_ref[s : s + 72, :] for s in places], axis=0)[:, :72]
            scores = nt(qs, k_ref[cells, :].astype(BF16)) * SCALE + bias
            if w == 3:
                row = lax.broadcasted_iota(jnp.int32, scores.shape, 0) % 72 < 36
                col = lax.broadcasted_iota(jnp.int32, scores.shape, 1) < 36
                scores = jnp.where(jnp.logical_and(row != col, last), MASKED, scores)
            weights = softmax(scores).astype(BF16)
            a_ref[block * 432 : (block + 1) * 432, :] = weights
            o_ref[cells, :] = heads_fold(nn(weights, v_ref[cells, :].astype(BF16)), H1, mask)
    for c in range(len(windows)):
        cells = slice(c * 144, (c + 1) * 144)
        att = nn(o_ref[cells, :].astype(BF16), wp_ref[...])
        att_ref[cells, :] = att
        normed, _ = norm_parts(att)
        middle = (x_ref[cells, :] + g1_ref[...][None, :] * normed).astype(BF16)
        act, slope = gelu_parts(nn(middle, we_ref[...]))
        slope_ref[cells, :] = slope.astype(BF16)
        red = nt(act.astype(BF16), wr_ref[...])
        red_ref[cells, :] = red
        normed, _ = norm_parts(red)
        out = middle.astype(F32) + g2_ref[...][None, :] * normed
        y_ref[cells, :] = out.astype(BF16)
        if edge:
            edge_ref[0:36, :] = out[36:72]
            edge_ref[36:72, :] = out[108:]
    if edge:
        strip_ref[...] = edge_ref[...].astype(BF16)


def fine_call(windows, cells, weights, bias):
    wa, wp, g1, we, wr, g2 = weights
    shape = jax.ShapeDtypeStruct
    count = len(windows)
    edge = windows[-1] == 3
    total = 144 * count
    return pl.pallas_call(
        functools.partial(fine_kernel, windows),
        out_shape=(shape((total, C1), BF16),)
        + ((shape((72, C1), BF16),) if edge else ())
        + (
            shape((3, total, C1), BF16),
            shape((count * 864, 72), BF16),
            shape((total, C1), F32),
            shape((total, 4 * C1), BF16),
            shape((total, C1), F32),
        ),
        in_specs=vmem(len(cells) + 7),
        scratch_shapes=[pltpu.VMEM((total, C1), F32)] * 4
        + [
            pltpu.VMEM((12 * count, WLON * C1), F32),
            pltpu.VMEM((total, 128), F32),
            pltpu.VMEM((total, 128), F32),
            pltpu.VMEM((total, C1), F32),
            pltpu.VMEM((72, C1), F32),
        ],
        compiler_params=pltpu.CompilerParams(vmem_limit_bytes=14 << 20),
        cost_estimate=cost(count + 0.5),
        name=f"fine_forward_{count}",
    )(*cells, wa, wp, g1, we, wr, g2, bias)


def merge_kernel(y_ref, last_ref, strip_ref, pick_ref, gain_ref, w_ref, both_ref, right_ref, f_ref):
    gain = gain_ref[...][None, :]
    cells = jnp.concatenate([y_ref[...], last_ref[...], strip_ref[...]], axis=0)
    f = nn(pick_ref[...], cells)
    f_ref[...] = f.astype(BF16)
    total = sum(jnp.sum(f[k * 192 : (k + 1) * 192], axis=-1, keepdims=True) for k in range(4))
    average = total * (1.0 / 768)
    centred = [f[k * 192 : (k + 1) * 192] - average for k in range(4)]
    square = sum(jnp.sum(c * c, axis=-1, keepdims=True) for c in centred)
    scale = lax.rsqrt(square * (1.0 / 768) + EPSILON)
    result = None
    for k in range(4):
        normed = (gain[:, k * C1 : (k + 1) * C1] * (centred[k] * scale)).astype(BF16)
        part = nn(normed, w_ref[k * 192 : (k + 1) * 192, :])
        result = part if result is None else result + part
    both_ref[...] = result.astype(BF16)
    right_ref[...] = result[96:].astype(BF16)


def merge_call(y, last, strip, pick, gain, weight):
    shape = jax.ShapeDtypeStruct
    return pl.pallas_call(
        merge_kernel,
        out_shape=(shape((192, C2), BF16), shape((96, C2), BF16), shape((768, C1), BF16)),
        in_specs=vmem(6),
        compiler_params=pltpu.CompilerParams(vmem_limit_bytes=8 << 20),
        cost_estimate=cost(1.5),
        name="merge_forward",
    )(y, last, strip, pick, gain, weight)


def window_places(par):
    row = lax.broadcasted_iota(jnp.int32, (144, 576), 0)
    z, a, c = row // 72, row // 12 % 6, row % 12
    group = c // 3
    even = jnp.where(group == 0, 4, jnp.where(group == 1, 0, jnp.where(group == 2, 1, 2)))
    odd = jnp.where(group == 0, 5, jnp.where(group == 1, 2, jnp.where(group == 2, 3, 0)))
    source = jnp.where(par == 0, even, odd)
    place = source * 96 + par * 48 + z * 18 + a * 3 + c % 3
    return (place == lax.broadcasted_iota(jnp.int32, (144, 576), 1)).astype(F32).astype(BF16)


def half_places(par):
    row = lax.broadcasted_iota(jnp.int32, (144, 288), 0)
    z, a, c = row // 72, row // 12 % 6, row % 12
    side = jnp.where(c // 6 == par, 0, 1)
    place = (side * 6 + c % 6) * 24 + z * 12 + par * 6 + a
    return (place == lax.broadcasted_iota(jnp.int32, (144, 288), 1)).astype(F32).astype(BF16)


def coarse_kernel(
    both_ref, pboth_ref, even_ref, odd_ref, seed_ref, pseed_ref,
    wa_ref, wp_ref, g1_ref, we_ref, wr_ref, g2_ref, bias_ref,
    gboth_ref, gpboth_ref, geven_ref, godd_ref, out_ref, ds_ref,
    a_ref, qs_ref, o_ref, slope_ref, band_ref, packed_ref,
):
    par = parity()
    pick = window_places(par)
    half = half_places(par)
    cells = [both_ref[...], pboth_ref[...], even_ref[...], odd_ref[...]]
    x = nn(pick, jnp.concatenate(cells, axis=0)).astype(BF16)
    for side, source_ref in enumerate((seed_ref, pseed_ref)):
        wide = source_ref[...].astype(F32)
        for z in range(2):
            band_ref[side, z * 12 : (z + 1) * 12, :] = wide[:, z, :]
    bands = [
        band_ref[side, :, col * C2 : (col + 1) * C2] for side in range(2) for col in range(6)
    ]
    seed = nn(half, jnp.concatenate(bands, axis=0).astype(BF16))
    ds_ref[1] = jnp.zeros_like(ds_ref[1])
    packed = nn(x, wa_ref[...]).astype(BF16)
    mask = head_mask(144, 4, 128)
    for g in range(3):
        lanes = slice(g * 128, (g + 1) * 128)
        rows = slice(g * 576, (g + 1) * 576)
        qs = heads_stack(packed[:, lanes].astype(F32), 4, mask)
        qs_ref[rows, :] = qs
        key = packed[:, C2 + g * 128 : C2 + (g + 1) * 128]
        value = packed[:, 2 * C2 + g * 128 : 2 * C2 + (g + 1) * 128]
        bias = jnp.concatenate([bias_ref[0, rows, :], bias_ref[1, rows, :]], axis=1)[:, :144]
        weights = softmax(nt(qs, key) * SCALE + bias).astype(BF16)
        a_ref[rows, :] = weights
        o_ref[:, lanes] = heads_fold(nn(weights, value), 4, mask)
    att = nn(o_ref[...].astype(BF16), wp_ref[...])
    normed1, scale1 = norm_parts(att)
    middle = (x.astype(F32) + g1_ref[...][None, :] * normed1).astype(BF16)
    act, slope = gelu_parts(nn(middle, we_ref[...]))
    slope_ref[...] = slope
    red = nn(act.astype(BF16), wr_ref[...])
    normed2, scale2 = norm_parts(red)
    out_ref[...] = (middle.astype(F32) + g2_ref[...][None, :] * normed2).astype(BF16)
    grad_red = norm_back(seed * g2_ref[...][None, :], normed2, scale2).astype(BF16)
    grad_act = nt(grad_red, wr_ref[...]).astype(BF16).astype(F32)
    grad_exp = (grad_act * slope_ref[...]).astype(BF16)
    grad_middle = (seed + nt(grad_exp, we_ref[...]).astype(BF16).astype(F32)).astype(BF16)
    grad_middle = grad_middle.astype(F32)
    grad_att = norm_back(grad_middle * g1_ref[...][None, :], normed1, scale1).astype(BF16)
    grad_o = nt(grad_att, wp_ref[...]).astype(BF16)
    for g in range(3):
        lanes = slice(g * 128, (g + 1) * 128)
        rows = slice(g * 576, (g + 1) * 576)
        os = heads_stack(grad_o[:, lanes].astype(F32), 4, mask)
        key = packed[:, C2 + g * 128 : C2 + (g + 1) * 128]
        value = packed[:, 2 * C2 + g * 128 : 2 * C2 + (g + 1) * 128]
        weights = a_ref[rows, :]
        grad_a = nt(os, value)
        wide = weights.astype(F32)
        grad_s = wide * (grad_a - jnp.sum(wide * grad_a, axis=-1, keepdims=True))
        ds_ref[0, rows, :] = grad_s[:, :128]
        ds_ref[1, rows, 0:16] = grad_s[:, 128:]
        short = grad_s.astype(BF16)
        grad_v = tn(weights, os).astype(BF16)
        grad_q = (heads_fold(nn(short, key), 4, mask) * SCALE).astype(BF16)
        grad_k = (tn(short, qs_ref[rows, :]) * SCALE).astype(BF16)
        for part, grad in enumerate((grad_q, grad_k, grad_v)):
            packed_ref[:, part * C2 + g * 128 : part * C2 + (g + 1) * 128] = grad
    grad_x = grad_middle + nt(packed_ref[...], wa_ref[...])
    parted = tn(pick, grad_x.astype(BF16)).astype(BF16)
    gboth_ref[...] = parted[:192]
    gpboth_ref[...] = parted[192:384]
    geven_ref[...] = parted[384:480]
    godd_ref[...] = parted[480:]


def coarse_rest_kernel(out_ref, ds_ref, ec_ref, okeep_ref, osend_ref, dt_ref, cells_ref):
    half = half_places(parity())
    out = out_ref[...]
    parted = tn(half, out)
    for side in range(2):
        for col in range(6):
            lanes = slice(col * C2, (col + 1) * C2)
            for z in range(2):
                place = (side * 6 + col) * 24 + z * 12
                cells_ref[side, :, z, lanes] = parted[place : place + 12]
    okeep_ref[...] = cells_ref[0].astype(BF16)
    osend_ref[...] = cells_ref[1].astype(BF16)
    table = None
    for p in range(WLON):
        places = pl.ds(p, 144, stride=12)
        piece = jnp.concatenate([ds_ref[0, places, :], ds_ref[1, places, :]], axis=1).astype(BF16)
        part = nt(piece, ec_ref[p])
        table = part if table is None else table + part
    for t in range(3):
        dt_ref[t * 144 : (t + 1) * 144, :] = table[:, t * 128 : (t + 1) * 128].astype(BF16)


def coarse_rest_call(out, ds, ec):
    shape = jax.ShapeDtypeStruct
    return pl.pallas_call(
        coarse_rest_kernel,
        out_shape=(
            shape((12, 2, 6 * C2), BF16),
            shape((12, 2, 6 * C2), BF16),
            shape((432, 128), BF16),
        ),
        in_specs=vmem(3),
        scratch_shapes=[pltpu.VMEM((2, 12, 2, 6 * C2), F32)],
        compiler_params=pltpu.CompilerParams(vmem_limit_bytes=10 << 20),
        cost_estimate=cost(1.5),
        name="coarse_rest",
    )(out, ds, ec)


def coarse_call(cells, seeds, weights, bias):
    wa, wp, g1, we, wr, g2 = weights
    shape = jax.ShapeDtypeStruct
    return pl.pallas_call(
        coarse_kernel,
        out_shape=(
            shape((192, C2), BF16),
            shape((192, C2), BF16),
            shape((96, C2), BF16),
            shape((96, C2), BF16),
            shape((144, C2), BF16),
            shape((2, 1728, 128), F32),
        ),
        in_specs=vmem(13),
        scratch_shapes=[
            pltpu.VMEM((1728, 144), BF16),
            pltpu.VMEM((1728, 128), BF16),
            pltpu.VMEM((144, C2), F32),
            pltpu.VMEM((144, 4 * C2), F32),
            pltpu.VMEM((2, 24, 6 * C2), F32),
            pltpu.VMEM((144, 3 * C2), BF16),
        ],
        compiler_params=pltpu.CompilerParams(vmem_limit_bytes=20 << 20),
        cost_estimate=cost(7),
        name="coarse_both",
    )(*cells, *seeds, wa, wp, g1, we, wr, g2, bias)


def merge_back_kernel(_, g_ref, pg_ref, even_ref, odd_ref, f_ref, place_ref, gain_ref, w_ref, gy_ref, glast_ref, gstrip_ref):
    f = f_ref[...].astype(F32)
    total = sum(jnp.sum(f[k * 192 : (k + 1) * 192], axis=-1, keepdims=True) for k in range(4))
    average = total * (1.0 / 768)
    centred = [f[k * 192 : (k + 1) * 192] - average for k in range(4)]
    square = sum(jnp.sum(c * c, axis=-1, keepdims=True) for c in centred)
    scale = lax.rsqrt(square * (1.0 / 768) + EPSILON)
    gain = gain_ref[...][None, :]
    both = g_ref[...].astype(F32) + pg_ref[...].astype(F32)
    right = both[96:] + even_ref[...].astype(F32) + odd_ref[...].astype(F32)
    g = jnp.concatenate([both[:96], right], axis=0).astype(BF16)
    normed = [c * scale for c in centred]
    grads = []
    for k in range(4):
        part = nt(g, w_ref[k * 192 : (k + 1) * 192, :]).astype(BF16).astype(F32)
        grads.append(part * gain[:, k * C1 : (k + 1) * C1])
    first = sum(jnp.sum(p, axis=-1, keepdims=True) for p in grads) * (1.0 / 768)
    second = sum(jnp.sum(p * n, axis=-1, keepdims=True) for p, n in zip(grads, normed))
    second = second * (1.0 / 768)
    back = [(scale * (p - first - n * second)).astype(BF16) for p, n in zip(grads, normed)]
    placed = nn(place_ref[...], jnp.concatenate(back, axis=0)).astype(BF16)
    gy_ref[...] = placed[:432]
    glast_ref[...] = placed[432:576]
    gstrip_ref[...] = placed[576:]


def merge_back_call(after, grads, f, place, gain, weight):
    shape = jax.ShapeDtypeStruct
    return pl.pallas_call(
        merge_back_kernel,
        out_shape=(shape((432, C1), BF16), shape((144, C1), BF16), shape((72, C1), BF16)),
        in_specs=[pl.BlockSpec(memory_space=pl.ANY)] + vmem(8),
        compiler_params=pltpu.CompilerParams(vmem_limit_bytes=8 << 20),
        cost_estimate=cost(1),
        name="merge_backward",
    )(after, *grads, f, place, gain, weight)


def fine_back_kernel(windows, *refs):
    edge = windows[-1] == 3
    count = len(windows)
    refs = list(refs)
    gy_ref = refs.pop(0)
    if edge:
        strip_ref, place_ref, table_ref, body_ref = refs[:4]
        refs = refs[4:]
    qkv_ref, a_ref, att_ref, slope_ref, red_ref = refs[:5]
    wa_ref, wp_ref, g1_ref, we_ref, wr_ref, g2_ref, ef_ref = refs[5:12]
    refs = refs[12:]
    if edge:
        own_ref, last_ref, keep_ref, send_ref = refs[:4]
        refs = refs[4:]
    else:
        gx_ref, dt_ref = refs[:2]
        refs = refs[2:]
    low_ref, high_ref, grid_ref, q_ref, k_ref, v_ref = refs[:6]
    gm_ref, go_ref, dq_ref, dk_ref, dv_ref, ds_ref = refs[6:12]
    for part, wide_ref in enumerate((q_ref, k_ref, v_ref)):
        wide_ref[...] = qkv_ref[part].astype(F32)
    ds_ref[...] = jnp.zeros_like(ds_ref)
    for c in range(count):
        cells = slice(c * 144, (c + 1) * 144)
        seed = gy_ref[cells, :].astype(F32)
        if edge:
            seed = seed + nn(place_ref[...], strip_ref[...])
        normed, scale = norm_parts(red_ref[cells, :])
        grad_red = norm_back(seed * g2_ref[...][None, :], normed, scale).astype(BF16)
        grad_act = nn(grad_red, wr_ref[...]).astype(BF16).astype(F32)
        grad_exp = (grad_act * slope_ref[cells, :].astype(F32)).astype(BF16)
        grad_middle = seed + nt(grad_exp, we_ref[...]).astype(BF16).astype(F32)
        grad_middle = grad_middle.astype(BF16).astype(F32)
        gm_ref[cells, :] = grad_middle
        normed, scale = norm_parts(att_ref[cells, :])
        grad_att = norm_back(grad_middle * g1_ref[...][None, :], normed, scale).astype(BF16)
        go_ref[cells, :] = nt(grad_att, wp_ref[...]).astype(BF16).astype(F32)
    mask = head_mask(HALF, H1, C1)
    for z in range(2):
        for n in range(count):
            block = z * count + n
            cells = slice(block * 72, block * 72 + 72)
            os = heads_stack(go_ref[cells, :], H1, mask)
            qs = heads_stack(q_ref[cells, :], H1, mask)
            weights = a_ref[block * 432 : (block + 1) * 432, :]
            grad_a = nt(os, v_ref[cells, :].astype(BF16))
            wide = weights.astype(F32)
            grad_s = wide * (grad_a - jnp.sum(wide * grad_a, axis=-1, keepdims=True))
            for h in range(H1):
                place = ((n * 6 + h) * 2 + 1 - z) * 72
                ds_ref[place : place + 72, 0:72] = grad_s[h * 72 : (h + 1) * 72]
            short = grad_s.astype(BF16)
            dv_ref[cells, :] = tn(weights, os)
            dq_ref[cells, :] = heads_fold(nn(short, k_ref[cells, :].astype(BF16)), H1, mask) * SCALE
            dk_ref[cells, :] = tn(short, qs) * SCALE
    table = None
    for p in range(WLON):
        piece = ds_ref[pl.ds(p, 72 * count, stride=12), :].astype(BF16)
        part = nt(piece, ef_ref[p])
        table = part if table is None else table + part
    if edge:
        first = parity() == 0
        whole = jnp.concatenate([table_ref[...], table], axis=0)
        for half_ref, taken in ((keep_ref, first), (send_ref, jnp.logical_not(first))):
            half = jnp.where(taken, whole[:144], whole[144:]).astype(BF16)
            half_ref[:144, :] = half[:, :128]
            half_ref[144:, :] = half[:, 128:]
    else:
        dt_ref[...] = table
    total = gm_ref[...]
    total = total + nt(dq_ref[...].astype(BF16), wa_ref[:, :C1])
    total = total + nt(dk_ref[...].astype(BF16), wa_ref[:, C1 : 2 * C1])
    total = total + nt(dv_ref[...].astype(BF16), wa_ref[:, 2 * C1 :])
    low_ref[...] = total[:, :128]
    high_ref[:, 0:64] = total[:, 128:]
    rows = 6 * count
    for col in range(WLON):
        lanes = slice(col * C1, (col + 1) * C1)
        low = low_ref[pl.ds(col, 2 * rows, stride=WLON), :]
        high = high_ref[pl.ds(col, 2 * rows, stride=WLON), :]
        grid_ref[:, lanes] = jnp.concatenate([low, high[:, :64]], axis=1)
    for z in range(2):
        band = grid_ref[z * rows : (z + 1) * rows, :]
        if edge:
            own_ref[z] = jnp.concatenate([body_ref[z].astype(F32), band[:3]], axis=0).astype(BF16)
            last_ref[z] = band[3:].astype(BF16)
        else:
            gx_ref[z] = band.astype(BF16)


def fine_back_call(windows, grads, saved, weights, ef):
    wa, wp, g1, we, wr, g2 = weights
    shape = jax.ShapeDtypeStruct
    count = len(windows)
    total = 144 * count
    width = WLON * C1
    if windows[-1] == 3:
        outs = (shape((2, 21, width), BF16), shape((2, 3, width), BF16))
        outs = outs + (shape((288, 128), BF16),) * 2
    else:
        outs = (shape((2, 6 * count, width), BF16), shape((72 * count, 256), F32))
    return pl.pallas_call(
        functools.partial(fine_back_kernel, windows),
        out_shape=outs,
        in_specs=vmem(len(grads) + 12),
        scratch_shapes=[pltpu.VMEM((total, 128), F32)] * 2
        + [pltpu.VMEM((12 * count, width), F32)]
        + [pltpu.VMEM((total, C1), F32)] * 8
        + [pltpu.VMEM((864 * count, 128), F32)],
        compiler_params=pltpu.CompilerParams(vmem_limit_bytes=16 << 20),
        cost_estimate=cost(2 * count),
        name=f"fine_backward_{count}",
    )(*grads, *saved, wa, wp, g1, we, wr, g2, ef)


def partial_kernel(keep_ref, got_ref, coarse_ref, out_ref):
    out_ref[:288, :] = (keep_ref[...].astype(F32) + got_ref[...].astype(F32)).astype(BF16)
    out_ref[288:720, :] = coarse_ref[...]
    out_ref[720:, :] = jnp.zeros((48, 128), BF16)


def partial_call(keep, got, coarse):
    return pl.pallas_call(
        partial_kernel,
        out_shape=jax.ShapeDtypeStruct((768, 128), BF16),
        in_specs=vmem(3),
        compiler_params=pltpu.CompilerParams(vmem_limit_bytes=4 << 20),
        cost_estimate=cost(0.5),
        name="partial_sums",
    )(keep, got, coarse)


def sum_kernel(parts_ref, _, out_ref):
    total = jnp.sum(parts_ref[...].astype(F32), axis=0, keepdims=True).astype(BF16)
    out_ref[...] = jnp.broadcast_to(total, out_ref.shape)


def sum_call(parts, after):
    return pl.pallas_call(
        sum_kernel,
        out_shape=jax.ShapeDtypeStruct(parts.shape, BF16),
        in_specs=vmem(1) + [pl.BlockSpec(memory_space=pl.ANY)],
        compiler_params=pltpu.CompilerParams(vmem_limit_bytes=4 << 20),
        cost_estimate=cost(0.7),
        name="chip_sums",
    )(parts, after)


def table_kernel(
    mine_ref, got_ref, okeep_ref, ogot_ref, right_ref, band_ref,
    out_ref, tokens_ref, fine_ref, coarse_ref, cols_f, cols_c,
):
    par = parity()
    half = right_ref.shape[2]
    tokens_ref[:, :, :half] = right_ref[...]
    tokens_ref[:, :, half:] = band_ref[:, :, :half]
    out_ref[...] = (okeep_ref[...].astype(F32) + ogot_ref[...].astype(F32)).astype(BF16)
    level = lax.broadcasted_iota(jnp.int32, (144, 128), 0) % 12 < 6
    for s in range(2):
        source = jnp.where(par == s, mine_ref[...].astype(F32), got_ref[...].astype(F32))
        for jm in range(6):
            tile = source[jm // 5 * 144 : jm // 5 * 144 + 144]
            if jm % 5:
                tile = pltpu.roll(tile, 128 - jm % 5 * 24, 1)
            base = s * 1728
            cols_f[pl.ds(base + jm, 144, stride=12), :] = jnp.where(level, tile, 0.0)
            cols_f[pl.ds(base + 6 + jm, 144, stride=12), :] = jnp.where(level, 0.0, tile)
        for b in range(12):
            tile = source[288 + b // 5 * 144 : 288 + b // 5 * 144 + 144]
            if b % 5:
                tile = pltpu.roll(tile, 128 - b % 5 * 24, 1)
            cols_c[pl.ds(s * 1728 + b, 144, stride=12), :] = tile
    for th in range(24):
        rows = slice(th * 144, (th + 1) * 144)
        fine_ref[th % 6, :, th // 6, :] = jnp.swapaxes(cols_f[rows, 0:24], 0, 1)[:23]
        coarse_ref[th % 12, :, th // 12, :] = jnp.swapaxes(cols_c[rows, 0:24], 0, 1)[:23]


def table_call(mine, got, okeep, ogot, right, band):
    shape = jax.ShapeDtypeStruct
    return pl.pallas_call(
        table_kernel,
        out_shape=(
            shape((12, 2, 6 * C2), BF16),
            shape((2, 24, WLON * C1), BF16),
            shape((6, 23, 4, 144), F32),
            shape((12, 23, 2, 144), F32),
        ),
        in_specs=vmem(6),
        scratch_shapes=[pltpu.VMEM((3456, 128), F32)] * 2,
        compiler_params=pltpu.CompilerParams(vmem_limit_bytes=10 << 20),
        cost_estimate=cost(2),
        name="results",
    )(mine, got, okeep, ogot, right, band)


def shifted(value, axis, steps):
    count = lax.axis_size(axis)
    return lax.ppermute(value, axis, [(s, (s + steps) % count) for s in range(count)])


def diagonal(value, steps):
    lon, lat = lax.axis_size("lon"), lax.axis_size("lat")
    pairs = [
        (a * lat + b, (a + steps) % lon * lat + (b + steps) % lat)
        for a in range(lon)
        for b in range(lat)
    ]
    return lax.ppermute(value, ("lon", "lat"), pairs)


def swapped(value):
    return lax.ppermute(value, "lon", [(s, s ^ 1) for s in range(lax.axis_size("lon"))])


def shards(
    tokens, fine_attend, fine_project, fine_gain_one, fine_expand, fine_reduce, fine_gain_two,
    fine_bias, merge_gain, merge_weight, coarse_attend, coarse_project, coarse_gain_one,
    coarse_expand, coarse_reduce, coarse_gain_two, coarse_bias, cotangent,
):
    fine_weights = (
        fine_attend, fine_project, fine_gain_one, fine_expand, fine_reduce.T, fine_gain_two,
    )
    coarse_weights = (
        coarse_attend, coarse_project, coarse_gain_one, coarse_expand, coarse_reduce,
        coarse_gain_two,
    )
    ef = spread_onehot(6, 128)
    ec = spread_onehot(12, 256)
    pick = merge_onehot()
    seed = jnp.transpose(cotangent, (1, 0, 2))
    seeds = (seed, swapped(seed))
    cols, top, corner = split_call(tokens)
    cols = shifted(cols, "lon", -1)
    corner = diagonal(corner, -1)
    top = shifted(top, "lat", -1)
    bias_fine = fine_bias_call(jnp.transpose(fine_bias, (1, 2, 0, 3)))
    bias_coarse = coarse_bias_call(jnp.transpose(coarse_bias, (1, 2, 0, 3)), ec)

    most, final = (0, 1, 2), (3,)
    y_last, strip, *saved_last = fine_call(
        final, (tokens, cols, top, corner), fine_weights, bias_fine
    )
    strip = shifted(strip, "lat", 1)
    y_most, *saved_most = fine_call(most, (tokens, cols), fine_weights, bias_fine)
    both, right, quads = merge_call(y_most, y_last, strip, pick, merge_gain, merge_weight)
    cells = (both, swapped(both), shifted(right, "lon", 1), shifted(right, "lon", 2))
    grad_both, grad_pboth, grad_even, grad_odd, out, grad_scores = coarse_call(
        cells, seeds, coarse_weights, bias_coarse
    )
    grads = (
        grad_both,
        swapped(grad_pboth),
        shifted(grad_even, "lon", -1),
        shifted(grad_odd, "lon", -2),
    )
    out_keep, out_send, table_coarse = coarse_rest_call(out, grad_scores, ec)
    grad_most, grad_last, grad_strip = merge_back_call(
        table_coarse, grads, quads, np.ascontiguousarray(pick.T), merge_gain, merge_weight
    )
    grad_strip = shifted(grad_strip, "lat", -1)
    body, table_most = fine_back_call(most, (grad_most,), saved_most, fine_weights, ef)
    grads = (grad_last, grad_strip, strip_onehot(), table_most, body)
    own, edge, table_keep, table_send = fine_back_call(
        final, grads, saved_last, fine_weights, ef
    )
    edge = shifted(edge, "lat", 1)
    partial = partial_call(table_keep, swapped(table_send), table_coarse).reshape(16, 48, 128)
    chips = [[2 * k + c for k in range(16)] for c in range(2)]
    partial = lax.all_to_all(partial, "lon", 0, 0, tiled=True, axis_index_groups=chips)
    sums = lax.all_to_all(sum_call(partial, edge), "lon", 0, 0, tiled=True, axis_index_groups=chips)
    sums = sums.reshape(768, 128)
    band = jnp.concatenate([edge, own], axis=1)
    right = shifted(band[:, :, band.shape[2] // 2 :], "lon", 1)
    coarse_out, grad_tokens, grad_fine, grad_coarse = table_call(
        sums, swapped(sums), out_keep, swapped(out_send), right, band
    )
    return (
        jnp.transpose(coarse_out, (1, 0, 2)),
        grad_tokens,
        jnp.transpose(grad_fine, (2, 0, 1, 3)),
        jnp.transpose(grad_coarse, (2, 0, 1, 3)),
    )


def solution(mesh):
    rows = P(None, "lat", "lon")
    table = P("lat", None, None, None)
    in_specs = (rows,) + (P(),) * 6 + (table,) + (P(),) * 8 + (table, rows)
    return jax.shard_map(
        shards, mesh=mesh, in_specs=in_specs, out_specs=(rows, rows, table, table), check_vma=False
    )
```

```python
import functools
import math

import jax
import jax.numpy as jnp
import numpy as np
from jax import lax
from jax.experimental import pallas as pl
from jax.experimental.pallas import tpu as pltpu
from jax.sharding import PartitionSpec as P

C1 = 192
C2 = 384
HD = 32
H1 = 6
H2 = 12
WLON = 12
HALF = 72
EPSILON = 1e-05
MASKED = -1000000000.0
SCALE = 1.0 / math.sqrt(HD)
F32 = jnp.float32
BF16 = jnp.bfloat16


def pair_lane(pair):
    return pair // 5 * 128 + pair % 5 * 24


def spread_onehot(pairs, lanes):
    onehot = np.zeros((WLON, (pairs + 4) // 5 * 128, lanes), np.float32)
    for p in range(WLON):
        for b in range(pairs):
            for q in range(WLON):
                onehot[p, pair_lane(b) + p - q + WLON - 1, b * WLON + q] = 1.0
    return onehot.astype(jnp.bfloat16)


def merge_onehot():
    onehot = np.zeros((4, 2, 2, 48, 648), np.float32)
    for rr in range(2):
        for cc in range(2):
            for bh in range(2):
                for lam in range(2):
                    for z in range(2):
                        for a in range(6):
                            for b in range(3):
                                row = 2 * (lam * 6 + a) + rr
                                col = 2 * (bh * 3 + b) + cc
                                if row < 3:
                                    cell = 576 + z * 36 + row * 12 + col
                                elif row < 21:
                                    cell = z * 216 + (row - 3) * 12 + col
                                else:
                                    cell = 432 + z * 72 + (row - 21) * 12 + col
                                onehot[rr * 2 + cc, bh, lam, z * 18 + a * 3 + b, cell] = 1.0
    return onehot.reshape(768, 648).astype(jnp.bfloat16)


def strip_onehot():
    onehot = np.zeros((144, 72), np.float32)
    for z in range(2):
        for k in range(36):
            onehot[z * 72 + 36 + k, z * 36 + k] = 1.0
    return onehot.astype(jnp.bfloat16)


def nn(left, right):
    return lax.dot_general(left, right, (((1,), (0,)), ((), ())), preferred_element_type=F32)


def nt(left, right):
    return lax.dot_general(left, right, (((1,), (1,)), ((), ())), preferred_element_type=F32)


def tn(left, right):
    return lax.dot_general(left, right, (((0,), (0,)), ((), ())), preferred_element_type=F32)


def norm_parts(values):
    average = jnp.mean(values, axis=-1, keepdims=True)
    centred = values - average
    scale = lax.rsqrt(jnp.mean(centred * centred, axis=-1, keepdims=True) + EPSILON)
    return centred * scale, scale


def norm_back(grad, normed, scale):
    first = jnp.mean(grad, axis=-1, keepdims=True)
    second = jnp.mean(grad * normed, axis=-1, keepdims=True)
    return scale * (grad - first - normed * second)


def split3(values):
    high = values.astype(BF16)
    rest = values - high.astype(F32)
    mid = rest.astype(BF16)
    low = (rest - mid.astype(F32)).astype(BF16)
    return high, mid, low


def head_mask(rows, heads, width):
    row = lax.broadcasted_iota(jnp.int32, (heads * rows, width), 0) // rows
    lane = lax.broadcasted_iota(jnp.int32, (heads * rows, width), 1) // HD
    return (row == lane).astype(F32)


def heads_stack(values, heads, mask):
    return (jnp.concatenate([values] * heads, axis=0) * mask).astype(BF16)


def heads_fold(stacked, heads, mask):
    rows = stacked.shape[0] // heads
    kept = stacked * mask
    total = kept[:rows]
    for h in range(1, heads):
        total = total + kept[h * rows : (h + 1) * rows]
    return total


def gelu_parts(values):
    phi = 0.5 * (1.0 + lax.erf(values * (1.0 / math.sqrt(2.0))))
    density = jnp.exp(-0.5 * values * values) * (1.0 / math.sqrt(2.0 * math.pi))
    return values * phi, phi + values * density


def softmax(scores):
    top = jnp.max(scores, axis=-1, keepdims=True)
    powers = jnp.exp(scores - top)
    return powers / jnp.sum(powers, axis=-1, keepdims=True)


def vmem(count):
    return [pl.BlockSpec(memory_space=pltpu.VMEM)] * count


def cost(microseconds):
    return pl.CostEstimate(
        flops=int(microseconds * 1e9), bytes_accessed=int(microseconds * 1e6), transcendentals=0
    )


def parity():
    return lax.rem(lax.axis_index("lon"), 2)


def fine_bias_kernel(table_ref, out_ref, cols_ref):
    key = lax.broadcasted_iota(jnp.int32, (256, 256), 0)
    lane = lax.broadcasted_iota(jnp.int32, (256, 256), 1) % 128
    second = lax.broadcasted_iota(jnp.int32, (256, 256), 1) // 128
    place = key % 128
    pair = key // 128 * 5 + place // 24
    meets = jnp.logical_and(pair == lane // 12, place < 120)
    column = jnp.where(meets, place % 24 + lane % 12 - (WLON - 1) - second, -2)
    cols_ref[...] = jnp.zeros_like(cols_ref)
    for th in range(24):
        cols_ref[th * 144 : (th + 1) * 144, 0:23] = jnp.swapaxes(
            table_ref[th % 6, :, th // 6, :], 0, 1
        )
    low_level = lax.broadcasted_iota(jnp.int32, (288, 128), 0) % 12 < 6
    tiles = []
    for t in range(2):
        tile = None
        for jm in range(t * 5, min(t * 5 + 5, 6)):
            piece = jnp.where(
                low_level,
                cols_ref[pl.ds(jm, 288, stride=12), :],
                cols_ref[pl.ds(6 + jm, 288, stride=12), :],
            )
            if jm % 5:
                piece = pltpu.roll(piece, jm % 5 * 24, 1)
            tile = piece if tile is None else tile + piece
        tiles.append(tile)
    parts = jnp.concatenate(split3(jnp.concatenate(tiles, axis=1)), axis=0)
    for p in range(0, WLON, 2):
        spread = nn(parts, (column == p).astype(F32).astype(BF16))
        total = spread[:288] + spread[288:576] + spread[576:]
        out_ref[pl.ds(p, 288, stride=12), :] = total[:, :128]
        out_ref[pl.ds(p + 1, 288, stride=12), :] = total[:, 128:]


def fine_bias_call(table):
    return pl.pallas_call(
        fine_bias_kernel,
        out_shape=jax.ShapeDtypeStruct((3456, 128), F32),
        in_specs=vmem(1),
        scratch_shapes=[pltpu.VMEM((3456, 128), F32)],
        compiler_params=pltpu.CompilerParams(vmem_limit_bytes=10 << 20),
        cost_estimate=cost(2),
        name="fine_bias_spread",
    )(table)


def coarse_bias_kernel(table_ref, onehot_ref, tail_ref, out_ref, cols_ref):
    cols_ref[...] = jnp.zeros_like(cols_ref)
    par = parity()
    for h in range(12):
        cols_ref[h * 144 : (h + 1) * 144, 0:23] = jnp.swapaxes(
            jnp.where(par == 0, table_ref[h, :, 0, :], table_ref[h, :, 1, :]), 0, 1
        )
    tiles = []
    for t in range(3):
        tile = None
        for b in range(t * 5, min(t * 5 + 5, 12)):
            piece = cols_ref[pl.ds(b, 144, stride=12), :]
            if b % 5:
                piece = pltpu.roll(piece, b % 5 * 24, 1)
            tile = piece if tile is None else tile + piece
        tiles.append(tile)
    parts = jnp.concatenate(split3(jnp.concatenate(tiles, axis=1)), axis=0)
    for p in range(0, WLON, 2):
        pair = jnp.concatenate([onehot_ref[p, :, :128], onehot_ref[p + 1, :, :128]], axis=1)
        spread = nn(parts, pair)
        total = spread[:144] + spread[144:288] + spread[288:]
        out_ref[0, pl.ds(p, 144, stride=12), :] = total[:, :128]
        out_ref[0, pl.ds(p + 1, 144, stride=12), :] = total[:, 128:]
    spread = nn(parts, tail_ref[...])
    total = spread[:144] + spread[144:288] + spread[288:]
    for p in range(WLON):
        tile = total[:, p // 8 * 128 : p // 8 * 128 + 128]
        if p % 8:
            tile = pltpu.roll(tile, 128 - p % 8 * 16, 1)
        out_ref[1, pl.ds(p, 144, stride=12), :] = tile


def coarse_bias_call(table, onehot):
    tail = np.zeros((onehot.shape[1], 256), onehot.dtype)
    for p in range(WLON):
        tail[:, p * 16 : p * 16 + 16] = onehot[p, :, 128:144]
    return pl.pallas_call(
        coarse_bias_kernel,
        out_shape=jax.ShapeDtypeStruct((2, 1728, 128), F32),
        in_specs=vmem(3),
        scratch_shapes=[pltpu.VMEM((1728, 128), F32)],
        compiler_params=pltpu.CompilerParams(vmem_limit_bytes=10 << 20),
        cost_estimate=cost(2),
        name="coarse_bias_spread",
    )(table, onehot, tail)


def split_kernel(tok_ref, left_ref, top_ref, corner_ref):
    half = left_ref.shape[2]
    left_ref[...] = tok_ref[:, :, :half]
    for z in range(2):
        rows = tok_ref[z].astype(F32)[:3]
        top_ref[z] = rows[:, half:].astype(BF16)
        corner_ref[z] = rows[:, :half].astype(BF16)


def split_call(tokens):
    levels, rows, width = tokens.shape
    shape = jax.ShapeDtypeStruct
    return pl.pallas_call(
        split_kernel,
        out_shape=(
            shape((levels, rows, width // 2), BF16),
            shape((levels, 3, width // 2), BF16),
            shape((levels, 3, width // 2), BF16),
        ),
        in_specs=vmem(1),
        compiler_params=pltpu.CompilerParams(vmem_limit_bytes=4 << 20),
        cost_estimate=cost(8),
        name="left_half",
    )(tokens)


def fine_kernel(windows, *refs):
    edge = windows[-1] == 3
    refs = list(refs)
    tok_ref, col_ref = refs[:2]
    top_ref, corner_ref = refs[2:4] if edge else (None, None)
    refs = refs[4:] if edge else refs[2:]
    wa_ref, wp_ref, g1_ref, we_ref, wr_ref, g2_ref, bias_ref, y_ref = refs[:8]
    strip_ref = refs[8] if edge else None
    refs = refs[9:] if edge else refs[8:]
    qkv_ref, a_ref, att_ref, slope_ref, red_ref = refs[:5]
    q_ref, k_ref, v_ref, o_ref, grid_ref, low_ref, high_ref, x_ref, edge_ref = refs[5:]
    rows = 6 * len(windows)
    own = rows - 3 if edge else rows
    start = 3 + 6 * windows[0]
    half = grid_ref.shape[1] // 2
    for z in range(2):
        base = z * rows
        grid_ref[base : base + own, :half] = tok_ref[z].astype(F32)[start : start + own, half:]
        grid_ref[base : base + own, half:] = col_ref[z].astype(F32)[start : start + own]
        if edge:
            grid_ref[base + own : base + rows, :half] = top_ref[z].astype(F32)
            grid_ref[base + own : base + rows, half:] = corner_ref[z].astype(F32)
    for col in range(WLON):
        piece = grid_ref[:, col * C1 : (col + 1) * C1]
        places = pl.ds(col, 2 * rows, stride=WLON)
        low_ref[places, :] = piece[:, :128]
        high_ref[places, :] = jnp.concatenate([piece[:, 128:]] * 2, axis=1)
    x_ref[...] = jnp.concatenate([low_ref[...], high_ref[:, :64]], axis=1)
    x = x_ref[...].astype(BF16)
    for part, wide_ref in enumerate((q_ref, k_ref, v_ref)):
        short = nn(x, wa_ref[:, part * C1 : (part + 1) * C1]).astype(BF16)
        qkv_ref[part] = short
        wide_ref[...] = short.astype(F32)
    mask = head_mask(HALF, H1, C1)
    last = lax.axis_index("lat") == lax.axis_size("lat") - 1
    for z in range(2):
        for n, w in enumerate(windows):
            block = z * len(windows) + n
            cells = slice(block * 72, block * 72 + 72)
            qs = heads_stack(q_ref[cells, :], H1, mask)
            places = [((w * 6 + h) * 2 + 1 - z) * 72 for h in range(H1)]
            bias = jnp.concatenate([bias_ref[s : s + 72, :] for s in places], axis=0)[:, :72]
            scores = nt(qs, k_ref[cells, :].astype(BF16)) * SCALE + bias
            if w == 3:
                row = lax.broadcasted_iota(jnp.int32, scores.shape, 0) % 72 < 36
                col = lax.broadcasted_iota(jnp.int32, scores.shape, 1) < 36
                scores = jnp.where(jnp.logical_and(row != col, last), MASKED, scores)
            weights = softmax(scores).astype(BF16)
            a_ref[block * 432 : (block + 1) * 432, :] = weights
            o_ref[cells, :] = heads_fold(nn(weights, v_ref[cells, :].astype(BF16)), H1, mask)
    for c in range(len(windows)):
        cells = slice(c * 144, (c + 1) * 144)
        att = nn(o_ref[cells, :].astype(BF16), wp_ref[...])
        att_ref[cells, :] = att
        normed, _ = norm_parts(att)
        middle = (x_ref[cells, :] + g1_ref[...][None, :] * normed).astype(BF16)
        act, slope = gelu_parts(nn(middle, we_ref[...]))
        slope_ref[cells, :] = slope.astype(BF16)
        red = nt(act.astype(BF16), wr_ref[...])
        red_ref[cells, :] = red
        normed, _ = norm_parts(red)
        out = middle.astype(F32) + g2_ref[...][None, :] * normed
        y_ref[cells, :] = out.astype(BF16)
        if edge:
            edge_ref[0:36, :] = out[36:72]
            edge_ref[36:72, :] = out[108:]
    if edge:
        strip_ref[...] = edge_ref[...].astype(BF16)


def fine_call(windows, cells, weights, bias):
    wa, wp, g1, we, wr, g2 = weights
    shape = jax.ShapeDtypeStruct
    count = len(windows)
    edge = windows[-1] == 3
    total = 144 * count
    return pl.pallas_call(
        functools.partial(fine_kernel, windows),
        out_shape=(shape((total, C1), BF16),)
        + ((shape((72, C1), BF16),) if edge else ())
        + (
            shape((3, total, C1), BF16),
            shape((count * 864, 72), BF16),
            shape((total, C1), F32),
            shape((total, 4 * C1), BF16),
            shape((total, C1), F32),
        ),
        in_specs=vmem(len(cells) + 7),
        scratch_shapes=[pltpu.VMEM((total, C1), F32)] * 4
        + [
            pltpu.VMEM((12 * count, WLON * C1), F32),
            pltpu.VMEM((total, 128), F32),
            pltpu.VMEM((total, 128), F32),
            pltpu.VMEM((total, C1), F32),
            pltpu.VMEM((72, C1), F32),
        ],
        compiler_params=pltpu.CompilerParams(vmem_limit_bytes=14 << 20),
        cost_estimate=cost(count + 0.5),
        name=f"fine_forward_{count}",
    )(*cells, wa, wp, g1, we, wr, g2, bias)


def merge_kernel(y_ref, last_ref, strip_ref, pick_ref, gain_ref, w_ref, both_ref, right_ref, f_ref):
    gain = gain_ref[...][None, :]
    cells = jnp.concatenate([y_ref[...], last_ref[...], strip_ref[...]], axis=0)
    f = nn(pick_ref[...], cells)
    f_ref[...] = f.astype(BF16)
    total = sum(jnp.sum(f[k * 192 : (k + 1) * 192], axis=-1, keepdims=True) for k in range(4))
    average = total * (1.0 / 768)
    centred = [f[k * 192 : (k + 1) * 192] - average for k in range(4)]
    square = sum(jnp.sum(c * c, axis=-1, keepdims=True) for c in centred)
    scale = lax.rsqrt(square * (1.0 / 768) + EPSILON)
    result = None
    for k in range(4):
        normed = (gain[:, k * C1 : (k + 1) * C1] * (centred[k] * scale)).astype(BF16)
        part = nn(normed, w_ref[k * 192 : (k + 1) * 192, :])
        result = part if result is None else result + part
    both_ref[...] = result.astype(BF16)
    right_ref[...] = result[96:].astype(BF16)


def merge_call(y, last, strip, pick, gain, weight):
    shape = jax.ShapeDtypeStruct
    return pl.pallas_call(
        merge_kernel,
        out_shape=(shape((192, C2), BF16), shape((96, C2), BF16), shape((768, C1), BF16)),
        in_specs=vmem(6),
        compiler_params=pltpu.CompilerParams(vmem_limit_bytes=8 << 20),
        cost_estimate=cost(1.5),
        name="merge_forward",
    )(y, last, strip, pick, gain, weight)


def window_places(par):
    row = lax.broadcasted_iota(jnp.int32, (144, 576), 0)
    z, a, c = row // 72, row // 12 % 6, row % 12
    group = c // 3
    even = jnp.where(group == 0, 4, jnp.where(group == 1, 0, jnp.where(group == 2, 1, 2)))
    odd = jnp.where(group == 0, 5, jnp.where(group == 1, 2, jnp.where(group == 2, 3, 0)))
    source = jnp.where(par == 0, even, odd)
    place = source * 96 + par * 48 + z * 18 + a * 3 + c % 3
    return (place == lax.broadcasted_iota(jnp.int32, (144, 576), 1)).astype(F32).astype(BF16)


def half_places(par):
    row = lax.broadcasted_iota(jnp.int32, (144, 288), 0)
    z, a, c = row // 72, row // 12 % 6, row % 12
    side = jnp.where(c // 6 == par, 0, 1)
    place = (side * 6 + c % 6) * 24 + z * 12 + par * 6 + a
    return (place == lax.broadcasted_iota(jnp.int32, (144, 288), 1)).astype(F32).astype(BF16)


def coarse_kernel(
    both_ref, pboth_ref, even_ref, odd_ref, seed_ref, pseed_ref,
    wa_ref, wp_ref, g1_ref, we_ref, wr_ref, g2_ref, bias_ref,
    gboth_ref, gpboth_ref, geven_ref, godd_ref, out_ref, ds_ref,
    a_ref, qs_ref, o_ref, slope_ref, band_ref, packed_ref,
):
    par = parity()
    pick = window_places(par)
    half = half_places(par)
    cells = [both_ref[...], pboth_ref[...], even_ref[...], odd_ref[...]]
    x = nn(pick, jnp.concatenate(cells, axis=0)).astype(BF16)
    for side, source_ref in enumerate((seed_ref, pseed_ref)):
        wide = source_ref[...].astype(F32)
        for z in range(2):
            band_ref[side, z * 12 : (z + 1) * 12, :] = wide[:, z, :]
    bands = [
        band_ref[side, :, col * C2 : (col + 1) * C2] for side in range(2) for col in range(6)
    ]
    seed = nn(half, jnp.concatenate(bands, axis=0).astype(BF16))
    ds_ref[1] = jnp.zeros_like(ds_ref[1])
    packed = nn(x, wa_ref[...]).astype(BF16)
    mask = head_mask(144, 4, 128)
    for g in range(3):
        lanes = slice(g * 128, (g + 1) * 128)
        rows = slice(g * 576, (g + 1) * 576)
        qs = heads_stack(packed[:, lanes].astype(F32), 4, mask)
        qs_ref[rows, :] = qs
        key = packed[:, C2 + g * 128 : C2 + (g + 1) * 128]
        value = packed[:, 2 * C2 + g * 128 : 2 * C2 + (g + 1) * 128]
        bias = jnp.concatenate([bias_ref[0, rows, :], bias_ref[1, rows, :]], axis=1)[:, :144]
        weights = softmax(nt(qs, key) * SCALE + bias).astype(BF16)
        a_ref[rows, :] = weights
        o_ref[:, lanes] = heads_fold(nn(weights, value), 4, mask)
    att = nn(o_ref[...].astype(BF16), wp_ref[...])
    normed1, scale1 = norm_parts(att)
    middle = (x.astype(F32) + g1_ref[...][None, :] * normed1).astype(BF16)
    act, slope = gelu_parts(nn(middle, we_ref[...]))
    slope_ref[...] = slope
    red = nn(act.astype(BF16), wr_ref[...])
    normed2, scale2 = norm_parts(red)
    out_ref[...] = (middle.astype(F32) + g2_ref[...][None, :] * normed2).astype(BF16)
    grad_red = norm_back(seed * g2_ref[...][None, :], normed2, scale2).astype(BF16)
    grad_act = nt(grad_red, wr_ref[...]).astype(BF16).astype(F32)
    grad_exp = (grad_act * slope_ref[...]).astype(BF16)
    grad_middle = (seed + nt(grad_exp, we_ref[...]).astype(BF16).astype(F32)).astype(BF16)
    grad_middle = grad_middle.astype(F32)
    grad_att = norm_back(grad_middle * g1_ref[...][None, :], normed1, scale1).astype(BF16)
    grad_o = nt(grad_att, wp_ref[...]).astype(BF16)
    for g in range(3):
        lanes = slice(g * 128, (g + 1) * 128)
        rows = slice(g * 576, (g + 1) * 576)
        os = heads_stack(grad_o[:, lanes].astype(F32), 4, mask)
        key = packed[:, C2 + g * 128 : C2 + (g + 1) * 128]
        value = packed[:, 2 * C2 + g * 128 : 2 * C2 + (g + 1) * 128]
        weights = a_ref[rows, :]
        grad_a = nt(os, value)
        wide = weights.astype(F32)
        grad_s = wide * (grad_a - jnp.sum(wide * grad_a, axis=-1, keepdims=True))
        ds_ref[0, rows, :] = grad_s[:, :128]
        ds_ref[1, rows, 0:16] = grad_s[:, 128:]
        short = grad_s.astype(BF16)
        grad_v = tn(weights, os).astype(BF16)
        grad_q = (heads_fold(nn(short, key), 4, mask) * SCALE).astype(BF16)
        grad_k = (tn(short, qs_ref[rows, :]) * SCALE).astype(BF16)
        for part, grad in enumerate((grad_q, grad_k, grad_v)):
            packed_ref[:, part * C2 + g * 128 : part * C2 + (g + 1) * 128] = grad
    grad_x = grad_middle + nt(packed_ref[...], wa_ref[...])
    parted = tn(pick, grad_x.astype(BF16)).astype(BF16)
    gboth_ref[...] = parted[:192]
    gpboth_ref[...] = parted[192:384]
    geven_ref[...] = parted[384:480]
    godd_ref[...] = parted[480:]


def coarse_rest_kernel(out_ref, ds_ref, ec_ref, okeep_ref, osend_ref, dt_ref, cells_ref):
    half = half_places(parity())
    out = out_ref[...]
    parted = tn(half, out)
    for side in range(2):
        for col in range(6):
            lanes = slice(col * C2, (col + 1) * C2)
            for z in range(2):
                place = (side * 6 + col) * 24 + z * 12
                cells_ref[side, :, z, lanes] = parted[place : place + 12]
    okeep_ref[...] = cells_ref[0].astype(BF16)
    osend_ref[...] = cells_ref[1].astype(BF16)
    table = None
    for p in range(WLON):
        places = pl.ds(p, 144, stride=12)
        piece = jnp.concatenate([ds_ref[0, places, :], ds_ref[1, places, :]], axis=1).astype(BF16)
        part = nt(piece, ec_ref[p])
        table = part if table is None else table + part
    for t in range(3):
        dt_ref[t * 144 : (t + 1) * 144, :] = table[:, t * 128 : (t + 1) * 128].astype(BF16)


def coarse_rest_call(out, ds, ec):
    shape = jax.ShapeDtypeStruct
    return pl.pallas_call(
        coarse_rest_kernel,
        out_shape=(
            shape((12, 2, 6 * C2), BF16),
            shape((12, 2, 6 * C2), BF16),
            shape((432, 128), BF16),
        ),
        in_specs=vmem(3),
        scratch_shapes=[pltpu.VMEM((2, 12, 2, 6 * C2), F32)],
        compiler_params=pltpu.CompilerParams(vmem_limit_bytes=10 << 20),
        cost_estimate=cost(1.5),
        name="coarse_rest",
    )(out, ds, ec)


def coarse_call(cells, seeds, weights, bias):
    wa, wp, g1, we, wr, g2 = weights
    shape = jax.ShapeDtypeStruct
    return pl.pallas_call(
        coarse_kernel,
        out_shape=(
            shape((192, C2), BF16),
            shape((192, C2), BF16),
            shape((96, C2), BF16),
            shape((96, C2), BF16),
            shape((144, C2), BF16),
            shape((2, 1728, 128), F32),
        ),
        in_specs=vmem(13),
        scratch_shapes=[
            pltpu.VMEM((1728, 144), BF16),
            pltpu.VMEM((1728, 128), BF16),
            pltpu.VMEM((144, C2), F32),
            pltpu.VMEM((144, 4 * C2), F32),
            pltpu.VMEM((2, 24, 6 * C2), F32),
            pltpu.VMEM((144, 3 * C2), BF16),
        ],
        compiler_params=pltpu.CompilerParams(vmem_limit_bytes=20 << 20),
        cost_estimate=cost(7),
        name="coarse_both",
    )(*cells, *seeds, wa, wp, g1, we, wr, g2, bias)


def merge_back_kernel(_, g_ref, pg_ref, even_ref, odd_ref, f_ref, place_ref, gain_ref, w_ref, gy_ref, glast_ref, gstrip_ref):
    f = f_ref[...].astype(F32)
    total = sum(jnp.sum(f[k * 192 : (k + 1) * 192], axis=-1, keepdims=True) for k in range(4))
    average = total * (1.0 / 768)
    centred = [f[k * 192 : (k + 1) * 192] - average for k in range(4)]
    square = sum(jnp.sum(c * c, axis=-1, keepdims=True) for c in centred)
    scale = lax.rsqrt(square * (1.0 / 768) + EPSILON)
    gain = gain_ref[...][None, :]
    both = g_ref[...].astype(F32) + pg_ref[...].astype(F32)
    right = both[96:] + even_ref[...].astype(F32) + odd_ref[...].astype(F32)
    g = jnp.concatenate([both[:96], right], axis=0).astype(BF16)
    normed = [c * scale for c in centred]
    grads = []
    for k in range(4):
        part = nt(g, w_ref[k * 192 : (k + 1) * 192, :]).astype(BF16).astype(F32)
        grads.append(part * gain[:, k * C1 : (k + 1) * C1])
    first = sum(jnp.sum(p, axis=-1, keepdims=True) for p in grads) * (1.0 / 768)
    second = sum(jnp.sum(p * n, axis=-1, keepdims=True) for p, n in zip(grads, normed))
    second = second * (1.0 / 768)
    back = [(scale * (p - first - n * second)).astype(BF16) for p, n in zip(grads, normed)]
    placed = nn(place_ref[...], jnp.concatenate(back, axis=0)).astype(BF16)
    gy_ref[...] = placed[:432]
    glast_ref[...] = placed[432:576]
    gstrip_ref[...] = placed[576:]


def merge_back_call(after, grads, f, place, gain, weight):
    shape = jax.ShapeDtypeStruct
    return pl.pallas_call(
        merge_back_kernel,
        out_shape=(shape((432, C1), BF16), shape((144, C1), BF16), shape((72, C1), BF16)),
        in_specs=[pl.BlockSpec(memory_space=pl.ANY)] + vmem(8),
        compiler_params=pltpu.CompilerParams(vmem_limit_bytes=8 << 20),
        cost_estimate=cost(1),
        name="merge_backward",
    )(after, *grads, f, place, gain, weight)


def fine_back_kernel(windows, *refs):
    edge = windows[-1] == 3
    count = len(windows)
    refs = list(refs)
    gy_ref = refs.pop(0)
    if edge:
        strip_ref, place_ref, table_ref, body_ref = refs[:4]
        refs = refs[4:]
    qkv_ref, a_ref, att_ref, slope_ref, red_ref = refs[:5]
    wa_ref, wp_ref, g1_ref, we_ref, wr_ref, g2_ref, ef_ref = refs[5:12]
    refs = refs[12:]
    if edge:
        own_ref, last_ref, keep_ref, send_ref = refs[:4]
        refs = refs[4:]
    else:
        gx_ref, dt_ref = refs[:2]
        refs = refs[2:]
    low_ref, high_ref, grid_ref, q_ref, k_ref, v_ref = refs[:6]
    gm_ref, go_ref, dq_ref, dk_ref, dv_ref, ds_ref = refs[6:12]
    for part, wide_ref in enumerate((q_ref, k_ref, v_ref)):
        wide_ref[...] = qkv_ref[part].astype(F32)
    ds_ref[...] = jnp.zeros_like(ds_ref)
    for c in range(count):
        cells = slice(c * 144, (c + 1) * 144)
        seed = gy_ref[cells, :].astype(F32)
        if edge:
            seed = seed + nn(place_ref[...], strip_ref[...])
        normed, scale = norm_parts(red_ref[cells, :])
        grad_red = norm_back(seed * g2_ref[...][None, :], normed, scale).astype(BF16)
        grad_act = nn(grad_red, wr_ref[...]).astype(BF16).astype(F32)
        grad_exp = (grad_act * slope_ref[cells, :].astype(F32)).astype(BF16)
        grad_middle = seed + nt(grad_exp, we_ref[...]).astype(BF16).astype(F32)
        grad_middle = grad_middle.astype(BF16).astype(F32)
        gm_ref[cells, :] = grad_middle
        normed, scale = norm_parts(att_ref[cells, :])
        grad_att = norm_back(grad_middle * g1_ref[...][None, :], normed, scale).astype(BF16)
        go_ref[cells, :] = nt(grad_att, wp_ref[...]).astype(BF16).astype(F32)
    mask = head_mask(HALF, H1, C1)
    for z in range(2):
        for n in range(count):
            block = z * count + n
            cells = slice(block * 72, block * 72 + 72)
            os = heads_stack(go_ref[cells, :], H1, mask)
            qs = heads_stack(q_ref[cells, :], H1, mask)
            weights = a_ref[block * 432 : (block + 1) * 432, :]
            grad_a = nt(os, v_ref[cells, :].astype(BF16))
            wide = weights.astype(F32)
            grad_s = wide * (grad_a - jnp.sum(wide * grad_a, axis=-1, keepdims=True))
            for h in range(H1):
                place = ((n * 6 + h) * 2 + 1 - z) * 72
                ds_ref[place : place + 72, 0:72] = grad_s[h * 72 : (h + 1) * 72]
            short = grad_s.astype(BF16)
            dv_ref[cells, :] = tn(weights, os)
            dq_ref[cells, :] = heads_fold(nn(short, k_ref[cells, :].astype(BF16)), H1, mask) * SCALE
            dk_ref[cells, :] = tn(short, qs) * SCALE
    table = None
    for p in range(WLON):
        piece = ds_ref[pl.ds(p, 72 * count, stride=12), :].astype(BF16)
        part = nt(piece, ef_ref[p])
        table = part if table is None else table + part
    if edge:
        first = parity() == 0
        whole = jnp.concatenate([table_ref[...], table], axis=0)
        for half_ref, taken in ((keep_ref, first), (send_ref, jnp.logical_not(first))):
            half = jnp.where(taken, whole[:144], whole[144:]).astype(BF16)
            half_ref[:144, :] = half[:, :128]
            half_ref[144:, :] = half[:, 128:]
    else:
        dt_ref[...] = table
    total = gm_ref[...]
    total = total + nt(dq_ref[...].astype(BF16), wa_ref[:, :C1])
    total = total + nt(dk_ref[...].astype(BF16), wa_ref[:, C1 : 2 * C1])
    total = total + nt(dv_ref[...].astype(BF16), wa_ref[:, 2 * C1 :])
    low_ref[...] = total[:, :128]
    high_ref[:, 0:64] = total[:, 128:]
    rows = 6 * count
    for col in range(WLON):
        lanes = slice(col * C1, (col + 1) * C1)
        low = low_ref[pl.ds(col, 2 * rows, stride=WLON), :]
        high = high_ref[pl.ds(col, 2 * rows, stride=WLON), :]
        grid_ref[:, lanes] = jnp.concatenate([low, high[:, :64]], axis=1)
    for z in range(2):
        band = grid_ref[z * rows : (z + 1) * rows, :]
        if edge:
            own_ref[z] = jnp.concatenate([body_ref[z].astype(F32), band[:3]], axis=0).astype(BF16)
            last_ref[z] = band[3:].astype(BF16)
        else:
            gx_ref[z] = band.astype(BF16)


def fine_back_call(windows, grads, saved, weights, ef):
    wa, wp, g1, we, wr, g2 = weights
    shape = jax.ShapeDtypeStruct
    count = len(windows)
    total = 144 * count
    width = WLON * C1
    if windows[-1] == 3:
        outs = (shape((2, 21, width), BF16), shape((2, 3, width), BF16))
        outs = outs + (shape((288, 128), BF16),) * 2
    else:
        outs = (shape((2, 6 * count, width), BF16), shape((72 * count, 256), F32))
    return pl.pallas_call(
        functools.partial(fine_back_kernel, windows),
        out_shape=outs,
        in_specs=vmem(len(grads) + 12),
        scratch_shapes=[pltpu.VMEM((total, 128), F32)] * 2
        + [pltpu.VMEM((12 * count, width), F32)]
        + [pltpu.VMEM((total, C1), F32)] * 8
        + [pltpu.VMEM((864 * count, 128), F32)],
        compiler_params=pltpu.CompilerParams(vmem_limit_bytes=16 << 20),
        cost_estimate=cost(2 * count),
        name=f"fine_backward_{count}",
    )(*grads, *saved, wa, wp, g1, we, wr, g2, ef)


def partial_kernel(keep_ref, got_ref, coarse_ref, out_ref):
    fine = keep_ref[...].astype(F32) + got_ref[...].astype(F32)
    coarse = coarse_ref[...].astype(F32)
    out_ref[:144, :] = fine[:144].astype(BF16)
    out_ref[144:288, :] = (pltpu.roll(fine[144:], 48, 1) + coarse[288:]).astype(BF16)
    out_ref[288:576, :] = coarse[:288].astype(BF16)
    out_ref[576:, :] = jnp.zeros((64, 128), BF16)


def partial_call(keep, got, coarse):
    return pl.pallas_call(
        partial_kernel,
        out_shape=jax.ShapeDtypeStruct((640, 128), BF16),
        in_specs=vmem(3),
        compiler_params=pltpu.CompilerParams(vmem_limit_bytes=4 << 20),
        cost_estimate=cost(0.5),
        name="partial_sums",
    )(keep, got, coarse)


def sum_kernel(parts_ref, _, out_ref):
    total = jnp.sum(parts_ref[...].astype(F32), axis=0, keepdims=True).astype(BF16)
    out_ref[...] = jnp.broadcast_to(total, out_ref.shape)


def sum_call(parts, after):
    return pl.pallas_call(
        sum_kernel,
        out_shape=jax.ShapeDtypeStruct(parts.shape, BF16),
        in_specs=vmem(1) + [pl.BlockSpec(memory_space=pl.ANY)],
        compiler_params=pltpu.CompilerParams(vmem_limit_bytes=4 << 20),
        cost_estimate=cost(0.7),
        name="chip_sums",
    )(parts, after)


def table_kernel(
    mine_ref, got_ref, okeep_ref, ogot_ref, right_ref, band_ref,
    out_ref, tokens_ref, fine_ref, coarse_ref, cols_f, cols_c,
):
    par = parity()
    half = right_ref.shape[2]
    tokens_ref[:, :, :half] = right_ref[...]
    tokens_ref[:, :, half:] = band_ref[:, :, :half]
    out_ref[...] = (okeep_ref[...].astype(F32) + ogot_ref[...].astype(F32)).astype(BF16)
    level = lax.broadcasted_iota(jnp.int32, (144, 128), 0) % 12 < 6
    for s in range(2):
        source = jnp.where(par == s, mine_ref[...].astype(F32), got_ref[...].astype(F32))
        for jm in range(6):
            tile = source[jm // 5 * 144 : jm // 5 * 144 + 144]
            lane = 48 if jm == 5 else jm * 24
            if lane:
                tile = pltpu.roll(tile, 128 - lane, 1)
            base = s * 1728
            cols_f[pl.ds(base + jm, 144, stride=12), :] = jnp.where(level, tile, 0.0)
            cols_f[pl.ds(base + 6 + jm, 144, stride=12), :] = jnp.where(level, 0.0, tile)
        for b in range(12):
            place = (288, 432, 144)[b // 5]
            tile = source[place : place + 144]
            if b % 5:
                tile = pltpu.roll(tile, 128 - b % 5 * 24, 1)
            cols_c[pl.ds(s * 1728 + b, 144, stride=12), :] = tile
    for th in range(24):
        rows = slice(th * 144, (th + 1) * 144)
        fine_ref[th % 6, :, th // 6, :] = jnp.swapaxes(cols_f[rows, 0:24], 0, 1)[:23]
        coarse_ref[th % 12, :, th // 12, :] = jnp.swapaxes(cols_c[rows, 0:24], 0, 1)[:23]


def table_call(mine, got, okeep, ogot, right, band):
    shape = jax.ShapeDtypeStruct
    return pl.pallas_call(
        table_kernel,
        out_shape=(
            shape((12, 2, 6 * C2), BF16),
            shape((2, 24, WLON * C1), BF16),
            shape((6, 23, 4, 144), F32),
            shape((12, 23, 2, 144), F32),
        ),
        in_specs=vmem(6),
        scratch_shapes=[pltpu.VMEM((3456, 128), F32)] * 2,
        compiler_params=pltpu.CompilerParams(vmem_limit_bytes=10 << 20),
        cost_estimate=cost(2),
        name="results",
    )(mine, got, okeep, ogot, right, band)


def shifted(value, axis, steps):
    count = lax.axis_size(axis)
    return lax.ppermute(value, axis, [(s, (s + steps) % count) for s in range(count)])


def diagonal(value, steps):
    lon, lat = lax.axis_size("lon"), lax.axis_size("lat")
    pairs = [
        (a * lat + b, (a + steps) % lon * lat + (b + steps) % lat)
        for a in range(lon)
        for b in range(lat)
    ]
    return lax.ppermute(value, ("lon", "lat"), pairs)


def swapped(value):
    return lax.ppermute(value, "lon", [(s, s ^ 1) for s in range(lax.axis_size("lon"))])


def shards(
    tokens, fine_attend, fine_project, fine_gain_one, fine_expand, fine_reduce, fine_gain_two,
    fine_bias, merge_gain, merge_weight, coarse_attend, coarse_project, coarse_gain_one,
    coarse_expand, coarse_reduce, coarse_gain_two, coarse_bias, cotangent,
):
    fine_weights = (
        fine_attend, fine_project, fine_gain_one, fine_expand, fine_reduce.T, fine_gain_two,
    )
    coarse_weights = (
        coarse_attend, coarse_project, coarse_gain_one, coarse_expand, coarse_reduce,
        coarse_gain_two,
    )
    ef = spread_onehot(6, 128)
    ec = spread_onehot(12, 256)
    pick = merge_onehot()
    seed = jnp.transpose(cotangent, (1, 0, 2))
    seeds = (seed, swapped(seed))
    cols, top, corner = split_call(tokens)
    cols = shifted(cols, "lon", -1)
    corner = diagonal(corner, -1)
    top = shifted(top, "lat", -1)
    bias_fine = fine_bias_call(jnp.transpose(fine_bias, (1, 2, 0, 3)))
    bias_coarse = coarse_bias_call(jnp.transpose(coarse_bias, (1, 2, 0, 3)), ec)

    most, final = (0, 1, 2), (3,)
    y_last, strip, *saved_last = fine_call(
        final, (tokens, cols, top, corner), fine_weights, bias_fine
    )
    strip = shifted(strip, "lat", 1)
    y_most, *saved_most = fine_call(most, (tokens, cols), fine_weights, bias_fine)
    both, right, quads = merge_call(y_most, y_last, strip, pick, merge_gain, merge_weight)
    cells = (both, swapped(both), shifted(right, "lon", 1), shifted(right, "lon", 2))
    grad_both, grad_pboth, grad_even, grad_odd, out, grad_scores = coarse_call(
        cells, seeds, coarse_weights, bias_coarse
    )
    grads = (
        grad_both,
        swapped(grad_pboth),
        shifted(grad_even, "lon", -1),
        shifted(grad_odd, "lon", -2),
    )
    out_keep, out_send, table_coarse = coarse_rest_call(out, grad_scores, ec)
    grad_most, grad_last, grad_strip = merge_back_call(
        table_coarse, grads, quads, np.ascontiguousarray(pick.T), merge_gain, merge_weight
    )
    grad_strip = shifted(grad_strip, "lat", -1)
    body, table_most = fine_back_call(most, (grad_most,), saved_most, fine_weights, ef)
    grads = (grad_last, grad_strip, strip_onehot(), table_most, body)
    own, edge, table_keep, table_send = fine_back_call(
        final, grads, saved_last, fine_weights, ef
    )
    edge = shifted(edge, "lat", 1)
    partial = partial_call(table_keep, swapped(table_send), table_coarse).reshape(16, 40, 128)
    chips = [[2 * k + c for k in range(16)] for c in range(2)]
    partial = lax.all_to_all(partial, "lon", 0, 0, tiled=True, axis_index_groups=chips)
    sums = lax.all_to_all(sum_call(partial, edge), "lon", 0, 0, tiled=True, axis_index_groups=chips)
    sums = sums.reshape(640, 128)
    band = jnp.concatenate([edge, own], axis=1)
    right = shifted(band[:, :, band.shape[2] // 2 :], "lon", 1)
    coarse_out, grad_tokens, grad_fine, grad_coarse = table_call(
        sums, swapped(sums), out_keep, swapped(out_send), right, band
    )
    return (
        jnp.transpose(coarse_out, (1, 0, 2)),
        grad_tokens,
        jnp.transpose(grad_fine, (2, 0, 1, 3)),
        jnp.transpose(grad_coarse, (2, 0, 1, 3)),
    )


def solution(mesh):
    rows = P(None, "lat", "lon")
    table = P("lat", None, None, None)
    in_specs = (rows,) + (P(),) * 6 + (table,) + (P(),) * 8 + (table, rows)
    return jax.shard_map(
        shards, mesh=mesh, in_specs=in_specs, out_specs=(rows, rows, table, table), check_vma=False
    )
```

```python
import functools
import math

import jax
import jax.numpy as jnp
import numpy as np
from jax import lax
from jax.experimental import pallas as pl
from jax.experimental.pallas import tpu as pltpu
from jax.sharding import PartitionSpec as P

C1 = 192
C2 = 384
HD = 32
H1 = 6
H2 = 12
WLON = 12
HALF = 72
EPSILON = 1e-05
MASKED = -1000000000.0
SCALE = 1.0 / math.sqrt(HD)
F32 = jnp.float32
BF16 = jnp.bfloat16


def pair_lane(pair):
    return pair // 5 * 128 + pair % 5 * 24


def spread_onehot(pairs, lanes):
    onehot = np.zeros((WLON, (pairs + 4) // 5 * 128, lanes), np.float32)
    for p in range(WLON):
        for b in range(pairs):
            for q in range(WLON):
                onehot[p, pair_lane(b) + p - q + WLON - 1, b * WLON + q] = 1.0
    return onehot.astype(jnp.bfloat16)


def merge_onehot():
    onehot = np.zeros((4, 2, 2, 48, 648), np.float32)
    for rr in range(2):
        for cc in range(2):
            for bh in range(2):
                for lam in range(2):
                    for z in range(2):
                        for a in range(6):
                            for b in range(3):
                                row = 2 * (lam * 6 + a) + rr
                                col = 2 * (bh * 3 + b) + cc
                                if row < 3:
                                    cell = 576 + z * 36 + row * 12 + col
                                elif row < 21:
                                    cell = z * 216 + (row - 3) * 12 + col
                                else:
                                    cell = 432 + z * 72 + (row - 21) * 12 + col
                                onehot[rr * 2 + cc, bh, lam, z * 18 + a * 3 + b, cell] = 1.0
    return onehot.reshape(768, 648).astype(jnp.bfloat16)


def strip_onehot():
    onehot = np.zeros((144, 72), np.float32)
    for z in range(2):
        for k in range(36):
            onehot[z * 72 + 36 + k, z * 36 + k] = 1.0
    return onehot.astype(jnp.bfloat16)


def nn(left, right):
    return lax.dot_general(left, right, (((1,), (0,)), ((), ())), preferred_element_type=F32)


def nt(left, right):
    return lax.dot_general(left, right, (((1,), (1,)), ((), ())), preferred_element_type=F32)


def tn(left, right):
    return lax.dot_general(left, right, (((0,), (0,)), ((), ())), preferred_element_type=F32)


def norm_parts(values):
    average = jnp.mean(values, axis=-1, keepdims=True)
    centred = values - average
    scale = lax.rsqrt(jnp.mean(centred * centred, axis=-1, keepdims=True) + EPSILON)
    return centred * scale, scale


def norm_back(grad, normed, scale):
    first = jnp.mean(grad, axis=-1, keepdims=True)
    second = jnp.mean(grad * normed, axis=-1, keepdims=True)
    return scale * (grad - first - normed * second)


def split3(values):
    high = values.astype(BF16)
    rest = values - high.astype(F32)
    mid = rest.astype(BF16)
    low = (rest - mid.astype(F32)).astype(BF16)
    return high, mid, low


def head_mask(rows, heads, width):
    row = lax.broadcasted_iota(jnp.int32, (heads * rows, width), 0) // rows
    lane = lax.broadcasted_iota(jnp.int32, (heads * rows, width), 1) // HD
    return (row == lane).astype(F32)


def heads_stack(values, heads, mask):
    return (jnp.concatenate([values] * heads, axis=0) * mask).astype(BF16)


def heads_fold(stacked, heads, mask):
    rows = stacked.shape[0] // heads
    kept = stacked * mask
    total = kept[:rows]
    for h in range(1, heads):
        total = total + kept[h * rows : (h + 1) * rows]
    return total


def gelu_parts(values):
    phi = 0.5 * (1.0 + lax.erf(values * (1.0 / math.sqrt(2.0))))
    density = jnp.exp(-0.5 * values * values) * (1.0 / math.sqrt(2.0 * math.pi))
    return values * phi, phi + values * density


def softmax(scores):
    top = jnp.max(scores, axis=-1, keepdims=True)
    powers = jnp.exp(scores - top)
    return powers / jnp.sum(powers, axis=-1, keepdims=True)


def vmem(count):
    return [pl.BlockSpec(memory_space=pltpu.VMEM)] * count


def cost(microseconds):
    return pl.CostEstimate(
        flops=int(microseconds * 1e9), bytes_accessed=int(microseconds * 1e6), transcendentals=0
    )


def parity():
    return lax.rem(lax.axis_index("lon"), 2)


def fine_bias_kernel(table_ref, out_ref, cols_ref):
    key = lax.broadcasted_iota(jnp.int32, (256, 256), 0)
    lane = lax.broadcasted_iota(jnp.int32, (256, 256), 1) % 128
    second = lax.broadcasted_iota(jnp.int32, (256, 256), 1) // 128
    place = key % 128
    pair = key // 128 * 5 + place // 24
    meets = jnp.logical_and(pair == lane // 12, place < 120)
    column = jnp.where(meets, place % 24 + lane % 12 - (WLON - 1) - second, -2)
    cols_ref[...] = jnp.zeros_like(cols_ref)
    for th in range(24):
        cols_ref[th * 144 : (th + 1) * 144, 0:23] = jnp.swapaxes(
            table_ref[th % 6, :, th // 6, :], 0, 1
        )
    low_level = lax.broadcasted_iota(jnp.int32, (288, 128), 0) % 12 < 6
    tiles = []
    for t in range(2):
        tile = None
        for jm in range(t * 5, min(t * 5 + 5, 6)):
            piece = jnp.where(
                low_level,
                cols_ref[pl.ds(jm, 288, stride=12), :],
                cols_ref[pl.ds(6 + jm, 288, stride=12), :],
            )
            if jm % 5:
                piece = pltpu.roll(piece, jm % 5 * 24, 1)
            tile = piece if tile is None else tile + piece
        tiles.append(tile)
    parts = jnp.concatenate(split3(jnp.concatenate(tiles, axis=1)), axis=0)
    for p in range(0, WLON, 2):
        spread = nn(parts, (column == p).astype(F32).astype(BF16))
        total = spread[:288] + spread[288:576] + spread[576:]
        out_ref[pl.ds(p, 288, stride=12), :] = total[:, :128]
        out_ref[pl.ds(p + 1, 288, stride=12), :] = total[:, 128:]


def fine_bias_call(table):
    return pl.pallas_call(
        fine_bias_kernel,
        out_shape=jax.ShapeDtypeStruct((3456, 128), F32),
        in_specs=vmem(1),
        scratch_shapes=[pltpu.VMEM((3456, 128), F32)],
        compiler_params=pltpu.CompilerParams(vmem_limit_bytes=10 << 20),
        cost_estimate=cost(2),
        name="fine_bias_spread",
    )(table)


def coarse_bias_kernel(table_ref, onehot_ref, tail_ref, out_ref, cols_ref):
    cols_ref[...] = jnp.zeros_like(cols_ref)
    par = parity()
    for h in range(12):
        cols_ref[h * 144 : (h + 1) * 144, 0:23] = jnp.swapaxes(
            jnp.where(par == 0, table_ref[h, :, 0, :], table_ref[h, :, 1, :]), 0, 1
        )
    tiles = []
    for t in range(3):
        tile = None
        for b in range(t * 5, min(t * 5 + 5, 12)):
            piece = cols_ref[pl.ds(b, 144, stride=12), :]
            if b % 5:
                piece = pltpu.roll(piece, b % 5 * 24, 1)
            tile = piece if tile is None else tile + piece
        tiles.append(tile)
    parts = jnp.concatenate(split3(jnp.concatenate(tiles, axis=1)), axis=0)
    for p in range(0, WLON, 2):
        pair = jnp.concatenate([onehot_ref[p, :, :128], onehot_ref[p + 1, :, :128]], axis=1)
        spread = nn(parts, pair)
        total = spread[:144] + spread[144:288] + spread[288:]
        out_ref[0, pl.ds(p, 144, stride=12), :] = total[:, :128]
        out_ref[0, pl.ds(p + 1, 144, stride=12), :] = total[:, 128:]
    spread = nn(parts, tail_ref[...])
    total = spread[:144] + spread[144:288] + spread[288:]
    for p in range(WLON):
        tile = total[:, p // 8 * 128 : p // 8 * 128 + 128]
        if p % 8:
            tile = pltpu.roll(tile, 128 - p % 8 * 16, 1)
        out_ref[1, pl.ds(p, 144, stride=12), :] = tile


def coarse_bias_call(table, onehot):
    tail = np.zeros((onehot.shape[1], 256), onehot.dtype)
    for p in range(WLON):
        tail[:, p * 16 : p * 16 + 16] = onehot[p, :, 128:144]
    return pl.pallas_call(
        coarse_bias_kernel,
        out_shape=jax.ShapeDtypeStruct((2, 1728, 128), F32),
        in_specs=vmem(3),
        scratch_shapes=[pltpu.VMEM((1728, 128), F32)],
        compiler_params=pltpu.CompilerParams(vmem_limit_bytes=10 << 20),
        cost_estimate=cost(2),
        name="coarse_bias_spread",
    )(table, onehot, tail)


def split_kernel(tok_ref, left_ref, top_ref, corner_ref):
    half = left_ref.shape[2]
    left_ref[...] = tok_ref[:, :, :half]
    for z in range(2):
        rows = tok_ref[z].astype(F32)[:3]
        top_ref[z] = rows[:, half:].astype(BF16)
        corner_ref[z] = rows[:, :half].astype(BF16)


def split_call(tokens):
    levels, rows, width = tokens.shape
    shape = jax.ShapeDtypeStruct
    return pl.pallas_call(
        split_kernel,
        out_shape=(
            shape((levels, rows, width // 2), BF16),
            shape((levels, 3, width // 2), BF16),
            shape((levels, 3, width // 2), BF16),
        ),
        in_specs=vmem(1),
        compiler_params=pltpu.CompilerParams(vmem_limit_bytes=4 << 20),
        cost_estimate=cost(8),
        name="left_half",
    )(tokens)


def fine_kernel(windows, *refs):
    edge = windows[-1] == 3
    refs = list(refs)
    tok_ref, col_ref = refs[:2]
    top_ref, corner_ref = refs[2:4] if edge else (None, None)
    refs = refs[4:] if edge else refs[2:]
    wa_ref, wp_ref, g1_ref, we_ref, wr_ref, g2_ref, bias_ref, y_ref = refs[:8]
    strip_ref = refs[8] if edge else None
    refs = refs[9:] if edge else refs[8:]
    qkv_ref, a_ref, att_ref, slope_ref, red_ref = refs[:5]
    q_ref, k_ref, v_ref, o_ref, grid_ref, low_ref, high_ref, x_ref, edge_ref = refs[5:]
    rows = 6 * len(windows)
    own = rows - 3 if edge else rows
    start = 3 + 6 * windows[0]
    half = grid_ref.shape[1] // 2
    for z in range(2):
        base = z * rows
        grid_ref[base : base + own, :half] = tok_ref[z].astype(F32)[start : start + own, half:]
        grid_ref[base : base + own, half:] = col_ref[z].astype(F32)[start : start + own]
        if edge:
            grid_ref[base + own : base + rows, :half] = top_ref[z].astype(F32)
            grid_ref[base + own : base + rows, half:] = corner_ref[z].astype(F32)
    for col in range(WLON):
        piece = grid_ref[:, col * C1 : (col + 1) * C1]
        places = pl.ds(col, 2 * rows, stride=WLON)
        low_ref[places, :] = piece[:, :128]
        high_ref[places, :] = jnp.concatenate([piece[:, 128:]] * 2, axis=1)
    x_ref[...] = jnp.concatenate([low_ref[...], high_ref[:, :64]], axis=1)
    x = x_ref[...].astype(BF16)
    for part, wide_ref in enumerate((q_ref, k_ref, v_ref)):
        short = nn(x, wa_ref[:, part * C1 : (part + 1) * C1]).astype(BF16)
        qkv_ref[part] = short
        wide_ref[...] = short.astype(F32)
    mask = head_mask(HALF, H1, C1)
    last = lax.axis_index("lat") == lax.axis_size("lat") - 1
    for z in range(2):
        for n, w in enumerate(windows):
            block = z * len(windows) + n
            cells = slice(block * 72, block * 72 + 72)
            qs = heads_stack(q_ref[cells, :], H1, mask)
            places = [((w * 6 + h) * 2 + 1 - z) * 72 for h in range(H1)]
            bias = jnp.concatenate([bias_ref[s : s + 72, :] for s in places], axis=0)[:, :72]
            scores = nt(qs, k_ref[cells, :].astype(BF16)) * SCALE + bias
            if w == 3:
                row = lax.broadcasted_iota(jnp.int32, scores.shape, 0) % 72 < 36
                col = lax.broadcasted_iota(jnp.int32, scores.shape, 1) < 36
                scores = jnp.where(jnp.logical_and(row != col, last), MASKED, scores)
            weights = softmax(scores).astype(BF16)
            a_ref[block * 432 : (block + 1) * 432, :] = weights
            o_ref[cells, :] = heads_fold(nn(weights, v_ref[cells, :].astype(BF16)), H1, mask)
    for c in range(len(windows)):
        cells = slice(c * 144, (c + 1) * 144)
        att = nn(o_ref[cells, :].astype(BF16), wp_ref[...])
        att_ref[cells, :] = att
        normed, _ = norm_parts(att)
        middle = (x_ref[cells, :] + g1_ref[...][None, :] * normed).astype(BF16)
        act, slope = gelu_parts(nn(middle, we_ref[...]))
        slope_ref[cells, :] = slope.astype(BF16)
        red = nt(act.astype(BF16), wr_ref[...])
        red_ref[cells, :] = red
        normed, _ = norm_parts(red)
        out = middle.astype(F32) + g2_ref[...][None, :] * normed
        y_ref[cells, :] = out.astype(BF16)
        if edge:
            edge_ref[0:36, :] = out[36:72]
            edge_ref[36:72, :] = out[108:]
    if edge:
        strip_ref[...] = edge_ref[...].astype(BF16)


def fine_call(windows, cells, weights, bias):
    wa, wp, g1, we, wr, g2 = weights
    shape = jax.ShapeDtypeStruct
    count = len(windows)
    edge = windows[-1] == 3
    total = 144 * count
    return pl.pallas_call(
        functools.partial(fine_kernel, windows),
        out_shape=(shape((total, C1), BF16),)
        + ((shape((72, C1), BF16),) if edge else ())
        + (
            shape((3, total, C1), BF16),
            shape((count * 864, 72), BF16),
            shape((total, C1), F32),
            shape((total, 4 * C1), BF16),
            shape((total, C1), F32),
        ),
        in_specs=vmem(len(cells) + 7),
        scratch_shapes=[pltpu.VMEM((total, C1), F32)] * 4
        + [
            pltpu.VMEM((12 * count, WLON * C1), F32),
            pltpu.VMEM((total, 128), F32),
            pltpu.VMEM((total, 128), F32),
            pltpu.VMEM((total, C1), F32),
            pltpu.VMEM((72, C1), F32),
        ],
        compiler_params=pltpu.CompilerParams(vmem_limit_bytes=14 << 20),
        cost_estimate=cost(count + 0.5),
        name=f"fine_forward_{count}",
    )(*cells, wa, wp, g1, we, wr, g2, bias)


def merge_kernel(y_ref, last_ref, strip_ref, pick_ref, gain_ref, w_ref, both_ref, upper_ref, lower_ref, f_ref):
    gain = gain_ref[...][None, :]
    cells = jnp.concatenate([y_ref[...], last_ref[...], strip_ref[...]], axis=0)
    f = nn(pick_ref[...], cells)
    f_ref[...] = f.astype(BF16)
    total = sum(jnp.sum(f[k * 192 : (k + 1) * 192], axis=-1, keepdims=True) for k in range(4))
    average = total * (1.0 / 768)
    centred = [f[k * 192 : (k + 1) * 192] - average for k in range(4)]
    square = sum(jnp.sum(c * c, axis=-1, keepdims=True) for c in centred)
    scale = lax.rsqrt(square * (1.0 / 768) + EPSILON)
    result = None
    for k in range(4):
        normed = (gain[:, k * C1 : (k + 1) * C1] * (centred[k] * scale)).astype(BF16)
        part = nn(normed, w_ref[k * 192 : (k + 1) * 192, :])
        result = part if result is None else result + part
    both_ref[...] = result.astype(BF16)
    upper_ref[...] = result[96:144].astype(BF16)
    lower_ref[...] = result[144:].astype(BF16)


def merge_call(y, last, strip, pick, gain, weight):
    shape = jax.ShapeDtypeStruct
    return pl.pallas_call(
        merge_kernel,
        out_shape=(
            shape((192, C2), BF16),
            shape((48, C2), BF16),
            shape((48, C2), BF16),
            shape((768, C1), BF16),
        ),
        in_specs=vmem(6),
        compiler_params=pltpu.CompilerParams(vmem_limit_bytes=8 << 20),
        cost_estimate=cost(1.5),
        name="merge_forward",
    )(y, last, strip, pick, gain, weight)


def window_places(par):
    row = lax.broadcasted_iota(jnp.int32, (144, 480), 0)
    z, a, c = row // 72, row // 12 % 6, row % 12
    group = c // 3
    even = jnp.where(group == 0, 8, jnp.where(group == 1, 0, jnp.where(group == 2, 2, 4)))
    odd = jnp.where(group == 0, 9, jnp.where(group == 1, 5, jnp.where(group == 2, 7, 1)))
    source = jnp.where(par == 0, even, odd)
    place = source * 48 + z * 18 + a * 3 + c % 3
    return (place == lax.broadcasted_iota(jnp.int32, (144, 480), 1)).astype(F32).astype(BF16)


def half_places(par):
    row = lax.broadcasted_iota(jnp.int32, (144, 288), 0)
    z, a, c = row // 72, row // 12 % 6, row % 12
    side = jnp.where(c // 6 == par, 0, 1)
    place = (side * 6 + c % 6) * 24 + z * 12 + par * 6 + a
    return (place == lax.broadcasted_iota(jnp.int32, (144, 288), 1)).astype(F32).astype(BF16)


def coarse_kernel(
    both_ref, pboth_ref, even_ref, odd_ref, seed_ref, pseed_ref,
    wa_ref, wp_ref, g1_ref, we_ref, wr_ref, g2_ref, bias_ref,
    gboth_ref, gpboth_ref, geven_ref, godd_ref, out_ref, ds_ref,
    a_ref, qs_ref, o_ref, slope_ref, band_ref, packed_ref,
):
    par = parity()
    pick = window_places(par)
    half = half_places(par)
    cells = [both_ref[...], pboth_ref[...], even_ref[...], odd_ref[...]]
    x = nn(pick, jnp.concatenate(cells, axis=0)).astype(BF16)
    for side, source_ref in enumerate((seed_ref, pseed_ref)):
        wide = source_ref[...].astype(F32)
        for z in range(2):
            band_ref[side, z * 12 : (z + 1) * 12, :] = wide[:, z, :]
    bands = [
        band_ref[side, :, col * C2 : (col + 1) * C2] for side in range(2) for col in range(6)
    ]
    seed = nn(half, jnp.concatenate(bands, axis=0).astype(BF16))
    ds_ref[1] = jnp.zeros_like(ds_ref[1])
    packed = nn(x, wa_ref[...]).astype(BF16)
    mask = head_mask(144, 4, 128)
    for g in range(3):
        lanes = slice(g * 128, (g + 1) * 128)
        rows = slice(g * 576, (g + 1) * 576)
        qs = heads_stack(packed[:, lanes].astype(F32), 4, mask)
        qs_ref[rows, :] = qs
        key = packed[:, C2 + g * 128 : C2 + (g + 1) * 128]
        value = packed[:, 2 * C2 + g * 128 : 2 * C2 + (g + 1) * 128]
        bias = jnp.concatenate([bias_ref[0, rows, :], bias_ref[1, rows, :]], axis=1)[:, :144]
        weights = softmax(nt(qs, key) * SCALE + bias).astype(BF16)
        a_ref[rows, :] = weights
        o_ref[:, lanes] = heads_fold(nn(weights, value), 4, mask)
    att = nn(o_ref[...].astype(BF16), wp_ref[...])
    normed1, scale1 = norm_parts(att)
    middle = (x.astype(F32) + g1_ref[...][None, :] * normed1).astype(BF16)
    act, slope = gelu_parts(nn(middle, we_ref[...]))
    slope_ref[...] = slope
    red = nn(act.astype(BF16), wr_ref[...])
    normed2, scale2 = norm_parts(red)
    out_ref[...] = (middle.astype(F32) + g2_ref[...][None, :] * normed2).astype(BF16)
    grad_red = norm_back(seed * g2_ref[...][None, :], normed2, scale2).astype(BF16)
    grad_act = nt(grad_red, wr_ref[...]).astype(BF16).astype(F32)
    grad_exp = (grad_act * slope_ref[...]).astype(BF16)
    grad_middle = (seed + nt(grad_exp, we_ref[...]).astype(BF16).astype(F32)).astype(BF16)
    grad_middle = grad_middle.astype(F32)
    grad_att = norm_back(grad_middle * g1_ref[...][None, :], normed1, scale1).astype(BF16)
    grad_o = nt(grad_att, wp_ref[...]).astype(BF16)
    for g in range(3):
        lanes = slice(g * 128, (g + 1) * 128)
        rows = slice(g * 576, (g + 1) * 576)
        os = heads_stack(grad_o[:, lanes].astype(F32), 4, mask)
        key = packed[:, C2 + g * 128 : C2 + (g + 1) * 128]
        value = packed[:, 2 * C2 + g * 128 : 2 * C2 + (g + 1) * 128]
        weights = a_ref[rows, :]
        grad_a = nt(os, value)
        wide = weights.astype(F32)
        grad_s = wide * (grad_a - jnp.sum(wide * grad_a, axis=-1, keepdims=True))
        ds_ref[0, rows, :] = grad_s[:, :128]
        ds_ref[1, rows, 0:16] = grad_s[:, 128:]
        short = grad_s.astype(BF16)
        grad_v = tn(weights, os).astype(BF16)
        grad_q = (heads_fold(nn(short, key), 4, mask) * SCALE).astype(BF16)
        grad_k = (tn(short, qs_ref[rows, :]) * SCALE).astype(BF16)
        for part, grad in enumerate((grad_q, grad_k, grad_v)):
            packed_ref[:, part * C2 + g * 128 : part * C2 + (g + 1) * 128] = grad
    grad_x = grad_middle + nt(packed_ref[...], wa_ref[...])
    parted = tn(pick, grad_x.astype(BF16)).astype(BF16)
    gboth_ref[...] = parted[:192]
    gpboth_ref[...] = parted[192:384]
    geven_ref[...] = parted[384:432]
    godd_ref[...] = parted[432:]


def coarse_rest_kernel(out_ref, ds_ref, ec_ref, okeep_ref, osend_ref, dt_ref, cells_ref):
    half = half_places(parity())
    out = out_ref[...]
    parted = tn(half, out)
    for side in range(2):
        for col in range(6):
            lanes = slice(col * C2, (col + 1) * C2)
            for z in range(2):
                place = (side * 6 + col) * 24 + z * 12
                cells_ref[side, :, z, lanes] = parted[place : place + 12]
    okeep_ref[...] = cells_ref[0].astype(BF16)
    osend_ref[...] = cells_ref[1].astype(BF16)
    table = None
    for p in range(WLON):
        places = pl.ds(p, 144, stride=12)
        piece = jnp.concatenate([ds_ref[0, places, :], ds_ref[1, places, :]], axis=1).astype(BF16)
        part = nt(piece, ec_ref[p])
        table = part if table is None else table + part
    for t in range(3):
        dt_ref[t * 144 : (t + 1) * 144, :] = table[:, t * 128 : (t + 1) * 128].astype(BF16)


def coarse_rest_call(out, ds, ec):
    shape = jax.ShapeDtypeStruct
    return pl.pallas_call(
        coarse_rest_kernel,
        out_shape=(
            shape((12, 2, 6 * C2), BF16),
            shape((12, 2, 6 * C2), BF16),
            shape((432, 128), BF16),
        ),
        in_specs=vmem(3),
        scratch_shapes=[pltpu.VMEM((2, 12, 2, 6 * C2), F32)],
        compiler_params=pltpu.CompilerParams(vmem_limit_bytes=10 << 20),
        cost_estimate=cost(1.5),
        name="coarse_rest",
    )(out, ds, ec)


def coarse_call(cells, seeds, weights, bias):
    wa, wp, g1, we, wr, g2 = weights
    shape = jax.ShapeDtypeStruct
    return pl.pallas_call(
        coarse_kernel,
        out_shape=(
            shape((192, C2), BF16),
            shape((192, C2), BF16),
            shape((48, C2), BF16),
            shape((48, C2), BF16),
            shape((144, C2), BF16),
            shape((2, 1728, 128), F32),
        ),
        in_specs=vmem(13),
        scratch_shapes=[
            pltpu.VMEM((1728, 144), BF16),
            pltpu.VMEM((1728, 128), BF16),
            pltpu.VMEM((144, C2), F32),
            pltpu.VMEM((144, 4 * C2), F32),
            pltpu.VMEM((2, 24, 6 * C2), F32),
            pltpu.VMEM((144, 3 * C2), BF16),
        ],
        compiler_params=pltpu.CompilerParams(vmem_limit_bytes=20 << 20),
        cost_estimate=cost(7),
        name="coarse_both",
    )(*cells, *seeds, wa, wp, g1, we, wr, g2, bias)


def merge_back_kernel(_, g_ref, pg_ref, even_ref, odd_ref, f_ref, place_ref, gain_ref, w_ref, gy_ref, glast_ref, gstrip_ref):
    f = f_ref[...].astype(F32)
    total = sum(jnp.sum(f[k * 192 : (k + 1) * 192], axis=-1, keepdims=True) for k in range(4))
    average = total * (1.0 / 768)
    centred = [f[k * 192 : (k + 1) * 192] - average for k in range(4)]
    square = sum(jnp.sum(c * c, axis=-1, keepdims=True) for c in centred)
    scale = lax.rsqrt(square * (1.0 / 768) + EPSILON)
    gain = gain_ref[...][None, :]
    both = g_ref[...].astype(F32) + pg_ref[...].astype(F32)
    upper = both[96:144] + even_ref[...].astype(F32)
    lower = both[144:] + odd_ref[...].astype(F32)
    g = jnp.concatenate([both[:96], upper, lower], axis=0).astype(BF16)
    normed = [c * scale for c in centred]
    grads = []
    for k in range(4):
        part = nt(g, w_ref[k * 192 : (k + 1) * 192, :]).astype(BF16).astype(F32)
        grads.append(part * gain[:, k * C1 : (k + 1) * C1])
    first = sum(jnp.sum(p, axis=-1, keepdims=True) for p in grads) * (1.0 / 768)
    second = sum(jnp.sum(p * n, axis=-1, keepdims=True) for p, n in zip(grads, normed))
    second = second * (1.0 / 768)
    back = [(scale * (p - first - n * second)).astype(BF16) for p, n in zip(grads, normed)]
    placed = nn(place_ref[...], jnp.concatenate(back, axis=0)).astype(BF16)
    gy_ref[...] = placed[:432]
    glast_ref[...] = placed[432:576]
    gstrip_ref[...] = placed[576:]


def merge_back_call(after, grads, f, place, gain, weight):
    shape = jax.ShapeDtypeStruct
    return pl.pallas_call(
        merge_back_kernel,
        out_shape=(shape((432, C1), BF16), shape((144, C1), BF16), shape((72, C1), BF16)),
        in_specs=[pl.BlockSpec(memory_space=pl.ANY)] + vmem(8),
        compiler_params=pltpu.CompilerParams(vmem_limit_bytes=8 << 20),
        cost_estimate=cost(1),
        name="merge_backward",
    )(after, *grads, f, place, gain, weight)


def fine_back_kernel(windows, *refs):
    edge = windows[-1] == 3
    count = len(windows)
    refs = list(refs)
    gy_ref = refs.pop(0)
    if edge:
        strip_ref, place_ref, table_ref, body_ref = refs[:4]
        refs = refs[4:]
    qkv_ref, a_ref, att_ref, slope_ref, red_ref = refs[:5]
    wa_ref, wp_ref, g1_ref, we_ref, wr_ref, g2_ref, ef_ref = refs[5:12]
    refs = refs[12:]
    if edge:
        own_ref, last_ref, keep_ref, send_ref = refs[:4]
        refs = refs[4:]
    else:
        gx_ref, dt_ref = refs[:2]
        refs = refs[2:]
    low_ref, high_ref, grid_ref, q_ref, k_ref, v_ref = refs[:6]
    gm_ref, go_ref, dq_ref, dk_ref, dv_ref, ds_ref = refs[6:12]
    for part, wide_ref in enumerate((q_ref, k_ref, v_ref)):
        wide_ref[...] = qkv_ref[part].astype(F32)
    ds_ref[...] = jnp.zeros_like(ds_ref)
    for c in range(count):
        cells = slice(c * 144, (c + 1) * 144)
        seed = gy_ref[cells, :].astype(F32)
        if edge:
            seed = seed + nn(place_ref[...], strip_ref[...])
        normed, scale = norm_parts(red_ref[cells, :])
        grad_red = norm_back(seed * g2_ref[...][None, :], normed, scale).astype(BF16)
        grad_act = nn(grad_red, wr_ref[...]).astype(BF16).astype(F32)
        grad_exp = (grad_act * slope_ref[cells, :].astype(F32)).astype(BF16)
        grad_middle = seed + nt(grad_exp, we_ref[...]).astype(BF16).astype(F32)
        grad_middle = grad_middle.astype(BF16).astype(F32)
        gm_ref[cells, :] = grad_middle
        normed, scale = norm_parts(att_ref[cells, :])
        grad_att = norm_back(grad_middle * g1_ref[...][None, :], normed, scale).astype(BF16)
        go_ref[cells, :] = nt(grad_att, wp_ref[...]).astype(BF16).astype(F32)
    mask = head_mask(HALF, H1, C1)
    for z in range(2):
        for n in range(count):
            block = z * count + n
            cells = slice(block * 72, block * 72 + 72)
            os = heads_stack(go_ref[cells, :], H1, mask)
            qs = heads_stack(q_ref[cells, :], H1, mask)
            weights = a_ref[block * 432 : (block + 1) * 432, :]
            grad_a = nt(os, v_ref[cells, :].astype(BF16))
            wide = weights.astype(F32)
            grad_s = wide * (grad_a - jnp.sum(wide * grad_a, axis=-1, keepdims=True))
            for h in range(H1):
                place = ((n * 6 + h) * 2 + 1 - z) * 72
                ds_ref[place : place + 72, 0:72] = grad_s[h * 72 : (h + 1) * 72]
            short = grad_s.astype(BF16)
            dv_ref[cells, :] = tn(weights, os)
            dq_ref[cells, :] = heads_fold(nn(short, k_ref[cells, :].astype(BF16)), H1, mask) * SCALE
            dk_ref[cells, :] = tn(short, qs) * SCALE
    table = None
    for p in range(WLON):
        piece = ds_ref[pl.ds(p, 72 * count, stride=12), :].astype(BF16)
        part = nt(piece, ef_ref[p])
        table = part if table is None else table + part
    if edge:
        first = parity() == 0
        whole = jnp.concatenate([table_ref[...], table], axis=0)
        for half_ref, taken in ((keep_ref, first), (send_ref, jnp.logical_not(first))):
            half = jnp.where(taken, whole[:144], whole[144:]).astype(BF16)
            half_ref[:144, :] = half[:, :128]
            half_ref[144:, :] = half[:, 128:]
    else:
        dt_ref[...] = table
    total = gm_ref[...]
    total = total + nt(dq_ref[...].astype(BF16), wa_ref[:, :C1])
    total = total + nt(dk_ref[...].astype(BF16), wa_ref[:, C1 : 2 * C1])
    total = total + nt(dv_ref[...].astype(BF16), wa_ref[:, 2 * C1 :])
    low_ref[...] = total[:, :128]
    high_ref[:, 0:64] = total[:, 128:]
    rows = 6 * count
    for col in range(WLON):
        lanes = slice(col * C1, (col + 1) * C1)
        low = low_ref[pl.ds(col, 2 * rows, stride=WLON), :]
        high = high_ref[pl.ds(col, 2 * rows, stride=WLON), :]
        grid_ref[:, lanes] = jnp.concatenate([low, high[:, :64]], axis=1)
    for z in range(2):
        band = grid_ref[z * rows : (z + 1) * rows, :]
        if edge:
            own_ref[z] = jnp.concatenate([body_ref[z].astype(F32), band[:3]], axis=0).astype(BF16)
            last_ref[z] = band[3:].astype(BF16)
        else:
            gx_ref[z] = band.astype(BF16)


def fine_back_call(windows, grads, saved, weights, ef):
    wa, wp, g1, we, wr, g2 = weights
    shape = jax.ShapeDtypeStruct
    count = len(windows)
    total = 144 * count
    width = WLON * C1
    if windows[-1] == 3:
        outs = (shape((2, 21, width), BF16), shape((2, 3, width), BF16))
        outs = outs + (shape((288, 128), BF16),) * 2
    else:
        outs = (shape((2, 6 * count, width), BF16), shape((72 * count, 256), F32))
    return pl.pallas_call(
        functools.partial(fine_back_kernel, windows),
        out_shape=outs,
        in_specs=vmem(len(grads) + 12),
        scratch_shapes=[pltpu.VMEM((total, 128), F32)] * 2
        + [pltpu.VMEM((12 * count, width), F32)]
        + [pltpu.VMEM((total, C1), F32)] * 8
        + [pltpu.VMEM((864 * count, 128), F32)],
        compiler_params=pltpu.CompilerParams(vmem_limit_bytes=16 << 20),
        cost_estimate=cost(2 * count),
        name=f"fine_backward_{count}",
    )(*grads, *saved, wa, wp, g1, we, wr, g2, ef)


def partial_kernel(keep_ref, got_ref, coarse_ref, out_ref):
    fine = keep_ref[...].astype(F32) + got_ref[...].astype(F32)
    coarse = coarse_ref[...].astype(F32)
    out_ref[:144, :] = fine[:144].astype(BF16)
    out_ref[144:288, :] = (pltpu.roll(fine[144:], 48, 1) + coarse[288:]).astype(BF16)
    out_ref[288:576, :] = coarse[:288].astype(BF16)
    out_ref[576:, :] = jnp.zeros((64, 128), BF16)


def partial_call(keep, got, coarse):
    return pl.pallas_call(
        partial_kernel,
        out_shape=jax.ShapeDtypeStruct((640, 128), BF16),
        in_specs=vmem(3),
        compiler_params=pltpu.CompilerParams(vmem_limit_bytes=4 << 20),
        cost_estimate=cost(0.5),
        name="partial_sums",
    )(keep, got, coarse)


def sum_kernel(parts_ref, _, out_ref):
    total = jnp.sum(parts_ref[...].astype(F32), axis=0, keepdims=True).astype(BF16)
    out_ref[...] = jnp.broadcast_to(total, out_ref.shape)


def sum_call(parts, after):
    return pl.pallas_call(
        sum_kernel,
        out_shape=jax.ShapeDtypeStruct(parts.shape, BF16),
        in_specs=vmem(1) + [pl.BlockSpec(memory_space=pl.ANY)],
        compiler_params=pltpu.CompilerParams(vmem_limit_bytes=4 << 20),
        cost_estimate=cost(0.7),
        name="chip_sums",
    )(parts, after)


def table_kernel(
    mine_ref, got_ref, okeep_ref, ogot_ref, right_ref, band_ref,
    out_ref, tokens_ref, fine_ref, coarse_ref, cols_f, cols_c,
):
    par = parity()
    half = right_ref.shape[2]
    tokens_ref[:, :, :half] = right_ref[...]
    tokens_ref[:, :, half:] = band_ref[:, :, :half]
    out_ref[...] = (okeep_ref[...].astype(F32) + ogot_ref[...].astype(F32)).astype(BF16)
    level = lax.broadcasted_iota(jnp.int32, (144, 128), 0) % 12 < 6
    for s in range(2):
        source = jnp.where(par == s, mine_ref[...].astype(F32), got_ref[...].astype(F32))
        for jm in range(6):
            tile = source[jm // 5 * 144 : jm // 5 * 144 + 144]
            lane = 48 if jm == 5 else jm * 24
            if lane:
                tile = pltpu.roll(tile, 128 - lane, 1)
            base = s * 1728
            cols_f[pl.ds(base + jm, 144, stride=12), :] = jnp.where(level, tile, 0.0)
            cols_f[pl.ds(base + 6 + jm, 144, stride=12), :] = jnp.where(level, 0.0, tile)
        for b in range(12):
            place = (288, 432, 144)[b // 5]
            tile = source[place : place + 144]
            if b % 5:
                tile = pltpu.roll(tile, 128 - b % 5 * 24, 1)
            cols_c[pl.ds(s * 1728 + b, 144, stride=12), :] = tile
    for th in range(24):
        rows = slice(th * 144, (th + 1) * 144)
        fine_ref[th % 6, :, th // 6, :] = jnp.swapaxes(cols_f[rows, 0:24], 0, 1)[:23]
        coarse_ref[th % 12, :, th // 12, :] = jnp.swapaxes(cols_c[rows, 0:24], 0, 1)[:23]


def table_call(mine, got, okeep, ogot, right, band):
    shape = jax.ShapeDtypeStruct
    return pl.pallas_call(
        table_kernel,
        out_shape=(
            shape((12, 2, 6 * C2), BF16),
            shape((2, 24, WLON * C1), BF16),
            shape((6, 23, 4, 144), F32),
            shape((12, 23, 2, 144), F32),
        ),
        in_specs=vmem(6),
        scratch_shapes=[pltpu.VMEM((3456, 128), F32)] * 2,
        compiler_params=pltpu.CompilerParams(vmem_limit_bytes=10 << 20),
        cost_estimate=cost(2),
        name="results",
    )(mine, got, okeep, ogot, right, band)


def shifted(value, axis, steps):
    count = lax.axis_size(axis)
    return lax.ppermute(value, axis, [(s, (s + steps) % count) for s in range(count)])


def diagonal(value, steps):
    lon, lat = lax.axis_size("lon"), lax.axis_size("lat")
    pairs = [
        (a * lat + b, (a + steps) % lon * lat + (b + steps) % lat)
        for a in range(lon)
        for b in range(lat)
    ]
    return lax.ppermute(value, ("lon", "lat"), pairs)


def swapped(value):
    return lax.ppermute(value, "lon", [(s, s ^ 1) for s in range(lax.axis_size("lon"))])


def shards(
    tokens, fine_attend, fine_project, fine_gain_one, fine_expand, fine_reduce, fine_gain_two,
    fine_bias, merge_gain, merge_weight, coarse_attend, coarse_project, coarse_gain_one,
    coarse_expand, coarse_reduce, coarse_gain_two, coarse_bias, cotangent,
):
    fine_weights = (
        fine_attend, fine_project, fine_gain_one, fine_expand, fine_reduce.T, fine_gain_two,
    )
    coarse_weights = (
        coarse_attend, coarse_project, coarse_gain_one, coarse_expand, coarse_reduce,
        coarse_gain_two,
    )
    ef = spread_onehot(6, 128)
    ec = spread_onehot(12, 256)
    pick = merge_onehot()
    seed = jnp.transpose(cotangent, (1, 0, 2))
    seeds = (seed, swapped(seed))
    cols, top, corner = split_call(tokens)
    cols = shifted(cols, "lon", -1)
    corner = diagonal(corner, -1)
    top = shifted(top, "lat", -1)
    bias_fine = fine_bias_call(jnp.transpose(fine_bias, (1, 2, 0, 3)))
    bias_coarse = coarse_bias_call(jnp.transpose(coarse_bias, (1, 2, 0, 3)), ec)

    most, final = (0, 1, 2), (3,)
    y_last, strip, *saved_last = fine_call(
        final, (tokens, cols, top, corner), fine_weights, bias_fine
    )
    strip = shifted(strip, "lat", 1)
    y_most, *saved_most = fine_call(most, (tokens, cols), fine_weights, bias_fine)
    both, upper, lower, quads = merge_call(y_most, y_last, strip, pick, merge_gain, merge_weight)
    cells = (both, swapped(both), shifted(upper, "lon", 1), shifted(lower, "lon", 2))
    grad_both, grad_pboth, grad_even, grad_odd, out, grad_scores = coarse_call(
        cells, seeds, coarse_weights, bias_coarse
    )
    grads = (
        grad_both,
        swapped(grad_pboth),
        shifted(grad_even, "lon", -1),
        shifted(grad_odd, "lon", -2),
    )
    out_keep, out_send, table_coarse = coarse_rest_call(out, grad_scores, ec)
    grad_most, grad_last, grad_strip = merge_back_call(
        table_coarse, grads, quads, np.ascontiguousarray(pick.T), merge_gain, merge_weight
    )
    grad_strip = shifted(grad_strip, "lat", -1)
    body, table_most = fine_back_call(most, (grad_most,), saved_most, fine_weights, ef)
    grads = (grad_last, grad_strip, strip_onehot(), table_most, body)
    own, edge, table_keep, table_send = fine_back_call(
        final, grads, saved_last, fine_weights, ef
    )
    edge = shifted(edge, "lat", 1)
    partial = partial_call(table_keep, swapped(table_send), table_coarse).reshape(16, 40, 128)
    chips = [[2 * k + c for k in range(16)] for c in range(2)]
    partial = lax.all_to_all(partial, "lon", 0, 0, tiled=True, axis_index_groups=chips)
    sums = lax.all_to_all(sum_call(partial, edge), "lon", 0, 0, tiled=True, axis_index_groups=chips)
    sums = sums.reshape(640, 128)
    band = jnp.concatenate([edge, own], axis=1)
    right = shifted(band[:, :, band.shape[2] // 2 :], "lon", 1)
    coarse_out, grad_tokens, grad_fine, grad_coarse = table_call(
        sums, swapped(sums), out_keep, swapped(out_send), right, band
    )
    return (
        jnp.transpose(coarse_out, (1, 0, 2)),
        grad_tokens,
        jnp.transpose(grad_fine, (2, 0, 1, 3)),
        jnp.transpose(grad_coarse, (2, 0, 1, 3)),
    )


def solution(mesh):
    rows = P(None, "lat", "lon")
    table = P("lat", None, None, None)
    in_specs = (rows,) + (P(),) * 6 + (table,) + (P(),) * 8 + (table, rows)
    return jax.shard_map(
        shards, mesh=mesh, in_specs=in_specs, out_specs=(rows, rows, table, table), check_vma=False
    )
```
